32 devices in a mesh: dp: 8 (over z, x), mp: 4 (over y, core).
Axes of the slice: x: 2, y: 2, z: 4, core: 2. Of those that a mesh axis runs over, the one named last changes fastest.
Arguments:
- tokens: bfloat16 [8192, 768], P('dp'), may hold values from -6 to 6
- cotangent: bfloat16 [8192, 768], P('dp'), may hold values from -6 to 6
- doc_lengths: int32 [8, 4], P('dp'), may hold values from 0 to 1024, as said below
- outer_norms: float32 [4, 768], replicated
- attn_norm: float32 [2, 768], P(None, 'mp')
- ffn_norm: float32 [2, 3072], P(None, 'mp')
- w_qkv: float32 [4, 768, 576], P('mp', 'dp')
- left_qkv: float32 [4, 768, 768], P('mp', 'dp')
- right_qkv: float32 [4, 576, 576], P('mp', 'dp')
- left_root_qkv: float32 [4, 768, 768], P('mp', 'dp')
- right_root_qkv: float32 [4, 576, 576], P('mp')
- w_out: float32 [4, 192, 768], P('mp', 'dp')
- left_out: float32 [4, 192, 192], P('mp', 'dp')
- right_out: float32 [4, 768, 768], P('mp', 'dp')
- left_root_out: float32 [4, 192, 192], P('mp', 'dp')
- right_root_out: float32 [4, 768, 768], P('mp')
- w_up: float32 [4, 768, 768], P('mp', 'dp')
- left_up: float32 [4, 768, 768], P('mp', 'dp')
- right_up: float32 [4, 768, 768], P('mp', 'dp')
- left_root_up: float32 [4, 768, 768], P('mp', 'dp')
- right_root_up: float32 [4, 768, 768], P('mp')
- w_down: float32 [4, 768, 768], P('mp', 'dp')
- left_down: float32 [4, 768, 768], P('mp', 'dp')
- right_down: float32 [4, 768, 768], P('mp', 'dp')
- left_root_down: float32 [4, 768, 768], P('mp', 'dp')
- right_root_down: float32 [4, 768, 768], P('mp')
Outputs:
- block_out: bfloat16 [8192, 768], P('dp')
- grad_tokens: bfloat16 [8192, 768], P('dp')
- grad_outer: float32 [4, 768], replicated
- grad_attn_norm: float32 [2, 768], P(None, 'mp')
- grad_ffn_norm: float32 [2, 3072], P(None, 'mp')
- new_outer: float32 [4, 768], replicated
- new_attn_norm: float32 [2, 768], P(None, 'mp')
- new_ffn_norm: float32 [2, 3072], P(None, 'mp')
- grad_qkv: float32 [4, 768, 576], P('mp')
- new_left_qkv: float32 [4, 768, 768], P('mp', 'dp')
- new_right_qkv: float32 [4, 576, 576], P('mp', 'dp')
- new_w_qkv: float32 [4, 768, 576], P('mp', 'dp')
- copy_qkv: bfloat16 [4, 768, 576], P('mp', 'dp')
- grad_out: float32 [4, 192, 768], P('mp')
- new_left_out: float32 [4, 192, 192], P('mp', 'dp')
- new_right_out: float32 [4, 768, 768], P('mp', 'dp')
- new_w_out: float32 [4, 192, 768], P('mp', 'dp')
- copy_out: bfloat16 [4, 192, 768], P('mp', 'dp')
- grad_up: float32 [4, 768, 768], P('mp')
- new_left_up: float32 [4, 768, 768], P('mp', 'dp')
- new_right_up: float32 [4, 768, 768], P('mp', 'dp')
- new_w_up: float32 [4, 768, 768], P('mp', 'dp')
- copy_up: bfloat16 [4, 768, 768], P('mp', 'dp')
- grad_down: float32 [4, 768, 768], P('mp')
- new_left_down: float32 [4, 768, 768], P('mp', 'dp')
- new_right_down: float32 [4, 768, 768], P('mp', 'dp')
- new_w_down: float32 [4, 768, 768], P('mp', 'dp')
- copy_down: bfloat16 [4, 768, 768], P('mp', 'dp')
The draws below stay inside these ranges and needn't reach their ends.
Inputs may be any that keep to these rules, and one draw needn't show every extreme that they name: `doc_lengths`: each row sums to 1024: either one document of 1024 tokens followed by zeros, or 4 documents of 128 to 384 tokens; both kinds of rows occur in every draw.
All inputs are finite; a program needn't handle non-finite values.
Results may differ from the reference program's by a relative error of at most 0.017.
The reference program's roundings to bfloat16 on the way count: a program that leaves them out, or rounds other values in their place, can miss the bound.
Values may be sent and summed in bfloat16 or wider, within the bound.
No kernel may reach another device: no remote copies, remote signals or barrier semaphores. Data moves between devices by JAX's collectives and lax.ppermute only.
A program may use at most 128 MiB of HBM per device.

```python
import math
import jax
import jax.numpy as jnp
from jax import lax

D = 768
H = 12
HD = 64
FF = 3072
TOK_DEV = 1024
DOCS = 4
HL = 3
HW = 192
FL = 768
INNER = 768
TOKENS = 8192
N_DP = 8
N_MP = 4


def tilted(base_draw, rise, fan_in):
    level = jnp.arange(base_draw.shape[0], dtype=jnp.float32) / max(base_draw.shape[0] - 1, 1)
    return base_draw * fan_in ** (-0.5) * jnp.exp(math.log(rise) * level)[:, None, None]


def stat_matrix(key, width, base, lowest, off_weight):
    first_key, second_key = jax.random.split(key)
    noise = jax.random.normal(first_key, (N_MP, width, width), jnp.float32)
    noise = (noise + jnp.swapaxes(noise, 1, 2)) * 0.5 ** 0.5
    level = jax.random.uniform(second_key, (N_MP, width), jnp.float32)
    diagonal = lowest * jnp.exp(math.log(4.0) * level)
    identity = jnp.eye(width, dtype=jnp.float32)
    return base * (identity * diagonal[:, :, None] + off_weight * width ** (-0.5) * noise * (1.0 - identity))


def draw_doc_lengths(key, part):
    key = jax.random.fold_in(key, 11)
    cut_key, kind_key, long_key, short_key = jax.random.split(key, 4)
    quarter = TOK_DEV // DOCS
    jitter_reach = TOK_DEV // (4 * DOCS)
    jitter = jax.random.randint(cut_key, (N_DP, DOCS - 1), -jitter_reach, jitter_reach + 1)
    cut_points = jnp.arange(1, DOCS, dtype=jnp.int32)[None, :] * quarter + jitter
    bounds = jnp.concatenate([jnp.zeros((N_DP, 1), jnp.int32), cut_points.astype(jnp.int32), jnp.full((N_DP, 1), TOK_DEV, jnp.int32)], axis=1)
    pieces = bounds[:, 1:] - bounds[:, :-1]
    single = jnp.concatenate([jnp.full((1,), TOK_DEV, jnp.int32), jnp.zeros((DOCS - 1,), jnp.int32)])
    row_kinds = jax.random.randint(kind_key, (N_DP,), 0, 2)
    long_row = jax.random.randint(long_key, (), 0, N_DP)
    short_row = (long_row + 1 + jax.random.randint(short_key, (), 0, N_DP - 1)) % N_DP
    row_index = jnp.arange(N_DP)
    row_kinds = jnp.where(row_index == long_row, 1, jnp.where(row_index == short_row, 0, row_kinds))
    return jnp.where(row_kinds[:, None] == 1, single[None, :], pieces).astype(jnp.int32)


def draw_outer_norms(key, part):
    key = jax.random.fold_in(key, 31)
    gain_key, bias_key = jax.random.split(key)
    gains = jax.random.uniform(gain_key, (2, D), jnp.float32, 0.7, 1.3)
    biases = 0.3 * jax.random.normal(bias_key, (2, D), jnp.float32)
    return jnp.stack([gains[0], biases[0], gains[1], biases[1]])


def draw_attn_norm(key, part):
    key = jax.random.fold_in(key, 32)
    gain_key, bias_key = jax.random.split(key)
    gains = jax.random.uniform(gain_key, (INNER,), jnp.float32, 0.7, 1.3)
    biases = 0.3 * jax.random.normal(bias_key, (INNER,), jnp.float32)
    return jnp.stack([gains, biases])


def draw_ffn_norm(key, part):
    key = jax.random.fold_in(key, 33)
    gain_key, bias_key = jax.random.split(key)
    gains = jax.random.uniform(gain_key, (FF,), jnp.float32, 0.7, 1.3)
    biases = 0.3 * jax.random.normal(bias_key, (FF,), jnp.float32)
    return jnp.stack([gains, biases])


def draw_w_qkv(key, part):
    key = jax.random.fold_in(key, 21)
    shape = (N_MP, D, 3 * HW)
    return tilted(jax.random.normal(key, shape, jnp.float32), 3.0 ** 0.5, D)


def draw_w_out(key, part):
    key = jax.random.fold_in(key, 22)
    shape = (N_MP, HW, D)
    return tilted(jax.random.normal(key, shape, jnp.float32), 3.0 ** 0.5, INNER)


def draw_w_up(key, part):
    key = jax.random.fold_in(key, 23)
    shape = (N_MP, D, FL)
    return tilted(jax.random.normal(key, shape, jnp.float32), 3.0 ** 0.5, D)


def draw_w_down(key, part):
    key = jax.random.fold_in(key, 24)
    shape = (N_MP, FL, D)
    return tilted(jax.random.normal(key, shape, jnp.float32), 3.0 ** 0.5, FF)


def draw_left_qkv(key, part):
    key = jax.random.fold_in(key, 41)
    return stat_matrix(key, D, 12.0 * HW / TOKENS, 1.0, 0.6)


def draw_right_qkv(key, part):
    key = jax.random.fold_in(key, 42)
    return stat_matrix(key, 3 * HW, 4.0 * D / TOKENS, 1.0, 0.6)


def draw_left_root_qkv(key, part):
    key = jax.random.fold_in(key, 43)
    return stat_matrix(key, D, (12.0 * HW / TOKENS) ** (-0.25), 0.5, 0.4)


def draw_right_root_qkv(key, part):
    key = jax.random.fold_in(key, 44)
    return stat_matrix(key, 3 * HW, (4.0 * D / TOKENS) ** (-0.25), 0.5, 0.4)


def draw_left_out(key, part):
    key = jax.random.fold_in(key, 51)
    return stat_matrix(key, HW, 1.0 * D / TOKENS, 1.0, 0.6)


def draw_right_out(key, part):
    key = jax.random.fold_in(key, 52)
    return stat_matrix(key, D, 1.0 * HW / TOKENS, 1.0, 0.6)


def draw_left_root_out(key, part):
    key = jax.random.fold_in(key, 53)
    return stat_matrix(key, HW, (1.0 * D / TOKENS) ** (-0.25), 0.5, 0.4)


def draw_right_root_out(key, part):
    key = jax.random.fold_in(key, 54)
    return stat_matrix(key, D, (1.0 * HW / TOKENS) ** (-0.25), 0.5, 0.4)


def draw_left_up(key, part):
    key = jax.random.fold_in(key, 61)
    return stat_matrix(key, D, 4.0 * FL / TOKENS, 1.0, 0.6)


def draw_right_up(key, part):
    key = jax.random.fold_in(key, 62)
    return stat_matrix(key, FL, 4.0 * D / TOKENS, 1.0, 0.6)


def draw_left_root_up(key, part):
    key = jax.random.fold_in(key, 63)
    return stat_matrix(key, D, (4.0 * FL / TOKENS) ** (-0.25), 0.5, 0.4)


def draw_right_root_up(key, part):
    key = jax.random.fold_in(key, 64)
    return stat_matrix(key, FL, (4.0 * D / TOKENS) ** (-0.25), 0.5, 0.4)


def draw_left_down(key, part):
    key = jax.random.fold_in(key, 71)
    return stat_matrix(key, FL, 1.0 * D / TOKENS, 1.0, 0.6)


def draw_right_down(key, part):
    key = jax.random.fold_in(key, 72)
    return stat_matrix(key, D, 1.0 * FL / TOKENS, 1.0, 0.6)


def draw_left_root_down(key, part):
    key = jax.random.fold_in(key, 73)
    return stat_matrix(key, FL, (1.0 * D / TOKENS) ** (-0.25), 0.5, 0.4)


def draw_right_root_down(key, part):
    key = jax.random.fold_in(key, 74)
    return stat_matrix(key, D, (1.0 * FL / TOKENS) ** (-0.25), 0.5, 0.4)


def levels(own_key, extent, shards, smallest, top_value):
    gain, own = 1.0, jax.random.fold_in(own_key, 6)
    for position, shards_of in shards:
        heights = jnp.exp(jax.random.uniform(jax.random.fold_in(own, position), (shards_of,), jnp.float32, smallest / len(shards), top_value / len(shards)))
        gain = gain * jnp.repeat(heights, extent[position] // shards_of).reshape([-1 if axis == position else 1 for axis in range(len(extent))])
    return gain


def gaussian(own_key, extent, scale, limit, shards=(), kind=jnp.bfloat16):
    drawn = scale * jax.random.normal(own_key, extent, jnp.float32)
    if shards:
        drawn = drawn * levels(own_key, extent, shards, -0.22, 0.18)
    return jnp.clip(drawn, -limit, limit).astype(kind)


def setup_inputs(seed: int = 0) -> dict:
    streams_of = jax.random.split(jax.random.key(seed), 27)
    return {
        "tokens": gaussian(streams_of[0], (TOKENS, D), 1.0, 6.0, ((0, 8),)),
        "cotangent": gaussian(streams_of[1], (TOKENS, D), 1.0, 6.0, ((0, 8),)),
        "doc_lengths": draw_doc_lengths(jax.random.fold_in(streams_of[26], 71), 0),
        "outer_norms": draw_outer_norms(jax.random.fold_in(streams_of[26], 71), 0),
        "attn_norm": draw_attn_norm(jax.random.fold_in(streams_of[26], 71), 0),
        "ffn_norm": draw_ffn_norm(jax.random.fold_in(streams_of[26], 71), 0),
        "w_qkv": draw_w_qkv(jax.random.fold_in(streams_of[26], 71), 0),
        "left_qkv": draw_left_qkv(jax.random.fold_in(streams_of[26], 71), 0),
        "right_qkv": draw_right_qkv(jax.random.fold_in(streams_of[26], 71), 0),
        "left_root_qkv": draw_left_root_qkv(jax.random.fold_in(streams_of[26], 71), 0),
        "right_root_qkv": draw_right_root_qkv(jax.random.fold_in(streams_of[26], 71), 0),
        "w_out": draw_w_out(jax.random.fold_in(streams_of[26], 71), 0),
        "left_out": draw_left_out(jax.random.fold_in(streams_of[26], 71), 0),
        "right_out": draw_right_out(jax.random.fold_in(streams_of[26], 71), 0),
        "left_root_out": draw_left_root_out(jax.random.fold_in(streams_of[26], 71), 0),
        "right_root_out": draw_right_root_out(jax.random.fold_in(streams_of[26], 71), 0),
        "w_up": draw_w_up(jax.random.fold_in(streams_of[26], 71), 0),
        "left_up": draw_left_up(jax.random.fold_in(streams_of[26], 71), 0),
        "right_up": draw_right_up(jax.random.fold_in(streams_of[26], 71), 0),
        "left_root_up": draw_left_root_up(jax.random.fold_in(streams_of[26], 71), 0),
        "right_root_up": draw_right_root_up(jax.random.fold_in(streams_of[26], 71), 0),
        "w_down": draw_w_down(jax.random.fold_in(streams_of[26], 71), 0),
        "left_down": draw_left_down(jax.random.fold_in(streams_of[26], 71), 0),
        "right_down": draw_right_down(jax.random.fold_in(streams_of[26], 71), 0),
        "left_root_down": draw_left_root_down(jax.random.fold_in(streams_of[26], 71), 0),
        "right_root_down": draw_right_root_down(jax.random.fold_in(streams_of[26], 71), 0),
    }


EPS = 1e-05
DECAY = 0.5
MAT_RATE = 0.5
VEC_RATE = 0.05
UNIT_RATE = 0.3
HIGH = lax.Precision.HIGHEST

@jax.custom_vjp
def low(v):
    return lax.optimization_barrier(v.astype(jnp.bfloat16)).astype(jnp.float32)

@jax.custom_vjp
def low_back(v):
    return v

def low_keep(v):
    return (low(v), None)

def low_pass(kept, grad):
    return (grad,)

def back_keep(v):
    return (v, None)

def back_low(kept, grad):
    return (low(grad),)
low.defvjp(low_keep, low_pass)
low_back.defvjp(back_keep, back_low)

def layer_norm(values_in, gain_row, bias_row):
    center = lax.optimization_barrier(jnp.mean(values_in, -1, keepdims=True))
    offset = values_in - center
    spread = lax.optimization_barrier(jnp.mean(offset * offset, -1, keepdims=True))
    return offset * lax.rsqrt(spread + EPS) * gain_row + bias_row

def forward(params, inputs, member):
    outer_norms, attn_norm, ffn_norm, w_qkv, w_out, w_up, w_down = params
    row_count = inputs.shape[0]
    normed_a = low(layer_norm(inputs, outer_norms[0], outer_norms[1]))
    projected = jnp.einsum('td,mdc->tmc', normed_a, low(w_qkv), precision=HIGH)
    projected = low(low_back(projected)).reshape(row_count, N_MP, 3, HL, HD)
    query_all = projected[:, :, 0].reshape(row_count, H, HD)
    key_all = projected[:, :, 1].reshape(row_count, H, HD)
    value_all = projected[:, :, 2].reshape(row_count, H, HD)
    places = jnp.arange(row_count, dtype=jnp.int32)
    visible = (member[:, None] == member[None, :]) & (places[None, :] <= places[:, None])
    scores = jnp.einsum('qhe,khe->hqk', query_all, key_all, precision=HIGH) * HD ** (-0.5)
    scores = low_back(jnp.where(visible[None], scores, -1e+30))
    weights = jax.nn.softmax(scores, axis=-1)
    attended = jnp.einsum('hqk,khe->qhe', low(weights), value_all, precision=HIGH).reshape(row_count, H * HD)
    attended = low_back(attended)
    normed_y = low(layer_norm(attended, attn_norm[0], attn_norm[1]))
    branch_attn = jnp.einsum('tmi,mid->td', normed_y.reshape(row_count, N_MP, HW), low(w_out), precision=HIGH)
    hidden = inputs + low_back(branch_attn)
    normed_c = low(layer_norm(hidden, outer_norms[2], outer_norms[3]))
    up_all = jnp.einsum('td,mdf->tmf', normed_c, low(w_up), precision=HIGH).reshape(row_count, FF)
    up_all = low_back(up_all)
    activated = jax.nn.gelu(up_all, approximate=True)
    normed_w = low(layer_norm(activated, ffn_norm[0], ffn_norm[1]))
    branch_ffn = jnp.einsum('tmf,mfd->td', normed_w.reshape(row_count, N_MP, FL), low(w_down), precision=HIGH)
    return hidden + branch_ffn

def shampoo_update(grad_sum, master, left_stat, right_stat, left_root, right_root):
    mean_grad = grad_sum / TOKENS
    new_left = DECAY * left_stat + (1.0 - DECAY) * jnp.einsum('mij,mkj->mik', mean_grad, mean_grad, precision=HIGH)
    new_right = DECAY * right_stat + (1.0 - DECAY) * jnp.einsum('mji,mjk->mik', mean_grad, mean_grad, precision=HIGH)
    left_part = jnp.einsum('mij,mjk->mik', left_root, mean_grad, precision=HIGH)
    step_size = jnp.einsum('mij,mjk->mik', left_part, right_root, precision=HIGH)
    new_master = master - MAT_RATE * step_size
    return (new_left, new_right, new_master, new_master.astype(jnp.bfloat16))

def add_pair(first_term, second_term):
    return first_term + second_term

def reference(tokens, cotangent, doc_lengths, outer_norms, attn_norm, ffn_norm, w_qkv, left_qkv, right_qkv, left_root_qkv, right_root_qkv, w_out, left_out, right_out, left_root_out, right_root_out, w_up, left_up, right_up, left_root_up, right_root_up, w_down, left_down, right_down, left_root_down, right_root_down):
    params = (outer_norms, attn_norm, ffn_norm, w_qkv, w_out, w_up, w_down)
    packs = tokens.astype(jnp.float32).reshape(N_DP, TOK_DEV, D)
    pack_grads = cotangent.astype(jnp.float32).reshape(N_DP, TOK_DEV, D)
    places = jnp.arange(TOK_DEV, dtype=jnp.int32)

    def pack_step(running, item):
        inputs, grad_output, lengths = item
        ends = jnp.cumsum(lengths).astype(jnp.int32)
        member = lax.optimization_barrier(jnp.sum((places[:, None] >= ends[None, :]).astype(jnp.int32), axis=1))

        def local_forward(weights_in, values_in):
            return forward(weights_in, values_in, member)
        output, backward = jax.vjp(local_forward, params, inputs)
        grad_params, grad_inputs = backward(grad_output)
        running = jax.tree.map(add_pair, running, grad_params)
        return (running, (output.astype(jnp.bfloat16), grad_inputs.astype(jnp.bfloat16)))
    zero_grads = jax.tree.map(jnp.zeros_like, params)
    totals, (outputs, grad_rows) = lax.scan(pack_step, zero_grads, (packs, pack_grads, doc_lengths))
    grad_outer, grad_attn, grad_ffn, grad_qkv, grad_out, grad_up, grad_down = totals
    factor = VEC_RATE / math.sqrt(TOKENS)
    unit_factor = UNIT_RATE / math.sqrt(TOKENS)
    qkv_left, qkv_right, qkv_new, qkv_copy = shampoo_update(grad_qkv, w_qkv, left_qkv, right_qkv, left_root_qkv, right_root_qkv)
    out_left, out_right, out_new, out_copy = shampoo_update(grad_out, w_out, left_out, right_out, left_root_out, right_root_out)
    up_left, up_right, up_new, up_copy = shampoo_update(grad_up, w_up, left_up, right_up, left_root_up, right_root_up)
    down_left, down_right, down_new, down_copy = shampoo_update(grad_down, w_down, left_down, right_down, left_root_down, right_root_down)
    return (outputs.reshape(TOKENS, D), grad_rows.reshape(TOKENS, D), grad_outer, grad_attn, grad_ffn, outer_norms - factor * grad_outer, attn_norm - factor * grad_attn, ffn_norm - unit_factor * grad_ffn, grad_qkv, qkv_left, qkv_right, qkv_new, qkv_copy, grad_out, out_left, out_right, out_new, out_copy, grad_up, up_left, up_right, up_new, up_copy, grad_down, down_left, down_right, down_new, down_copy)
```

```python
import math

import jax
import jax.numpy as jnp
from jax import lax
from jax.experimental import pallas as pl
from jax.experimental.pallas import tpu as pltpu
from jax.sharding import PartitionSpec as P

HD = 64
EPS = 1e-05
DECAY = 0.5
MAT_RATE = 0.5
VEC_RATE = 0.05
UNIT_RATE = 0.3
GELU_A = math.sqrt(2.0 / math.pi)
GELU_B = 0.044715
BF = jnp.bfloat16
F32 = jnp.float32
VMEM = 48 * 1024 * 1024
WAYS = 8
BLK = 256


def full(shape):
    return pl.BlockSpec(shape, lambda *args: (0,) * len(shape))


def fulls(arrays):
    return [full(x.shape) for x in arrays]


def run(kernel, grid, ins, in_specs, outs, out_specs, idx, name, flops, scratch=()):
    traffic = sum(x.size * x.dtype.itemsize for x in ins)
    traffic += sum(math.prod(o.shape) * o.dtype.itemsize for o in outs)
    return pl.pallas_call(
        kernel,
        grid_spec=pltpu.PrefetchScalarGridSpec(
            num_scalar_prefetch=1,
            grid=grid,
            in_specs=in_specs,
            out_specs=out_specs,
            scratch_shapes=list(scratch),
        ),
        out_shape=outs,
        compiler_params=pltpu.CompilerParams(vmem_limit_bytes=VMEM),
        cost_estimate=pl.CostEstimate(
            flops=int(flops), bytes_accessed=int(traffic), transcendentals=0
        ),
        name=name,
    )(idx, *ins)


def sds(shape, dtype):
    return jax.ShapeDtypeStruct(shape, dtype)


def dot(x, y):
    return jnp.dot(x, y, preferred_element_type=F32)


def dot_nt(x, y):
    return lax.dot_general(x, y, (((1,), (1,)), ((), ())), preferred_element_type=F32)


def dot_tn(x, y):
    return lax.dot_general(x, y, (((0,), (0,)), ((), ())), preferred_element_type=F32)


def rowsum(x):
    return jnp.sum(x, -1, keepdims=True)


def normalize(x):
    n = x.shape[-1]
    off = x - rowsum(x) / n
    r = lax.rsqrt(rowsum(off * off) / n + EPS)
    return off * r, r


def gelu_parts(u):
    t = jnp.tanh(GELU_A * (u + GELU_B * (u * u * u)))
    return 0.5 * u * (1.0 + t), t


def unpack_rows(tail, narrow):
    n = tail.shape[-1]
    low = tail.shape[0] * n // (n + narrow)
    rest = tail[low:]
    step = tail.shape[0] - low
    side = jnp.concatenate([rest[:, i * narrow : (i + 1) * narrow] for i in range(low // step)], axis=0)
    return jnp.concatenate([tail[:low], side], axis=1)


def pack_rows(block, wide):
    rows, n = block.shape
    narrow = n - wide
    step = rows * narrow // wide
    side = block[:, wide:]
    rest = jnp.concatenate([side[i * step : (i + 1) * step] for i in range(rows // step)], axis=1)
    return jnp.concatenate([block[:, :wide], rest], axis=0)


def project_kernel(idx, a_ref, *refs):
    pieces = refs[:WAYS]
    q_ref, k_ref, v_ref, wq_ref, wo_ref, scr = refs[WAYS:]
    rows = wq_ref.shape[0] // WAYS
    orows = wo_ref.shape[0] // WAYS
    hw = q_ref.shape[1]

    @pl.when(pl.program_id(0) == 0)
    def _():
        for k in range(WAYS):
            j = jnp.bitwise_xor(idx[0], k)
            wq_ref[pl.ds(pl.multiple_of(j * rows, rows), rows), :] = pieces[k][:rows, :]
            tail = pieces[k][rows:, :].astype(F32)
            scr[pl.ds(pl.multiple_of(j * orows, orows), orows), :] = unpack_rows(
                tail, wo_ref.shape[1] - wq_ref.shape[1]
            )
        wo_ref[...] = scr[...].astype(BF)

    res = dot(a_ref[...], wq_ref[...]).astype(BF)
    q_ref[...] = res[:, :hw] * BF(HD ** (-0.5))
    k_ref[...] = res[:, hw : 2 * hw]
    v_ref[...] = res[:, 2 * hw :]


def project(a, pieces, hw, idx):
    rows, d = a.shape
    n = 3 * hw
    blk = lambda w: pl.BlockSpec((BLK, w), lambda s, i: (s, 0))
    return run(
        project_kernel,
        (rows // BLK,),
        [a, *pieces],
        [blk(d)] + fulls(pieces),
        [sds((rows, hw), BF)] * 3 + [sds((d, n), BF), sds((hw, d), BF)],
        [blk(hw)] * 3 + [full((d, n)), full((hw, d))],
        idx,
        "project",
        2 * rows * d * n,
        [pltpu.VMEM((hw, d), F32)],
    )


def attend_kernel(idx, start_ref, q_ref, k_ref, v_ref, o_ref, p_ref):
    h = pl.program_id(0)
    rows, hw = q_ref.shape
    lane = (lax.broadcasted_iota(jnp.int32, (1, hw), 1) // HD) == h
    for i in range(rows // BLK):
        lo, hi = i * BLK, (i + 1) * BLK
        qb = jnp.where(lane, q_ref[lo:hi, :], BF(0))
        s = dot_nt(qb, k_ref[:hi, :])
        kpos = lax.broadcasted_iota(jnp.int32, (BLK, hi), 1)
        qpos = lo + lax.broadcasted_iota(jnp.int32, (BLK, hi), 0)
        s = jnp.where((kpos >= start_ref[lo:hi, :]) & (kpos <= qpos), s, -1e30)
        p = jnp.exp(s - jnp.max(s, -1, keepdims=True))
        p = (p * (1.0 / rowsum(p))).astype(BF)
        p_ref[0, lo:hi, :hi] = p
        ob = dot(p, v_ref[:hi, :]).astype(BF)
        o_ref[lo:hi, :] = jnp.where(lane, ob, o_ref[lo:hi, :])


def attend(start, q, k, v, idx):
    rows, hw = q.shape
    heads = hw // HD
    return run(
        attend_kernel,
        (heads,),
        [start, q, k, v],
        fulls([start, q, k, v]),
        [sds((rows, hw), BF), sds((heads, rows, rows), BF)],
        [full((rows, hw)), pl.BlockSpec((1, rows, rows), lambda s, i: (s, 0, 0))],
        idx,
        "attend",
        heads * rows * rows * 256 * 4,
    )


def wide_norm(o_refs):
    parts = [x[...].astype(F32) for x in o_refs]
    n = sum(x.shape[-1] for x in parts)
    mean = sum(rowsum(x) for x in parts) / n
    parts = [x - mean for x in parts]
    r = lax.rsqrt(sum(rowsum(x * x) for x in parts) / n + EPS)
    return [x * r for x in parts], r


def outproj_kernel(idx, an_ref, on_ref, tok_ref, *refs):
    g = (len(refs) - 2) // 2
    o_refs, w_refs = refs[:g], refs[g : 2 * g]
    h_ref, c_ref = refs[2 * g :]
    hats, _ = wide_norm(o_refs)
    acc = tok_ref[...].astype(F32)
    for k in range(g):
        norm = an_ref[jnp.bitwise_xor(idx[1], k)]
        y = (hats[k] * norm[0:1] + norm[1:2]).astype(BF)
        acc = acc + dot(y, w_refs[k][...])
    h_ref[...] = acc
    hat, _ = normalize(acc)
    c_ref[...] = (hat * on_ref[2:3, :] + on_ref[3:4, :]).astype(BF)


def outproj(an, on, tok, o, w, idx):
    rows, d = tok.shape
    hw = o[0].shape[1]
    blk = lambda n: pl.BlockSpec((BLK, n), lambda s, i: (s, 0))
    return run(
        outproj_kernel,
        (rows // BLK,),
        [an, on, tok, *o, *w],
        fulls([an, on]) + [blk(d)] + [blk(hw)] * len(o) + fulls(w),
        [sds((rows, d), F32), sds((rows, d), BF)],
        [blk(d), blk(d)],
        idx,
        "outproj",
        2 * rows * d * hw * len(o),
    )


def ffn_up_kernel(idx, c_ref, e_ref, fn_ref, *refs):
    up, down = refs[:WAYS], refs[WAYS : 2 * WAYS]
    u_ref, dw_ref, st_ref, wu_ref, wd_ref = refs[2 * WAYS :]
    rows = up[0].shape[0]

    @pl.when(pl.program_id(0) == 0)
    def _():
        for k in range(WAYS):
            j = jnp.bitwise_xor(idx[0], k)
            at = pl.ds(pl.multiple_of(j * rows, rows), rows)
            wu_ref[at, :] = up[k][...]
            wd_ref[at, :] = down[k][...]

    u = dot(c_ref[...], wu_ref[...])
    u_ref[...] = u
    z, _ = gelu_parts(u)
    mean = rowsum(z) / z.shape[-1]
    z = z - mean
    dw = dot_nt(e_ref[...], wd_ref[...])
    dw_ref[...] = dw
    eg = dw * fn_ref[0:1, :]
    stats = [mean, rowsum(z * z), rowsum(eg), rowsum(eg * z)]
    place = lax.broadcasted_iota(jnp.int32, (BLK, 128), 1)
    tile = jnp.zeros((BLK, 128), F32)
    for i, x in enumerate(stats):
        tile = jnp.where(place == i, x, tile)
    st_ref[...] = tile.T[:8, :]


def ffn_up(c, e, fn, up, down, idx):
    rows, d = c.shape
    fl = up[0].shape[1]
    rblk = lambda n: pl.BlockSpec((BLK, n), lambda s, i: (s, 0))
    return run(
        ffn_up_kernel,
        (rows // BLK,),
        [c, e, fn, *up, *down],
        [rblk(d), rblk(d), full(fn.shape)] + fulls(up) + fulls(down),
        [sds((rows, fl), F32), sds((rows, fl), F32), sds((8, rows), F32), sds((d, fl), BF), sds((fl, d), BF)],
        [rblk(fl), rblk(fl), pl.BlockSpec((8, BLK), lambda s, i: (0, s)), full((d, fl)), full((fl, d))],
        idx,
        "ffn_up",
        4 * rows * d * fl,
    )


def rel_of(s):
    return jnp.where(s < 2, 2 * s + 1, 2 * s - 4)


def rel_block(s, i):
    return jnp.bitwise_xor(rel_of(s), i[1])


def rel_spec(n):
    return pl.BlockSpec((BLK, n), lambda s, i: (rel_block(s, i), 0))


SEND_SPEC = lambda n: pl.BlockSpec((1, BLK, n), lambda s, i: (jnp.minimum(s, 1), 0, 0))
KEEP_SPEC = lambda n: pl.BlockSpec((1, BLK, n), lambda s, i: (jnp.maximum(s - 2, 0), 0, 0))


def put_rel(send_ref, keep_ref, value):
    @pl.when(pl.program_id(0) < 2)
    def _():
        send_ref[0] = value.astype(BF)

    @pl.when(pl.program_id(0) >= 2)
    def _():
        keep_ref[0] = value


def ffn_mid_kernel(idx, u_ref, dw_ref, st_ref, fn_ref, wu_ref, w_ref, du_ref, send_ref, keep_ref, fg_ref):
    g = st_ref.shape[0]
    fl = u_ref.shape[1]
    n = g * fl
    st = [st_ref[k] for k in range(g)]
    mean = sum(x[0:1] for x in st) / g
    gap = [x[0:1] - mean for x in st]
    spread = sum(x[1:2] + fl * (gp * gp) for x, gp in zip(st, gap)) / n
    r = lax.rsqrt(spread + EPS)
    s_plain = sum(x[2:3] for x in st) / n
    s_norm = r * (sum(x[3:4] + gp * x[2:3] for x, gp in zip(st, gap)) / n)
    cols = jnp.concatenate([mean, r, s_plain, s_norm, jnp.zeros((124, BLK), F32)], axis=0).T
    mean, r, s_plain, s_norm = (cols[:, i : i + 1] for i in range(4))
    u = u_ref[...]
    z, t = gelu_parts(u)
    hat = (z - mean) * r
    w_ref[...] = (hat * fn_ref[0:1, :] + fn_ref[1:2, :]).astype(BF)
    dw = dw_ref[...]
    dz = r * (dw * fn_ref[0:1, :] - s_plain - hat * s_norm)
    slope = 0.5 * (1.0 + t) + 0.5 * u * (1.0 - t * t) * (GELU_A * (1.0 + (3.0 * GELU_B) * (u * u)))
    du = (dz * slope).astype(BF)
    du_ref[...] = du
    put_rel(send_ref, keep_ref, dot_nt(du, wu_ref[...]))
    grads = jnp.concatenate([jnp.sum(dw * hat, 0, keepdims=True), jnp.sum(dw, 0, keepdims=True)], axis=0)

    @pl.when(pl.program_id(0) == 0)
    def _():
        fg_ref[...] = grads

    @pl.when(pl.program_id(0) > 0)
    def _():
        fg_ref[...] += grads


def ffn_mid(u, dw, st, fn, wu, idx):
    rows, fl = u.shape
    d = wu.shape[0]
    return run(
        ffn_mid_kernel,
        (rows // BLK,),
        [u, dw, st, fn, wu],
        [rel_spec(fl), rel_spec(fl), pl.BlockSpec((st.shape[0], 8, BLK), lambda s, i: (0, 0, rel_block(s, i)))]
        + fulls([fn, wu]),
        [sds((rows, fl), BF), sds((rows, fl), BF), sds((2, BLK, d), BF), sds((2, BLK, d), F32), sds((2, fl), F32)],
        [rel_spec(fl), rel_spec(fl), SEND_SPEC(d), KEEP_SPEC(d), full((2, fl))],
        idx,
        "ffn_mid",
        2 * rows * d * fl,
    )


def rel_matmul(x, w, transposed, idx, name):
    rows, depth = x.shape
    d = w.shape[0] if transposed else w.shape[1]

    def kernel(idx, x_ref, w_ref, send_ref, keep_ref):
        op = dot_nt if transposed else dot
        put_rel(send_ref, keep_ref, op(x_ref[...], w_ref[...]))

    return run(
        kernel,
        (rows // BLK,),
        [x, w],
        [rel_spec(depth), full(w.shape)],
        [sds((2, BLK, d), BF), sds((2, BLK, d), F32)],
        [SEND_SPEC(d), KEEP_SPEC(d)],
        idx,
        name,
        2 * rows * d * depth,
    )


def weight_grad(x, y, idx, name, extra=None):
    rows, d = x.shape
    n = y.shape[1]
    step = d // WAYS
    steps = d // BLK
    extra_rows = 0 if extra is None else extra.size // (WAYS * n)
    out = step + extra_rows

    def kernel(idx, x_ref, y_ref, *refs):
        send_ref, keep_ref, scr = refs[-3:]
        s = pl.program_id(0)
        scr[pl.ds(pl.multiple_of(s * BLK, BLK), BLK), :] = dot_tn(x_ref[...], y_ref[...])

        @pl.when(s == steps - 1)
        def _():
            for k in range(WAYS):
                j = jnp.bitwise_xor(idx[0], k)
                value = scr[pl.ds(pl.multiple_of(j * step, step), step), :]
                dest = send_ref if k % 2 else keep_ref
                dest[k // 2, :step, :] = value.astype(dest.dtype)
                if extra_rows:
                    er = refs[0].shape[0] // WAYS
                    tail = pack_rows(refs[0][pl.ds(pl.multiple_of(j * er, er), er), :], n)
                    dest[k // 2, step:, :] = tail.astype(dest.dtype)

    ins = [x, y] + ([] if extra is None else [extra])
    return run(
        kernel,
        (steps,),
        ins,
        [pl.BlockSpec((rows, BLK), lambda s, i: (0, s))] + fulls(ins[1:]),
        [sds((WAYS // 2, out, n), BF), sds((WAYS // 2, out, n), F32)],
        [full((WAYS // 2, out, n))] * 2,
        idx,
        name,
        2 * rows * d * n,
        [pltpu.VMEM((d, n), F32)],
    )


def shard_back_kernel(idx, dc0_ref, dc1_ref, dc2_ref, h_ref, e_ref, an_ref, on_ref, *refs):
    g = 4
    o_refs, w_refs = refs[:g], refs[g : 2 * g]
    dh_ref, ol_ref, ag_ref, *do_refs = refs[2 * g :]
    do_refs, (gs_ref, gk_ref) = do_refs[:g], do_refs[g:]
    dc = dc0_ref[0] + dc1_ref[0].astype(F32) + dc2_ref[...].astype(F32)
    hat, r = normalize(h_ref[...])
    wgt = dc * on_ref[2:3, :]
    n = dc.shape[-1]
    dh = e_ref[...].astype(F32) + r * (wgt - rowsum(wgt) / n - hat * (rowsum(wgt * hat) / n))
    dh_ref[...] = dh
    ol_ref[...] = jnp.concatenate([jnp.sum(dc * hat, 0, keepdims=True), jnp.sum(dc, 0, keepdims=True)], axis=0)
    dhb = dh.astype(BF)
    hats, r = wide_norm(o_refs)
    norms = [an_ref[jnp.bitwise_xor(idx[1], k)] for k in range(g)]
    dys = [dot_nt(dhb, w_refs[k][...]) for k in range(g)]
    wgts = [dys[k] * norms[k][0:1] for k in range(g)]
    s_plain = sum(rowsum(x) for x in wgts) / n
    s_norm = sum(rowsum(x * y) for x, y in zip(wgts, hats)) / n
    for k in range(g):
        do_refs[k][...] = (r * (wgts[k] - s_plain - hats[k] * s_norm)).astype(BF)
        ag_ref[jnp.bitwise_xor(idx[1], k)] = jnp.concatenate(
            [jnp.sum(dys[k] * hats[k], 0, keepdims=True), jnp.sum(dys[k], 0, keepdims=True)], axis=0
        )
    for k in range(g):
        y = (hats[k] * norms[k][0:1] + norms[k][1:2]).astype(BF)
        dest = gs_ref if k % 2 else gk_ref
        dest[k // 2] = dot_tn(y, dhb).astype(dest.dtype)


def shard_back(dc_keep, dc_one, dc_two, h, e, an, on, o, w, idx):
    rows, d = h.shape
    g = len(o)
    hw = o[0].shape[1]
    mine = lambda n: pl.BlockSpec((BLK, n), lambda s, i: (i[1], 0))
    lead = pl.BlockSpec((1, BLK, d), lambda s, i: (0, 0, 0))
    ins = [dc_keep, dc_one, dc_two, h, e, an, on, *o, *w]
    return run(
        shard_back_kernel,
        (1,),
        ins,
        [lead, lead, full((BLK, d)), mine(d), mine(d)] + fulls([an, on]) + [mine(hw)] * g + fulls(w),
        [sds((BLK, d), F32), sds((2, d), F32), sds((g, 2, hw), F32)]
        + [sds((BLK, hw), BF)] * g
        + [sds((2, hw, d), BF), sds((2, hw, d), F32)],
        [full((BLK, d)), full((2, d)), full((g, 2, hw))]
        + [full((BLK, hw))] * g
        + [full((2, hw, d))] * 2,
        idx,
        "shard_back",
        4 * BLK * d * d,
    )


def attend_back_kernel(idx, q_ref, k_ref, v_ref, p_ref, *refs):
    d_refs = refs[:4]
    out_ref, do_scr, dq_scr, dk_scr, dv_scr = refs[4:]
    h = pl.program_id(0)
    rows, hw = q_ref.shape

    @pl.when(h == 0)
    def _():
        for k in range(4):
            j = jnp.bitwise_xor(idx[1], k)
            do_scr[pl.ds(pl.multiple_of(j * BLK, BLK), BLK), :] = d_refs[k][...]
        dk_scr[...] = jnp.zeros_like(dk_scr)
        dv_scr[...] = jnp.zeros_like(dv_scr)
        dq_scr[...] = jnp.zeros_like(dq_scr)

    lane = (lax.broadcasted_iota(jnp.int32, (1, hw), 1) // HD) == h
    for i in range(rows // BLK):
        lo, hi = i * BLK, (i + 1) * BLK
        dob = jnp.where(lane, do_scr[lo:hi, :], BF(0))
        qb = jnp.where(lane, q_ref[lo:hi, :], BF(0))
        pb = p_ref[0, lo:hi, :hi]
        p = pb.astype(F32)
        dp = dot_nt(dob, v_ref[:hi, :])
        ds = (p * (dp - rowsum(p * dp))).astype(BF)
        dq_scr[lo:hi, :] = jnp.where(lane, dot(ds, k_ref[:hi, :]), dq_scr[lo:hi, :])
        dk_scr[:hi, :] += dot_tn(ds, qb)
        dv_scr[:hi, :] += dot_tn(pb, dob)

    @pl.when(h == pl.num_programs(0) - 1)
    def _():
        out_ref[...] = jnp.concatenate([dq_scr[...] * HD ** (-0.5), dk_scr[...], dv_scr[...]], axis=1).astype(BF)


def attend_back(q, k, v, p, do, idx):
    rows, hw = q.shape
    heads = hw // HD
    return run(
        attend_back_kernel,
        (heads,),
        [q, k, v, p, *do],
        fulls([q, k, v]) + [pl.BlockSpec((1, rows, rows), lambda s, i: (s, 0, 0))] + fulls(do),
        [sds((rows, 3 * hw), BF)],
        [full((rows, 3 * hw))],
        idx,
        "attend_back",
        heads * rows * rows * 256 * 8,
        [pltpu.VMEM((rows, hw), BF)] + [pltpu.VMEM((rows, hw), F32)] * 3,
    )[0]


def shard_end_kernel(idx, da0_ref, da1_ref, da2_ref, tok_ref, on_ref, dh_ref, gt_ref, oe_ref):
    da = da0_ref[0] + da1_ref[0].astype(F32) + da2_ref[...].astype(F32)
    hat, r = normalize(tok_ref[...].astype(F32))
    wgt = da * on_ref[0:1, :]
    n = da.shape[-1]
    grad = r * (wgt - rowsum(wgt) / n - hat * (rowsum(wgt * hat) / n))
    gt_ref[...] = (dh_ref[...] + grad).astype(BF)
    oe_ref[...] = jnp.concatenate([jnp.sum(da * hat, 0, keepdims=True), jnp.sum(da, 0, keepdims=True)], axis=0)


def shard_end(da_keep, da_one, da_two, tok, on, dh, idx):
    d = tok.shape[1]
    lead = pl.BlockSpec((1, BLK, d), lambda s, i: (0, 0, 0))
    return run(
        shard_end_kernel,
        (1,),
        [da_keep, da_one, da_two, tok, on, dh],
        [lead, lead, full((BLK, d)), pl.BlockSpec((BLK, d), lambda s, i: (i[1], 0)), full(on.shape), full((BLK, d))],
        [sds((BLK, d), BF), sds((2, d), F32)],
        [full((BLK, d)), full((2, d))],
        idx,
        "shard_end",
        0,
    )


def spread_rows(parts, idx, name):
    d = parts[0].shape[1]

    def kernel(idx, *refs):
        for k in range(len(parts)):

            @pl.when(pl.program_id(0) == k)
            def _():
                refs[-1][...] = refs[k][...]

    return run(
        kernel,
        (len(parts),),
        parts,
        fulls(parts),
        [sds((BLK * len(parts), d), BF)],
        [pl.BlockSpec((BLK, d), lambda s, i: (jnp.bitwise_xor(s, i[1]), 0))],
        idx,
        name,
        0,
    )[0]


def precondition(pieces, w, left, right, left_root, right_root, total, packed, idx, name):
    rows, n = w.shape
    d = left.shape[1]
    side = right.shape[0]
    step = d // WAYS

    def kernel(idx, w_ref, l_ref, r_ref, lr_ref, rr_ref, *refs):
        parts = refs[:WAYS]
        g_ref, nl_ref, nr_ref, nw_ref, copy_ref = refs[WAYS:]
        for k in range(WAYS):
            j = jnp.bitwise_xor(idx[0], k)
            if packed == "head":
                value = parts[k][:step, :].astype(F32)
            elif packed == "tail":
                wide = parts[k].shape[1]
                head = parts[k].shape[0] - step * n // wide
                value = unpack_rows(parts[k][head:, :].astype(F32), n - wide)
            else:
                value = parts[k][...].astype(F32)
            g_ref[pl.ds(pl.multiple_of(j * step, step), step), :] = value
        grad = g_ref[...].astype(BF)
        place = idx[2]

        def one_hot(count, width):
            at = lax.broadcasted_iota(jnp.int32, (count, width), 1)
            want = place * count + lax.broadcasted_iota(jnp.int32, (count, width), 0)
            return jnp.where(at == want, 1.0, 0.0).astype(BF)

        scale = 1.0 / total
        own_cols = dot_nt(one_hot(side, n), grad).astype(BF)
        own_rows = dot(one_hot(rows, d), grad).astype(BF)
        nr_ref[...] = DECAY * r_ref[...] + ((1.0 - DECAY) * scale * scale) * dot(own_cols, grad)
        nl_ref[...] = DECAY * l_ref[...] + ((1.0 - DECAY) * scale * scale) * dot_nt(own_rows, grad)
        part = dot(lr_ref[...].astype(BF), grad).astype(BF)
        new = w_ref[...] - (MAT_RATE * scale) * dot(part, rr_ref[...].astype(BF))
        nw_ref[...] = new
        copy_ref[...] = new.astype(BF)

    ins = [w, left, right, left_root, right_root, *pieces]
    outs = [sds((d, n), F32), sds((rows, d), F32), sds((side, n), F32), sds((rows, n), F32), sds((rows, n), BF)]
    return run(
        kernel,
        (1,),
        ins,
        fulls(ins),
        outs,
        fulls(outs),
        idx,
        name,
        2 * rows * n * (2 * d + n) + 4 * rows * d * n,
    )


def body(
    tokens,
    cotangent,
    doc_lengths,
    outer_norms,
    attn_norm,
    ffn_norm,
    w_qkv,
    left_qkv,
    right_qkv,
    left_root_qkv,
    right_root_qkv,
    w_out,
    left_out,
    right_out,
    left_root_out,
    right_root_out,
    w_up,
    left_up,
    right_up,
    left_root_up,
    right_root_up,
    w_down,
    left_down,
    right_down,
    left_root_down,
    right_root_down,
):
    row_count = tokens.shape[0]
    n_dp, n_mp = lax.axis_size("dp"), lax.axis_size("mp")
    fine = n_dp // WAYS
    total = row_count * n_dp
    dp_at, mp_at = lax.axis_index("dp"), lax.axis_index("mp")
    idx = jnp.stack([dp_at // fine, mp_at, dp_at]).astype(jnp.int32)
    hw = w_qkv.shape[2] // 3

    def swap(x, axis, size, k):
        return lax.ppermute(x, axis, [(i, i ^ k) for i in range(size)])

    def dp(x, k):
        return swap(x, "dp", n_dp, k * fine)

    def mp(x, k):
        return swap(x, "mp", n_mp, k)

    def fine_rows(x):
        k = 1
        while k < fine:
            got = swap(x, "dp", n_dp, k)
            x = jnp.where((dp_at & k) == 0, jnp.concatenate([x, got], 0), jnp.concatenate([got, x], 0))
            k *= 2
        return x

    def fine_sum(x):
        k = 1
        while k < fine:
            x = x + swap(x, "dp", n_dp, k)
            k *= 2
        return x

    def gather8(own):
        parts = {0: own}
        for k in (2, 4, 6):
            parts[k] = dp(own, k)
        parts[1] = dp(own, 1)
        for k in (2, 4, 6):
            parts[k ^ 1] = dp(parts[k], 1)
        return [parts[k] for k in range(WAYS)]

    def gather4(own):
        far = mp(own, 2)
        return [own, mp(own, 1), far, mp(far, 1)]

    def scatter4(send, keep):
        got = mp(send, 1)
        return keep, got, mp((keep[1] + got[1].astype(F32)).astype(BF), 2)

    def scatter8(send, keep):
        part = keep + dp(send, 1).astype(F32)
        low = part.astype(BF)
        total_own = part[0]
        for i in range(1, WAYS // 2):
            total_own = total_own + dp(low[i], 2 * i).astype(F32)
        return fine_sum(total_own.astype(BF))

    out_rows = fine_rows(w_out[0].astype(BF))
    first = jnp.concatenate(
        [fine_rows(w_qkv[0].astype(BF)), pack_rows(out_rows, 3 * hw)], axis=0
    )
    first = gather8(first)
    up = gather8(fine_rows(w_up[0].astype(BF)))
    down = gather8(fine_rows(w_down[0].astype(BF)))
    attn_all = lax.all_gather(attn_norm, "mp")

    ends = jnp.cumsum(doc_lengths[0])
    places = jnp.arange(row_count, dtype=jnp.int32)
    start = jnp.max(jnp.where(ends[None, :] <= places[:, None], ends[None, :], 0), axis=1, keepdims=True)
    start = start.astype(jnp.int32)
    hat, _ = normalize(tokens.astype(F32))
    a_low = (hat * outer_norms[0] + outer_norms[1]).astype(BF)

    q, k, v, wq, wo = project(a_low, first, hw, idx)
    o, probs = attend(start, q, k, v, idx)
    wo_all = gather4(wo)
    o_all = gather4(o)
    hidden, c_low = outproj(attn_all, outer_norms, tokens, o_all, wo_all, idx)
    u, dw, stats, wu, wd = ffn_up(c_low, cotangent, ffn_norm, up, down, idx)
    stats = lax.all_gather(stats, "mp")
    w_low, du, dc_send, dc_keep, ffn_grads = ffn_mid(u, dw, stats, ffn_norm, wu, idx)
    dc = scatter4(dc_send, dc_keep)
    down_own = scatter8(*weight_grad(w_low, cotangent, idx, "grad_down"))
    up_own = scatter8(*weight_grad(c_low, du, idx, "grad_up"))
    bo = scatter4(*rel_matmul(w_low, wd, False, idx, "ffn_out"))
    dh, outer_late, attn_grads, *rest = shard_back(*dc, hidden, cotangent, attn_all, outer_norms, o_all, wo_all, idx)
    do, (go_send, go_keep) = rest[:n_mp], rest[n_mp:]
    do = [do[0]] + [mp(do[k], k) for k in range(1, n_mp)]
    go = scatter4(go_send, go_keep)
    grad_out_part = go[0][0] + go[1][0].astype(F32) + go[2].astype(F32)
    dqkv = attend_back(q, k, v, probs, do, idx)
    qkv_own = scatter8(*weight_grad(a_low, dqkv, idx, "grad_qkv", grad_out_part))
    da = scatter4(*rel_matmul(dqkv, wq, True, idx, "grad_a"))
    gt, outer_early = shard_end(*da, tokens, outer_norms, dh, idx)
    grad_tokens = spread_rows(gather4(gt), idx, "spread_tokens")
    h_own = lax.dynamic_slice_in_dim(hidden, mp_at * BLK, BLK, 0)
    out_own = (h_own + bo[0][0] + bo[1][0].astype(F32) + bo[2].astype(F32)).astype(BF)
    block_out = spread_rows(gather4(out_own), idx, "spread_out")

    outer_grads, attn_grads = lax.psum((jnp.concatenate([outer_early, outer_late], 0), attn_grads), "mp")
    attn_own = lax.dynamic_index_in_dim(attn_grads, mp_at, 0, False)
    vec = jnp.concatenate(
        [outer_grads.reshape(-1), attn_own.reshape(-1), ffn_grads.reshape(-1)]
    )
    size = vec.shape[0]
    vec = jnp.pad(vec, (0, -size % 1024)).reshape(-1, 128)
    step = 1
    while step < n_dp:
        vec = vec + swap(vec, "dp", n_dp, step)
        step *= 2
    vec = vec.reshape(-1)
    cut = outer_grads.size
    cut2 = cut + attn_own.size
    outer_grads = vec[:cut].reshape(outer_grads.shape)
    attn_grads = vec[cut:cut2].reshape(attn_own.shape)
    ffn_grads = vec[cut2:size].reshape(ffn_grads.shape)

    factor = VEC_RATE / math.sqrt(total)
    unit_factor = UNIT_RATE / math.sqrt(total)

    def update(pieces, w, left, right, left_root, right_root, packed, name):
        return precondition(
            pieces, w[0], left[0], right[0], left_root[0], right_root[0], total, packed, idx, name
        )

    down_pieces, up_pieces, qkv_pieces = gather8(down_own), gather8(up_own), gather8(qkv_own)
    down_res = update(down_pieces, w_down, left_down, right_down, left_root_down, right_root_down, None, "update_down")
    up_res = update(up_pieces, w_up, left_up, right_up, left_root_up, right_root_up, None, "update_up")
    out_res = update(qkv_pieces, w_out, left_out, right_out, left_root_out, right_root_out, "tail", "update_out")
    qkv_res = update(qkv_pieces, w_qkv, left_qkv, right_qkv, left_root_qkv, right_root_qkv, "head", "update_qkv")
    return (
        block_out,
        grad_tokens,
        outer_grads,
        attn_grads,
        ffn_grads,
        outer_norms - factor * outer_grads,
        attn_norm - factor * attn_grads,
        ffn_norm - unit_factor * ffn_grads,
        *(x[None] for x in qkv_res),
        *(x[None] for x in out_res),
        *(x[None] for x in up_res),
        *(x[None] for x in down_res),
    )


def solution(mesh):
    rows = P("dp", None)
    mats = (P("mp", "dp", None),) * 4 + (P("mp", None, None),)
    res = (P("mp", None, None),) + (P("mp", "dp", None),) * 4
    cols = P(None, "mp")
    return jax.shard_map(
        body,
        mesh=mesh,
        in_specs=(rows, rows, rows, P(), cols, cols) + mats * 4,
        out_specs=(rows, rows, P(), cols, cols, P(), cols, cols) + res * 4,
        check_vma=False,
    )
```

```python
import math

import jax
import jax.numpy as jnp
from jax import lax
from jax.experimental import pallas as pl
from jax.experimental.pallas import tpu as pltpu
from jax.sharding import PartitionSpec as P

HD = 64
EPS = 1e-05
DECAY = 0.5
MAT_RATE = 0.5
VEC_RATE = 0.05
UNIT_RATE = 0.3
GELU_A = math.sqrt(2.0 / math.pi)
GELU_B = 0.044715
BF = jnp.bfloat16
F32 = jnp.float32
VMEM = 22 * 1024 * 1024
WAYS = 8
RATE = 4e8
TICK = 5
BLK = 256
ORDER = (0, 4, 2, 6)


def full(shape):
    return pl.BlockSpec(shape, lambda *args: (0,) * len(shape))


def fulls(arrays):
    return [full(x.shape) for x in arrays]


def run(kernel, grid, ins, in_specs, outs, out_specs, idx, name, micros, scratch=(), after=(), hbm=()):
    count, kernel_in = len(ins), kernel
    ins = [pltpu.with_memory_space_constraint(x, pltpu.HBM) if i in hbm else x for i, x in enumerate(ins)]

    def kernel(idx, *refs):
        kernel_in(idx, *refs[:count], *refs[count + len(after) :])

    return pl.pallas_call(
        kernel,
        grid_spec=pltpu.PrefetchScalarGridSpec(
            num_scalar_prefetch=1,
            grid=grid,
            in_specs=list(in_specs) + [pl.BlockSpec(memory_space=pl.ANY)] * len(after),
            out_specs=out_specs,
            scratch_shapes=list(scratch),
        ),
        out_shape=outs,
        compiler_params=pltpu.CompilerParams(vmem_limit_bytes=VMEM),
        cost_estimate=pl.CostEstimate(flops=int(micros * RATE), bytes_accessed=1024, transcendentals=0),
        name=name,
    )(idx, *ins, *after)


def sds(shape, dtype):
    return jax.ShapeDtypeStruct(shape, dtype)


def near(shape, dtype):
    return pltpu.VMEM(shape, dtype)


def far(shape, dtype):
    return pltpu.HBM(shape, dtype)


def dot(x, y):
    return jnp.dot(x, y, preferred_element_type=F32)


def dot_nt(x, y):
    return lax.dot_general(x, y, (((1,), (1,)), ((), ())), preferred_element_type=F32)


def dot_tn(x, y):
    return lax.dot_general(x, y, (((0,), (0,)), ((), ())), preferred_element_type=F32)


def rowsum(x):
    return jnp.sum(x, -1, keepdims=True)


def normalize(x):
    n = x.shape[-1]
    off = x - rowsum(x) / n
    r = lax.rsqrt(rowsum(off * off) / n + EPS)
    return off * r, r


def gelu_parts(u):
    t = jnp.tanh(GELU_A * (u + GELU_B * (u * u * u)))
    return 0.5 * u * (1.0 + t), t


def unpack_rows(side, wide):
    groups = wide // side.shape[1]
    rows = side.shape[0] // groups
    return jnp.concatenate([side[i * rows : (i + 1) * rows] for i in range(groups)], axis=1)


def pack_rows(block, groups):
    n = block.shape[1] // groups
    return jnp.concatenate([block[:, i * n : (i + 1) * n] for i in range(groups)], axis=0)


def project_kernel(idx, a_ref, an_ref, *refs):
    pieces = refs[:WAYS]
    q_ref, k_ref, v_ref, wq_ref, wo_ref, scr = refs[WAYS:]
    rows = wq_ref.shape[0] // WAYS
    orows = scr.shape[0] // WAYS
    hw = q_ref.shape[1]

    @pl.when(pl.program_id(0) == 0)
    def _():
        for k in range(WAYS):
            j = jnp.bitwise_xor(idx[0], k)
            wq_ref[pl.ds(pl.multiple_of(j * rows, rows), rows), :] = pieces[k][:, : 3 * hw]
            tail = pieces[k][:, 3 * hw :].astype(F32)
            scr[pl.ds(pl.multiple_of(j * orows, orows), orows), :] = unpack_rows(tail, wo_ref.shape[1])
        wo_ref[:hw, :] = scr[...].astype(BF)
        norm = jnp.concatenate([an_ref[0:1, :], an_ref[1:2, :]], axis=1)
        high = norm.astype(BF).astype(F32)
        row = jnp.concatenate([high, norm - high], axis=1)
        pad = wo_ref.shape[0] - hw
        at = lax.broadcasted_iota(jnp.int32, (pad, row.shape[1]), 0)
        wo_ref[hw:, :] = jnp.where(at == 0, row, 0.0).astype(BF)

    res = dot(a_ref[...], wq_ref[...]).astype(BF)
    q_ref[...] = res[:, :hw] * BF(HD ** (-0.5))
    k_ref[...] = res[:, hw : 2 * hw]
    v_ref[...] = res[:, 2 * hw :]


def project(a, norm, pieces, hw, idx):
    rows, d = a.shape
    n = 3 * hw
    blk = lambda w: pl.BlockSpec((BLK, w), lambda s, i: (s, 0))
    return run(
        project_kernel,
        (rows // BLK,),
        [a, norm, *pieces],
        [blk(d), full(norm.shape)] + fulls(pieces),
        [far((rows, hw), BF)] * 3 + [far((d, n), BF), far((hw + 16, d), BF)],
        [blk(hw)] * 3 + [full((d, n)), full((hw + 16, d))],
        idx,
        "project",
        40,
        [pltpu.VMEM((hw, d), F32)],
    )


def attend_kernel(idx, start_ref, q_ref, k_ref, v_ref, o_ref, p_ref):
    h = pl.program_id(0)
    rows, hw = q_ref.shape
    lane = (lax.broadcasted_iota(jnp.int32, (1, hw), 1) // HD) == h
    for i in range(rows // BLK):
        lo, hi = i * BLK, (i + 1) * BLK
        qb = jnp.where(lane, q_ref[lo:hi, :], BF(0))
        s = dot_nt(qb, k_ref[:hi, :])
        kpos = lax.broadcasted_iota(jnp.int32, (BLK, hi), 1)
        qpos = lo + lax.broadcasted_iota(jnp.int32, (BLK, hi), 0)
        s = jnp.where((kpos >= start_ref[lo:hi, :]) & (kpos <= qpos), s, -1e30)
        p = jnp.exp(s - jnp.max(s, -1, keepdims=True))
        p = (p * (1.0 / rowsum(p))).astype(BF)
        p_ref[0, lo:hi, :hi] = p
        ob = dot(p, v_ref[:hi, :]).astype(BF)
        o_ref[lo:hi, :] = jnp.where(lane, ob, o_ref[lo:hi, :])


def attend(start, q, k, v, idx, after=()):
    rows, hw = q.shape
    heads = hw // HD
    return run(
        attend_kernel,
        (heads,),
        [start, q, k, v],
        fulls([start, q, k, v]),
        [far((rows, hw), BF), far((heads, rows, rows), BF)],
        [full((rows, hw)), pl.BlockSpec((1, rows, rows), lambda s, i: (s, 0, 0))],
        idx,
        "attend",
        10,
        after=after,
        hbm=(1, 2, 3),
    )


def wide_norm(o_refs):
    parts = [x[...].astype(F32) for x in o_refs]
    n = sum(x.shape[-1] for x in parts)
    mean = sum(rowsum(x) for x in parts) / n
    parts = [x - mean for x in parts]
    r = lax.rsqrt(sum(rowsum(x * x) for x in parts) / n + EPS)
    return [x * r for x in parts], r


def unpack_norm(w_ref):
    hw = w_ref.shape[0] - 16
    row = w_ref[hw:, :].astype(F32)[0:1, :]
    gain, bias, gain_low, bias_low = (row[:, i * hw : (i + 1) * hw] for i in range(4))
    return gain + gain_low, bias + bias_low


def outproj_kernel(idx, on_ref, tok_ref, *refs):
    g = (len(refs) - 2) // 2
    o_refs, w_refs = refs[:g], refs[g : 2 * g]
    h_ref, c_ref = refs[2 * g :]
    hats, _ = wide_norm(o_refs)
    acc = tok_ref[...].astype(F32)
    for k in range(g):
        gain, bias = unpack_norm(w_refs[k])
        y = (hats[k] * gain + bias).astype(BF)
        acc = acc + dot(y, w_refs[k][: gain.shape[1], :])
    h_ref[...] = acc
    hat, _ = normalize(acc)
    c_ref[...] = (hat * on_ref[2:3, :] + on_ref[3:4, :]).astype(BF)


def outproj(on, tok, o, w, idx, after=()):
    rows, d = tok.shape
    hw = o[0].shape[1]
    blk = lambda n: pl.BlockSpec((BLK, n), lambda s, i: (s, 0))
    return run(
        outproj_kernel,
        (rows // BLK,),
        [on, tok, *o, *w],
        fulls([on]) + [blk(d)] + [blk(hw)] * len(o) + fulls(w),
        [far((rows, d), F32), near((rows, d), BF)],
        [blk(d), blk(d)],
        idx,
        "outproj",
        0,
        after=after,
        hbm=range(1, 2 + 2 * len(o)),
    )


def ffn_up_kernel(idx, c_ref, e_ref, fn_ref, *refs):
    ups, downs = refs[:2], refs[2:6]
    u_ref, dw_ref, st_ref, wu_ref, wd_ref = refs[6:]
    rows = ups[0].shape[1]

    @pl.when(pl.program_id(0) == 0)
    def _():
        for i, k in enumerate(ORDER):
            for odd in range(2):
                j = jnp.bitwise_xor(idx[0], k + odd)
                at = pl.ds(pl.multiple_of(j * rows, rows), rows)
                wu_ref[at, :] = ups[odd][i]
                wd_ref[at, :] = downs[i][odd]

    u = dot(c_ref[...], wu_ref[...])
    u_ref[...] = u
    z, _ = gelu_parts(u)
    mean = rowsum(z) / z.shape[-1]
    z = z - mean
    dw = dot_nt(e_ref[...], wd_ref[...])
    dw_ref[...] = dw
    eg = dw * fn_ref[0:1, :]
    stats = [mean, rowsum(z * z), rowsum(eg), rowsum(eg * z)]
    place = lax.broadcasted_iota(jnp.int32, (BLK, 128), 1)
    tile = jnp.zeros((BLK, 128), F32)
    for i, x in enumerate(stats):
        tile = jnp.where(place == i, x, tile)
    st_ref[...] = tile.T[:8, :]


def ffn_up(c, e, fn, pieces, idx):
    rows, d = c.shape
    fl = fn.shape[1]
    rblk = lambda n: pl.BlockSpec((BLK, n), lambda s, i: (s, 0))
    return run(
        ffn_up_kernel,
        (rows // BLK,),
        [c, e, fn, *pieces],
        [rblk(d), rblk(d), full(fn.shape)] + fulls(pieces),
        [near((rows, fl), F32), near((rows, fl), F32), sds((8, rows), F32), near((d, fl), BF), far((fl, d), BF)],
        [rblk(fl), rblk(fl), pl.BlockSpec((8, BLK), lambda s, i: (0, s)), full((d, fl)), full((fl, d))],
        idx,
        "ffn_up",
        7.5,
        hbm=(1,) + tuple(range(3, 9)),
    )


def rel_of(s):
    return jnp.where(s < 2, 2 * s + 1, 2 * s - 4)


def rel_block(s, i):
    return jnp.bitwise_xor(rel_of(s), i[1])


def rel_spec(n):
    return pl.BlockSpec((BLK, n), lambda s, i: (rel_block(s, i), 0))


SEND_SPEC = lambda n: pl.BlockSpec((1, BLK, n), lambda s, i: (jnp.minimum(s, 1), 0, 0))
KEEP_SPEC = lambda n: pl.BlockSpec((1, BLK, n), lambda s, i: (jnp.maximum(s - 2, 0), 0, 0))


def put_rel(send_ref, keep_ref, value):
    @pl.when(pl.program_id(0) < 2)
    def _():
        send_ref[0] = value.astype(BF)

    @pl.when(pl.program_id(0) >= 2)
    def _():
        keep_ref[0] = value


def ffn_mid_kernel(idx, u_ref, dw_ref, st_ref, fn_ref, wu_ref, w_ref, du_ref, send_ref, keep_ref, fg_ref):
    g = st_ref.shape[0]
    fl = u_ref.shape[1]
    n = g * fl
    st = [st_ref[k] for k in range(g)]
    mean = sum(x[0:1] for x in st) / g
    gap = [x[0:1] - mean for x in st]
    spread = sum(x[1:2] + fl * (gp * gp) for x, gp in zip(st, gap)) / n
    r = lax.rsqrt(spread + EPS)
    s_plain = sum(x[2:3] for x in st) / n
    s_norm = r * (sum(x[3:4] + gp * x[2:3] for x, gp in zip(st, gap)) / n)
    cols = jnp.concatenate([mean, r, s_plain, s_norm, jnp.zeros((124, BLK), F32)], axis=0).T
    mean, r, s_plain, s_norm = (cols[:, i : i + 1] for i in range(4))
    u = u_ref[...]
    z, t = gelu_parts(u)
    hat = (z - mean) * r
    w_ref[...] = (hat * fn_ref[0:1, :] + fn_ref[1:2, :]).astype(BF)
    dw = dw_ref[...]
    dz = r * (dw * fn_ref[0:1, :] - s_plain - hat * s_norm)
    slope = 0.5 * (1.0 + t) + 0.5 * u * (1.0 - t * t) * (GELU_A * (1.0 + (3.0 * GELU_B) * (u * u)))
    du = (dz * slope).astype(BF)
    du_ref[...] = du
    put_rel(send_ref, keep_ref, dot_nt(du, wu_ref[...]))
    grads = jnp.concatenate([jnp.sum(dw * hat, 0, keepdims=True), jnp.sum(dw, 0, keepdims=True)], axis=0)

    @pl.when(pl.program_id(0) == 0)
    def _():
        fg_ref[...] = grads

    @pl.when(pl.program_id(0) > 0)
    def _():
        fg_ref[...] += grads


def ffn_mid(u, dw, st, fn, wu, idx):
    rows, fl = u.shape
    d = wu.shape[0]
    return run(
        ffn_mid_kernel,
        (rows // BLK,),
        [u, dw, st, fn, wu],
        [rel_spec(fl), rel_spec(fl), pl.BlockSpec((st.shape[0], 8, BLK), lambda s, i: (0, 0, rel_block(s, i)))]
        + fulls([fn, wu]),
        [far((rows, fl), BF), far((rows, fl), BF), sds((2, BLK, d), BF), far((2, BLK, d), F32), sds((2, fl), F32)],
        [rel_spec(fl), rel_spec(fl), SEND_SPEC(d), KEEP_SPEC(d), full((2, fl))],
        idx,
        "ffn_mid",
        6.5,
    )


def ffn_out(x, w, idx, after):
    rows, depth = x.shape
    d = w.shape[1]

    def kernel(idx, x_ref, w_ref, send_ref, keep_ref):
        put_rel(send_ref, keep_ref, dot(x_ref[...], w_ref[...]))

    return run(
        kernel,
        (rows // BLK,),
        [x, w],
        [rel_spec(depth), full(w.shape)],
        [sds((2, BLK, d), BF), far((2, BLK, d), F32)],
        [SEND_SPEC(d), KEEP_SPEC(d)],
        idx,
        "ffn_out",
        0,
        (),
        after,
        (0, 1),
    )


def put_blocks(scr, send_ref, keep_ref, first, step):
    for i, k in enumerate(ORDER):
        for odd, dest in enumerate((keep_ref, send_ref)):
            j = jnp.bitwise_xor(first, k + odd)
            value = scr[pl.ds(pl.multiple_of(j * step, step), step), :]
            dest[i, :, : value.shape[1]] = value.astype(dest.dtype)


def weight_grad(x, y, idx, name, after=()):
    rows, d = x.shape
    n = y.shape[1]
    step = d // WAYS
    steps = d // BLK

    def kernel(idx, x_ref, y_ref, send_ref, keep_ref, scr):
        s = pl.program_id(0)
        scr[pl.ds(pl.multiple_of(s * BLK, BLK), BLK), :] = dot_tn(x_ref[...], y_ref[...])

        @pl.when(s == steps - 1)
        def _():
            put_blocks(scr, send_ref, keep_ref, idx[0], step)

    return run(
        kernel,
        (steps,),
        [x, y],
        [pl.BlockSpec((rows, BLK), lambda s, i: (0, s)), full(y.shape)],
        [sds((WAYS // 2, step, n), BF), far((WAYS // 2, step, n), F32)],
        [full((WAYS // 2, step, n))] * 2,
        idx,
        name,
        3.5,
        [pltpu.VMEM((d, n), F32)],
        after,
    )


def qkv_back(a, dqkv, wq, go, idx, after=()):
    rows, d = a.shape
    n = dqkv.shape[1]
    step = d // WAYS
    hw = go[2].shape[0]
    groups = d // hw
    orows = hw // WAYS

    def kernel(idx, a_ref, d_ref, w_ref, go0_ref, go1_ref, go2_ref, gs_ref, gk_ref, send_ref, keep_ref, scr, go_ref):
        go_ref[...] = go0_ref[0] + go1_ref[0].astype(F32) + go2_ref[...].astype(F32)
        for s in range(d // BLK):
            scr[s * BLK : (s + 1) * BLK, :] = dot_tn(a_ref[:, s * BLK : (s + 1) * BLK], d_ref[...])
        put_blocks(scr, gs_ref, gk_ref, idx[0], step)
        for i, k in enumerate(ORDER):
            for odd, dest in enumerate((gk_ref, gs_ref)):
                j = jnp.bitwise_xor(idx[0], k + odd)
                tail = pack_rows(go_ref[pl.ds(pl.multiple_of(j * orows, orows), orows), :], groups)
                dest[i, :, n:] = tail.astype(dest.dtype)
        for k in range(4):
            j = jnp.bitwise_xor(idx[1], k)
            dest = send_ref if k % 2 else keep_ref
            value = dot_nt(d_ref[pl.ds(pl.multiple_of(j * BLK, BLK), BLK), :], w_ref[...])
            dest[k // 2] = value.astype(dest.dtype)

    ins = [a, dqkv, wq, *go]
    lead = pl.BlockSpec((1, hw, d), lambda s, i: (0, 0, 0))
    half = (WAYS // 2, step, d)
    part = (2, BLK, d)
    outs = [sds(half, BF), far(half, F32), sds(part, BF), far(part, F32)]
    return run(
        kernel, (1,), ins, fulls(ins[:3]) + [lead, lead, full(go[2].shape)], outs, fulls(outs), idx, "qkv_back", 5.5,
        [pltpu.VMEM((d, n), F32), pltpu.VMEM((hw, d), F32)],
        after=after,
        hbm=(0, 2, 3),
    )


def shard_back_kernel(idx, dc0_ref, dc1_ref, dc2_ref, h_ref, e_ref, on_ref, *refs):
    g = 4
    o_refs, w_refs = refs[:g], refs[g : 2 * g]
    dh_ref, ol_ref, ag_ref, *do_refs = refs[2 * g :]
    do_refs, (gs_ref, gk_ref) = do_refs[:g], do_refs[g:]
    dc = dc0_ref[0] + dc1_ref[0].astype(F32) + dc2_ref[...].astype(F32)
    hat, r = normalize(h_ref[...])
    wgt = dc * on_ref[2:3, :]
    n = dc.shape[-1]
    dh = e_ref[...].astype(F32) + r * (wgt - rowsum(wgt) / n - hat * (rowsum(wgt * hat) / n))
    dh_ref[...] = dh
    ol_ref[...] = jnp.concatenate([jnp.sum(dc * hat, 0, keepdims=True), jnp.sum(dc, 0, keepdims=True)], axis=0)
    dhb = dh.astype(BF)
    hats, r = wide_norm(o_refs)
    norms = [unpack_norm(w_refs[k]) for k in range(g)]
    dys = [dot_nt(dhb, w_refs[k][: norms[k][0].shape[1], :]) for k in range(g)]
    wgts = [dys[k] * norms[k][0] for k in range(g)]
    s_plain = sum(rowsum(x) for x in wgts) / n
    s_norm = sum(rowsum(x * y) for x, y in zip(wgts, hats)) / n
    for k in range(g):
        do_refs[k][...] = (r * (wgts[k] - s_plain - hats[k] * s_norm)).astype(BF)
        ag_ref[jnp.bitwise_xor(idx[1], k)] = jnp.concatenate(
            [jnp.sum(dys[k] * hats[k], 0, keepdims=True), jnp.sum(dys[k], 0, keepdims=True)], axis=0
        )
    for k in range(g):
        y = (hats[k] * norms[k][0] + norms[k][1]).astype(BF)
        dest = gs_ref if k % 2 else gk_ref
        dest[k // 2] = dot_tn(y, dhb).astype(dest.dtype)


def shard_back(dc_keep, dc_one, dc_two, h, e, on, o, w, idx, after):
    rows, d = h.shape
    g = len(o)
    hw = o[0].shape[1]
    mine = lambda n: pl.BlockSpec((BLK, n), lambda s, i: (i[1], 0))
    lead = pl.BlockSpec((1, BLK, d), lambda s, i: (0, 0, 0))
    ins = [dc_keep, dc_one, dc_two, h, e, on, *o, *w]
    return run(
        shard_back_kernel,
        (1,),
        ins,
        [lead, lead, full((BLK, d)), mine(d), mine(d)] + fulls([on]) + [mine(hw)] * g + fulls(w),
        [far((BLK, d), F32), sds((2, d), F32), sds((g, 2, hw), F32)]
        + [sds((BLK, hw), BF)] * g
        + [sds((2, hw, d), BF), far((2, hw, d), F32)],
        [full((BLK, d)), full((2, d)), full((g, 2, hw))]
        + [full((BLK, hw))] * g
        + [full((2, hw, d))] * 2,
        idx,
        "shard_back",
        0,
        after=after,
        hbm=(0, 1, 2, 3, 4) + tuple(range(6, 6 + 2 * g)),
    )


def attend_back_kernel(idx, q_ref, k_ref, v_ref, p_ref, *refs):
    d_refs = refs[:4]
    out_ref, do_scr, dq_scr, dk_scr, dv_scr = refs[4:]
    h = pl.program_id(0)
    rows, hw = q_ref.shape

    @pl.when(h == 0)
    def _():
        for k in range(4):
            j = jnp.bitwise_xor(idx[1], k)
            do_scr[pl.ds(pl.multiple_of(j * BLK, BLK), BLK), :] = d_refs[k][...]
        dk_scr[...] = jnp.zeros_like(dk_scr)
        dv_scr[...] = jnp.zeros_like(dv_scr)
        dq_scr[...] = jnp.zeros_like(dq_scr)

    lane = (lax.broadcasted_iota(jnp.int32, (1, hw), 1) // HD) == h
    for i in range(rows // BLK):
        lo, hi = i * BLK, (i + 1) * BLK
        dob = jnp.where(lane, do_scr[lo:hi, :], BF(0))
        qb = jnp.where(lane, q_ref[lo:hi, :], BF(0))
        pb = p_ref[0, lo:hi, :hi]
        p = pb.astype(F32)
        dp = dot_nt(dob, v_ref[:hi, :])
        ds = (p * (dp - rowsum(p * dp))).astype(BF)
        dq_scr[lo:hi, :] = jnp.where(lane, dot(ds, k_ref[:hi, :]), dq_scr[lo:hi, :])
        dk_scr[:hi, :] += dot_tn(ds, qb)
        dv_scr[:hi, :] += dot_tn(pb, dob)

    @pl.when(h == pl.num_programs(0) - 1)
    def _():
        out_ref[...] = jnp.concatenate([dq_scr[...] * HD ** (-0.5), dk_scr[...], dv_scr[...]], axis=1).astype(BF)


def attend_back(q, k, v, p, do, idx, after):
    rows, hw = q.shape
    heads = hw // HD
    return run(
        attend_back_kernel,
        (heads,),
        [q, k, v, p, *do],
        fulls([q, k, v]) + [pl.BlockSpec((1, rows, rows), lambda s, i: (s, 0, 0))] + fulls(do),
        [sds((rows, 3 * hw), BF)],
        [full((rows, 3 * hw))],
        idx,
        "attend_back",
        11,
        [pltpu.VMEM((rows, hw), BF)] + [pltpu.VMEM((rows, hw), F32)] * 3,
        after=after,
        hbm=range(8),
    )[0]


def shard_end_kernel(idx, da0_ref, da1_ref, da2_ref, tok_ref, on_ref, dh_ref, gt_ref, oe_ref):
    da = da0_ref[0] + da1_ref[0].astype(F32) + da2_ref[...].astype(F32)
    hat, r = normalize(tok_ref[...].astype(F32))
    wgt = da * on_ref[0:1, :]
    n = da.shape[-1]
    grad = r * (wgt - rowsum(wgt) / n - hat * (rowsum(wgt * hat) / n))
    gt_ref[...] = (dh_ref[...] + grad).astype(BF)
    oe_ref[...] = jnp.concatenate([jnp.sum(da * hat, 0, keepdims=True), jnp.sum(da, 0, keepdims=True)], axis=0)


def shard_end(da_keep, da_one, da_two, tok, on, dh, idx, after=()):
    d = tok.shape[1]
    lead = pl.BlockSpec((1, BLK, d), lambda s, i: (0, 0, 0))
    return run(
        shard_end_kernel,
        (1,),
        [da_keep, da_one, da_two, tok, on, dh],
        [lead, lead, full((BLK, d)), pl.BlockSpec((BLK, d), lambda s, i: (i[1], 0)), full(on.shape), full((BLK, d))],
        [sds((BLK, d), BF), sds((2, d), F32)],
        [full((BLK, d)), full((2, d))],
        idx,
        "shard_end",
        0,
        after=after,
    )


def spread_rows(parts, idx, name, after=()):
    rows, d = parts[0].shape

    def kernel(idx, *refs):
        for k, part in enumerate(refs[:-1]):
            at = pl.ds(pl.multiple_of(jnp.bitwise_xor(idx[1], k) * rows, rows), rows)
            refs[-1][at, :] = part[...]

    out = (rows * len(parts), d)
    return run(kernel, (1,), parts, fulls(parts), [far(out, BF)], [full(out)], idx, name, 2, (), after)[0]


def far_sum(keep, got, idx, after=(), tick=TICK):
    rows, d = keep.shape[1:]

    def kernel(idx, keep_ref, got_ref, out_ref):
        out_ref[...] = (keep_ref[0] + got_ref[0].astype(F32)).astype(BF)

    second = pl.BlockSpec((1, rows, d), lambda s, i: (1, 0, 0))
    out = [sds((rows, d), BF)]
    return run(kernel, (1,), [keep, got], [second] * 2, out, fulls(out), idx, "far_sum", tick, (), after)[0]


def fold(keep, got, idx, after=(), tick=TICK):
    count, rows, d = keep.shape
    half = count // 2

    def kernel(idx, keep_ref, got_ref, stay_ref, send_ref):
        stay_ref[...] = keep_ref[:half] + got_ref[:half].astype(F32)
        send = (keep_ref[half:] + got_ref[half:].astype(F32)).astype(BF)
        send_ref[...] = send if half > 1 else send[0]

    outs = [sds((half, rows, d), F32), sds((half, rows, d) if half > 1 else (rows, d), BF)]
    return run(kernel, (1,), [keep, got], fulls([keep, got]), outs, fulls(outs), idx, "fold", tick, (), after)


def close(own, got, idx, after=(), vec=None):
    rows, d = got[0].shape

    def kernel(idx, own_ref, *refs):
        out_ref = refs[-1]
        total = own_ref[...].reshape(rows, d)
        for ref in refs[: len(got)]:
            total = total + ref[...].astype(F32)
        out_ref[:rows, :] = total.astype(BF)
        if vec is not None:
            x = refs[len(got)][...]
            high = x.astype(BF).astype(F32)
            out_ref[rows:, :] = jnp.concatenate([high, x - high], axis=0).astype(BF)

    ins = [own, *got] + ([] if vec is None else [vec])
    out = [sds((rows if vec is None else rows + 2 * vec.shape[0], d), BF)]
    return run(kernel, (1,), ins, fulls(ins), out, fulls(out), idx, "close", TICK, (), after)[0]


def join(parts, idx, after=()):
    shapes = [x.shape if len(x.shape) == 3 else (1, *x.shape) for x in parts]

    def kernel(idx, *refs):
        at = 0
        for ref, shape in zip(refs, shapes):
            refs[-1][at : at + shape[0]] = ref[...].reshape(shape)
            at += shape[0]

    out = [sds((sum(x[0] for x in shapes), *shapes[0][1:]), BF)]
    return run(kernel, (1,), parts, fulls(parts), out, fulls(out), idx, "join", 2 * TICK, (), after)[0]


def block_end(h, keep, got, last, idx, after=()):
    rows, d = last.shape

    def kernel(idx, h_ref, keep_ref, got_ref, last_ref, out_ref):
        total = h_ref[...] + keep_ref[0] + got_ref[0].astype(F32) + last_ref[...].astype(F32)
        out_ref[...] = total.astype(BF)

    lead = pl.BlockSpec((1, rows, d), lambda s, i: (0, 0, 0))
    mine = pl.BlockSpec((rows, d), lambda s, i: (i[1], 0))
    ins = [h, keep, got, last]
    out = [sds((rows, d), BF)]
    return run(
        kernel, (1,), ins, [mine, lead, lead, full((rows, d))], out, fulls(out), idx, "block_end", TICK, (), after, (0,)
    )[0]


def vec_add(x, y, idx, after=()):
    def kernel(idx, x_ref, y_ref, out_ref):
        out_ref[...] = x_ref[...] + y_ref[...]

    out = [sds(x.shape, F32)]
    return run(kernel, (1,), [x, y], fulls([x, y]), out, fulls(out), idx, "vec_add", TICK, (), after)[0]


def one_hot(place, count, width):
    at = lax.broadcasted_iota(jnp.int32, (count, width), 1)
    want = place * count + lax.broadcasted_iota(jnp.int32, (count, width), 0)
    return jnp.where(at == want, 1.0, 0.0).astype(BF)


def precondition(idx, ins, outs, scr, total, flip):
    w_ref, l_ref, r_ref, lr_ref, rr_ref = ins
    g_ref, nl_ref, nr_ref, nw_ref, copy_ref = outs
    d, n = scr.shape
    rows, side = w_ref.shape[0], r_ref.shape[0]
    whole = scr[...]
    g_ref[...] = whole.T if flip else whole
    grad = whole.astype(BF)
    scale = 1.0 / total
    own_cols = dot_nt(one_hot(idx[2], side, n), grad).astype(BF)
    own_rows = dot(one_hot(idx[2], rows, d), grad).astype(BF)
    nr_ref[...] = DECAY * r_ref[...] + ((1.0 - DECAY) * scale * scale) * dot(own_cols, grad)
    nl_ref[...] = DECAY * l_ref[...] + ((1.0 - DECAY) * scale * scale) * dot_nt(own_rows, grad)
    part = dot(lr_ref[...].astype(BF), grad).astype(BF)
    new = w_ref[...] - (MAT_RATE * scale) * dot(part, rr_ref[...].astype(BF))
    nw_ref[...] = new
    copy_ref[...] = new.astype(BF)


def update_outs(mats):
    w, left, right = mats[:3]
    (rows, n), d, side = w.shape, left.shape[1], right.shape[0]
    flip = n % 128 != 0
    outs = [sds((n, d) if flip else (d, n), F32), sds((rows, d), F32), sds((side, n), F32)]
    return outs + [sds((rows, n), F32), sds((rows, n), BF)], flip, pltpu.VMEM((d, n), F32)


def update_one(mats, near_blocks, far_blocks, total, idx, name, after=()):
    outs, flip, scr = update_outs(mats)
    step = mats[1].shape[1] // WAYS

    def kernel(idx, *refs):
        ins, (even, odd), rest = refs[:5], refs[5:7], refs[7:]
        for i, k in enumerate(ORDER):
            for far_one, blocks in enumerate((even, odd)):
                j = jnp.bitwise_xor(idx[0], k + far_one)
                rest[5][pl.ds(pl.multiple_of(j * step, step), step), :] = blocks[i].astype(F32)
        precondition(idx, ins, rest[:5], rest[5], total, flip)

    ins = [*mats, near_blocks, far_blocks]
    res = run(kernel, (1,), ins, fulls(ins), outs, fulls(outs), idx, name, 4, [scr], after, range(7))
    return [res[0].T if flip else res[0], *res[1:]]


def update_pair(mats, mats2, near_blocks, far_blocks, params, rates, total, idx, name, after=()):
    outs, flip, scr = update_outs(mats)
    outs2, flip2, scr2 = update_outs(mats2)
    step, n = mats[1].shape[1] // WAYS, mats[0].shape[1]
    step2, n2 = mats2[1].shape[1] // WAYS, mats2[0].shape[1]
    half = params.shape[0]

    def kernel(idx, *refs):
        ins, ins2, (even, odd), par_ref, rest = refs[:5], refs[5:10], refs[10:12], refs[12], refs[13:]
        sums = 0.0
        for i, k in enumerate(ORDER):
            for far_one, blocks in enumerate((even, odd)):
                j = jnp.bitwise_xor(idx[0], k + far_one)
                block = blocks[i].astype(F32)
                rest[-2][pl.ds(pl.multiple_of(j * step, step), step), :] = block[:step, :n]
                rest[-1][pl.ds(pl.multiple_of(j * step2, step2), step2), :] = unpack_rows(block[:step, n:], n2)
                sums = sums + (block[step : step + half] + block[step + half :])
        at = lax.broadcasted_iota(jnp.int32, sums.shape, 0) * sums.shape[1]
        at = at + lax.broadcasted_iota(jnp.int32, sums.shape, 1)
        slow, fast, border = rates
        rest[10][...] = sums
        rest[11][...] = par_ref[...] - jnp.where(at < border, slow, fast) * sums
        precondition(idx, ins2, rest[5:10], rest[-1], total, flip2)
        precondition(idx, ins, rest[:5], rest[-2], total, flip)

    all_outs = outs + outs2 + [sds(params.shape, F32)] * 2
    ins = [*mats, *mats2, near_blocks, far_blocks, params]
    res = run(kernel, (1,), ins, fulls(ins), all_outs, fulls(all_outs), idx, name, 6, [scr, scr2], after, range(13))
    res = list(res)
    res[0] = res[0].T if flip else res[0]
    res[5] = res[5].T if flip2 else res[5]
    return res[:5], res[5:10], res[10], res[11]


def body(
    tokens,
    cotangent,
    doc_lengths,
    outer_norms,
    attn_norm,
    ffn_norm,
    w_qkv,
    left_qkv,
    right_qkv,
    left_root_qkv,
    right_root_qkv,
    w_out,
    left_out,
    right_out,
    left_root_out,
    right_root_out,
    w_up,
    left_up,
    right_up,
    left_root_up,
    right_root_up,
    w_down,
    left_down,
    right_down,
    left_root_down,
    right_root_down,
):
    row_count = tokens.shape[0]
    n_dp, n_mp = lax.axis_size("dp"), lax.axis_size("mp")
    fine = n_dp // WAYS
    total = row_count * n_dp
    dp_at, mp_at = lax.axis_index("dp"), lax.axis_index("mp")
    idx = jnp.stack([dp_at // fine, mp_at, dp_at]).astype(jnp.int32)
    hw = w_qkv.shape[2] // 3

    def swap(x, axis, size, k):
        return lax.ppermute(x, axis, [(i, i ^ k) for i in range(size)])

    def dp(x, k):
        return swap(x, "dp", n_dp, k * fine)

    def mp(x, k):
        return swap(x, "mp", n_mp, k)

    def fine_rows(x):
        k = 1
        while k < fine:
            got = swap(x, "dp", n_dp, k)
            x = jnp.where((dp_at & k) == 0, jnp.concatenate([x, got], 0), jnp.concatenate([got, x], 0))
            k *= 2
        return x

    def fine_sum(x):
        k = 1
        while k < fine:
            x = x + swap(x, "dp", n_dp, k)
            k *= 2
        return x

    def gather8(own, *early):
        parts = {0: own}
        for k in (2, 4, 6):
            parts[k] = dp(own, k)
        parts[1] = dp(own, 1)
        for k in (2, 4, 6):
            parts[k ^ 1] = dp(after(parts[k], *early) if early else parts[k], 1)
        return [parts[k] for k in range(WAYS)]

    def gather4(own):
        far = mp(own, 2)
        return [own, mp(own, 1), far, mp(far, 1)]

    def scatter4(send, keep):
        got = mp(send, 1)
        return keep, got, mp((keep[1] + got[1].astype(F32)).astype(BF), 2)

    def gather8_halves(own):
        two = jnp.stack([own, dp(own, 4)])
        four = jnp.concatenate([two, dp(two, 2)])
        return four, dp(four, 1)

    def after(x, *deps):
        return lax.optimization_barrier((x, *deps))[0]

    out_rows = fine_rows(w_out[0].astype(BF))
    groups = tokens.shape[1] // hw
    first = jnp.concatenate([fine_rows(w_qkv[0].astype(BF)), pack_rows(out_rows, groups)], axis=1)
    up_own = fine_rows(w_up[0].astype(BF))
    down_own = fine_rows(w_down[0].astype(BF))
    down_two = jnp.stack([down_own, dp(down_own, 1)])
    first = gather8(first, down_two)

    ends = jnp.cumsum(doc_lengths[0])
    places = jnp.arange(row_count, dtype=jnp.int32)
    start = jnp.max(jnp.where(ends[None, :] <= places[:, None], ends[None, :], 0), axis=1, keepdims=True)
    start = start.astype(jnp.int32)
    hat, _ = normalize(tokens.astype(F32))
    a_low = (hat * outer_norms[0] + outer_norms[1]).astype(BF)

    up_go = after(up_own, first[2], first[4], first[6], down_two)
    up_z = [dp(up_go, k) for k in ORDER[1:]]
    q, k, v, wq, wo = project(a_low, attn_norm, first, hw, idx)
    wo_far = mp(wo, 2)
    o, probs = attend(start, q, k, v, idx)
    o, *up_z = lax.optimization_barrier((o, *up_z))
    up_four = jnp.stack([up_own, *up_z])
    o, wo, wo_far, up_four = lax.optimization_barrier((o, wo, wo_far, up_four))
    o_far = mp(o, 2)
    up_x = dp(up_four, 1)
    down_go = after(down_two, up_four)
    down_z = [dp(down_go, k) for k in ORDER[1:]]
    o_near, wo_near, wo_last = mp(after(o, o_far), 1), mp(after(wo, o_far), 1), mp(after(wo_far, o_far), 1)
    o_all = [o, o_near, o_far, mp(o_far, 1)]
    wo_all = [wo, wo_near, wo_far, wo_last]
    hidden, c_low = outproj(outer_norms, tokens, o_all, wo_all, idx, [up_x])
    u, dw, stats, wu, wd = ffn_up(c_low, cotangent, ffn_norm, [up_four, up_x, down_two, *down_z], idx)
    stats = lax.all_gather(stats, "mp")
    w_low, du, dc_send, dc_keep, ffn_grads = ffn_mid(u, dw, stats, ffn_norm, wu, idx)
    dc_got = mp(dc_send, 1)
    dc_sum = far_sum(dc_keep, dc_got, idx)
    down_send, down_keep = weight_grad(w_low, cotangent, idx, "grad_down", [dc_sum])
    down_x = dp(down_send, 1)
    up_send, up_keep = weight_grad(c_low, du, idx, "grad_up", [down_send])
    up_x2 = dp(after(up_send, down_send), 1)
    dh, outer_late, attn_grads, *rest = shard_back(
        dc_keep, dc_got, mp(dc_sum, 2), hidden, cotangent, outer_norms, o_all, wo_all, idx, [up_send]
    )
    do, (go_send, go_keep) = rest[:n_mp], rest[n_mp:]
    do = [do[0]] + [mp(do[k], k) for k in range(1, n_mp)]
    go_got = mp(go_send, 1)
    down_t, down_low = fold(down_keep, down_x, idx, [do[1]], 0)
    go_sum = far_sum(go_keep, go_got, idx, [down_low], 0)
    dqkv = attend_back(q, k, v, probs, do, idx, [go_sum])
    down_z1 = dp(down_low, 2)
    go_far = mp(go_sum, 2)
    down_t, down_low = fold(down_t, down_z1, idx, [dqkv])
    up_t, up_low = fold(up_keep, up_x2, idx, [down_low])
    qkv_send, qkv_keep, da_send, da_keep = qkv_back(a_low, dqkv, wq, [go_keep, go_got, go_far], idx, [up_low])

    down_z2, up_z1 = dp(down_low, 4), dp(up_low, 2)
    qkv_x = dp(qkv_send, 1)
    da_got = mp(da_send, 1)
    da_sum = far_sum(da_keep, da_got, idx)
    da_far = mp(da_sum, 2)
    down_done = fine_sum(close(down_t, [down_z2], idx, [da_sum]))
    down_r4 = dp(down_done, 4)
    up_t, up_low = fold(up_t, up_z1, idx, [down_done])
    up_z2 = dp(up_low, 4)
    bo_send, bo_keep = ffn_out(w_low, wd, idx, [up_low])
    bo_got = mp(bo_send, 1)
    qkv_t, qkv_low = fold(qkv_keep, qkv_x, idx, [bo_send], 0)
    qkv_z1 = dp(qkv_low, 2)
    gt, outer_early = shard_end(da_keep, da_got, da_far, tokens, outer_norms, dh, idx, [qkv_low])
    gt_far = mp(gt, 2)
    lanes = outer_late.shape[1]
    vec = jnp.concatenate([outer_early, outer_late, attn_grads.reshape(-1, lanes)])
    vec_got = mp(vec, 1)
    down_two = join([down_done, down_r4], idx, [gt])
    down_r2 = dp(down_two, 2)
    up_done = fine_sum(close(up_t, [up_z2], idx, [down_two]))
    up_r4 = dp(up_done, 4)
    vec = vec_add(vec, vec_got, idx, [up_done])
    vec_got = mp(vec, 2)
    bo_sum = far_sum(bo_keep, bo_got, idx, [vec])
    bo_far = mp(bo_sum, 2)
    qkv_t, qkv_low = fold(qkv_t, qkv_z1, idx, [bo_sum])
    qkv_z2 = dp(qkv_low, 4)
    out_own = block_end(hidden, bo_keep, bo_got, bo_far, idx, [qkv_low])
    out_far = mp(out_own, 2)
    gt_far = after(gt_far, out_own)
    gt_all = [gt, mp(after(gt, gt_far), 1), gt_far, mp(gt_far, 1)]
    down_four = join([down_two, down_r2], idx, [out_own])
    down_other = dp(down_four, 1)
    vec = vec_add(vec, vec_got, idx, [down_four])
    up_two = join([up_done, up_r4], idx, [vec])
    up_r2 = dp(up_two, 2)
    grad_tokens = spread_rows(gt_all, idx, "spread_tokens", [up_two])
    attn_own = lax.dynamic_index_in_dim(vec[4:].reshape(attn_grads.shape), mp_at, 0, False)

    def flat(*parts):
        x = jnp.concatenate([p.reshape(-1) for p in parts])
        return jnp.pad(x, (0, WAYS * lanes - x.shape[0])).reshape(WAYS, lanes)

    vec = fine_sum(flat(vec[:4], attn_own, ffn_grads))
    cut = outer_norms.size
    cut2 = cut + attn_norm.size
    size = cut2 + ffn_norm.size
    params = flat(outer_norms, attn_norm, ffn_norm)
    rates = (VEC_RATE / math.sqrt(total), UNIT_RATE / math.sqrt(total), cut2)

    qkv_own = close(qkv_t, [qkv_z2], idx, [grad_tokens], None if fine > 1 else vec)
    if fine > 1:
        high = vec.astype(BF)
        qkv_own = jnp.concatenate([fine_sum(qkv_own), high, (vec - high.astype(F32)).astype(BF)])
    qkv_z = [dp(qkv_own, k) for k in ORDER[1:]]
    up_four = join([up_two, up_r2], idx, [qkv_own])
    up_other = dp(up_four, 1)
    down_mats = [x[0] for x in (w_down, left_down, right_down, left_root_down, right_root_down)]
    down_res = update_one(down_mats, down_four, down_other, total, idx, "update_down", [up_four])
    qkv_four = join([qkv_own, *qkv_z], idx, [down_res[3]])
    qkv_other = dp(qkv_four, 1)
    out_far = after(out_far, qkv_four)
    out_all = [out_own, mp(after(out_own, out_far), 1), out_far, mp(out_far, 1)]
    block_out = spread_rows(out_all, idx, "spread_out", [qkv_four])

    def mats(*arrays):
        return [x[0] for x in arrays]

    up_mats = mats(w_up, left_up, right_up, left_root_up, right_root_up)
    up_res = update_one(up_mats, up_four, up_other, total, idx, "update_up", [block_out])
    qkv_res, out_res, vec, new_vec = update_pair(
        mats(w_qkv, left_qkv, right_qkv, left_root_qkv, right_root_qkv),
        mats(w_out, left_out, right_out, left_root_out, right_root_out),
        qkv_four,
        qkv_other,
        params,
        rates,
        total,
        idx,
        "update_qkv",
        [up_res[3]],
    )

    def cut_up(x):
        x = x.reshape(-1)
        return (
            x[:cut].reshape(outer_norms.shape),
            x[cut:cut2].reshape(attn_norm.shape),
            x[cut2:size].reshape(ffn_norm.shape),
        )

    return (
        block_out,
        grad_tokens,
        *cut_up(vec),
        *cut_up(new_vec),
        *(x[None] for x in qkv_res),
        *(x[None] for x in out_res),
        *(x[None] for x in up_res),
        *(x[None] for x in down_res),
    )


def solution(mesh):
    rows = P("dp", None)
    mats = (P("mp", "dp", None),) * 4 + (P("mp", None, None),)
    res = (P("mp", None, None),) + (P("mp", "dp", None),) * 4
    cols = P(None, "mp")
    return jax.shard_map(
        body,
        mesh=mesh,
        in_specs=(rows, rows, rows, P(), cols, cols) + mats * 4,
        out_specs=(rows, rows, P(), cols, cols, P(), cols, cols) + res * 4,
        check_vma=False,
    )
```

```python
import math

import jax
import jax.numpy as jnp
from jax import lax
from jax.experimental import pallas as pl
from jax.experimental.pallas import tpu as pltpu
from jax.sharding import PartitionSpec as P

HD = 64
EPS = 1e-05
DECAY = 0.5
MAT_RATE = 0.5
VEC_RATE = 0.05
UNIT_RATE = 0.3
GELU_A = math.sqrt(2.0 / math.pi)
GELU_B = 0.044715
BF = jnp.bfloat16
F32 = jnp.float32
VMEM = 22 * 1024 * 1024
WAYS = 8
RATE = 4e8
TICK = 5
BLK = 256
ORDER = (0, 4, 2, 6)


def full(shape):
    return pl.BlockSpec(shape, lambda *args: (0,) * len(shape))


def fulls(arrays):
    return [full(x.shape) for x in arrays]


def run(kernel, grid, ins, in_specs, outs, out_specs, idx, name, micros, scratch=(), after=(), hbm=()):
    count, kernel_in = len(ins), kernel
    ins = [pltpu.with_memory_space_constraint(x, pltpu.HBM) if i in hbm else x for i, x in enumerate(ins)]

    def kernel(idx, *refs):
        kernel_in(idx, *refs[:count], *refs[count + len(after) :])

    return pl.pallas_call(
        kernel,
        grid_spec=pltpu.PrefetchScalarGridSpec(
            num_scalar_prefetch=1,
            grid=grid,
            in_specs=list(in_specs) + [pl.BlockSpec(memory_space=pl.ANY)] * len(after),
            out_specs=out_specs,
            scratch_shapes=list(scratch),
        ),
        out_shape=outs,
        compiler_params=pltpu.CompilerParams(vmem_limit_bytes=VMEM),
        cost_estimate=pl.CostEstimate(flops=int(micros * RATE), bytes_accessed=1024, transcendentals=0),
        name=name,
    )(idx, *ins, *after)


def sds(shape, dtype):
    return jax.ShapeDtypeStruct(shape, dtype)


def near(shape, dtype):
    return pltpu.VMEM(shape, dtype)


def far(shape, dtype):
    return pltpu.HBM(shape, dtype)


def dot(x, y):
    return jnp.dot(x, y, preferred_element_type=F32)


def dot_nt(x, y):
    return lax.dot_general(x, y, (((1,), (1,)), ((), ())), preferred_element_type=F32)


def dot_tn(x, y):
    return lax.dot_general(x, y, (((0,), (0,)), ((), ())), preferred_element_type=F32)


def rowsum(x):
    return jnp.sum(x, -1, keepdims=True)


def normalize(x):
    n = x.shape[-1]
    off = x - rowsum(x) / n
    r = lax.rsqrt(rowsum(off * off) / n + EPS)
    return off * r, r


def gelu_parts(u):
    t = jnp.tanh(GELU_A * (u + GELU_B * (u * u * u)))
    return 0.5 * u * (1.0 + t), t


def unpack_rows(side, wide):
    groups = wide // side.shape[1]
    rows = side.shape[0] // groups
    return jnp.concatenate([side[i * rows : (i + 1) * rows] for i in range(groups)], axis=1)


def pack_rows(block, groups):
    n = block.shape[1] // groups
    return jnp.concatenate([block[:, i * n : (i + 1) * n] for i in range(groups)], axis=0)


def project_kernel(idx, a_ref, an_ref, *refs):
    pieces = refs[:WAYS]
    q_ref, k_ref, v_ref, wq_ref, wo_ref, scr = refs[WAYS:]
    rows = wq_ref.shape[0] // WAYS
    orows = scr.shape[0] // WAYS
    hw = q_ref.shape[1]

    @pl.when(pl.program_id(0) == 0)
    def _():
        for k in range(WAYS):
            j = jnp.bitwise_xor(idx[0], k)
            wq_ref[pl.ds(pl.multiple_of(j * rows, rows), rows), :] = pieces[k][:, : 3 * hw]
            tail = pieces[k][:, 3 * hw :].astype(F32)
            scr[pl.ds(pl.multiple_of(j * orows, orows), orows), :] = unpack_rows(tail, wo_ref.shape[1])
        wo_ref[:hw, :] = scr[...].astype(BF)
        norm = jnp.concatenate([an_ref[0:1, :], an_ref[1:2, :]], axis=1)
        high = norm.astype(BF).astype(F32)
        row = jnp.concatenate([high, norm - high], axis=1)
        pad = wo_ref.shape[0] - hw
        at = lax.broadcasted_iota(jnp.int32, (pad, row.shape[1]), 0)
        wo_ref[hw:, :] = jnp.where(at == 0, row, 0.0).astype(BF)

    res = dot(a_ref[...], wq_ref[...]).astype(BF)
    q_ref[...] = res[:, :hw] * BF(HD ** (-0.5))
    k_ref[...] = res[:, hw : 2 * hw]
    v_ref[...] = res[:, 2 * hw :]


def project(a, norm, pieces, hw, idx):
    rows, d = a.shape
    n = 3 * hw
    blk = lambda w: pl.BlockSpec((BLK, w), lambda s, i: (s, 0))
    return run(
        project_kernel,
        (rows // BLK,),
        [a, norm, *pieces],
        [blk(d), full(norm.shape)] + fulls(pieces),
        [far((rows, hw), BF)] * 3 + [far((d, n), BF), far((hw + 16, d), BF)],
        [blk(hw)] * 3 + [full((d, n)), full((hw + 16, d))],
        idx,
        "project",
        40,
        [pltpu.VMEM((hw, d), F32)],
    )


def attend_kernel(idx, start_ref, q_ref, k_ref, v_ref, o_ref, p_ref):
    h = pl.program_id(0)
    rows, hw = q_ref.shape
    lane = (lax.broadcasted_iota(jnp.int32, (1, hw), 1) // HD) == h
    for i in range(rows // BLK):
        lo, hi = i * BLK, (i + 1) * BLK
        qb = jnp.where(lane, q_ref[lo:hi, :], BF(0))
        s = dot_nt(qb, k_ref[:hi, :])
        kpos = lax.broadcasted_iota(jnp.int32, (BLK, hi), 1)
        qpos = lo + lax.broadcasted_iota(jnp.int32, (BLK, hi), 0)
        s = jnp.where((kpos >= start_ref[lo:hi, :]) & (kpos <= qpos), s, -1e30)
        p = jnp.exp(s - jnp.max(s, -1, keepdims=True))
        p = (p * (1.0 / rowsum(p))).astype(BF)
        p_ref[0, lo:hi, :hi] = p
        ob = dot(p, v_ref[:hi, :]).astype(BF)
        o_ref[lo:hi, :] = jnp.where(lane, ob, o_ref[lo:hi, :])


def attend(start, q, k, v, idx, after=()):
    rows, hw = q.shape
    heads = hw // HD
    return run(
        attend_kernel,
        (heads,),
        [start, q, k, v],
        fulls([start, q, k, v]),
        [far((rows, hw), BF), far((heads, rows, rows), BF)],
        [full((rows, hw)), pl.BlockSpec((1, rows, rows), lambda s, i: (s, 0, 0))],
        idx,
        "attend",
        10,
        after=after,
        hbm=(1, 2, 3),
    )


def wide_norm(o_refs):
    parts = [x[...].astype(F32) for x in o_refs]
    n = sum(x.shape[-1] for x in parts)
    mean = sum(rowsum(x) for x in parts) / n
    parts = [x - mean for x in parts]
    r = lax.rsqrt(sum(rowsum(x * x) for x in parts) / n + EPS)
    return [x * r for x in parts], r


def unpack_norm(w_ref):
    hw = w_ref.shape[0] - 16
    row = w_ref[hw:, :].astype(F32)[0:1, :]
    gain, bias, gain_low, bias_low = (row[:, i * hw : (i + 1) * hw] for i in range(4))
    return gain + gain_low, bias + bias_low


def outproj_kernel(idx, on_ref, tok_ref, *refs):
    g = (len(refs) - 2) // 2
    o_refs, w_refs = refs[:g], refs[g : 2 * g]
    h_ref, c_ref = refs[2 * g :]
    hats, _ = wide_norm(o_refs)
    acc = tok_ref[...].astype(F32)
    for k in range(g):
        gain, bias = unpack_norm(w_refs[k])
        y = (hats[k] * gain + bias).astype(BF)
        acc = acc + dot(y, w_refs[k][: gain.shape[1], :])
    h_ref[...] = acc
    hat, _ = normalize(acc)
    c_ref[...] = (hat * on_ref[2:3, :] + on_ref[3:4, :]).astype(BF)


def outproj(on, tok, o, w, idx, after=()):
    rows, d = tok.shape
    hw = o[0].shape[1]
    blk = lambda n: pl.BlockSpec((BLK, n), lambda s, i: (s, 0))
    return run(
        outproj_kernel,
        (rows // BLK,),
        [on, tok, *o, *w],
        fulls([on]) + [blk(d)] + [blk(hw)] * len(o) + fulls(w),
        [far((rows, d), F32), near((rows, d), BF)],
        [blk(d), blk(d)],
        idx,
        "outproj",
        0,
        after=after,
        hbm=(1,),
    )


def ffn_up_kernel(idx, c_ref, e_ref, fn_ref, *refs):
    ups, downs = refs[:2], refs[2:4]
    u_ref, dw_ref, st_ref, wu_ref, wd_ref = refs[4:]
    rows = ups[0].shape[1]

    @pl.when(pl.program_id(0) == 0)
    def _():
        for i, k in enumerate(ORDER):
            for odd in range(2):
                j = jnp.bitwise_xor(idx[0], k + odd)
                at = pl.ds(pl.multiple_of(j * rows, rows), rows)
                wu_ref[at, :] = ups[odd][i]
                wd_ref[at, :] = downs[i // 2][i % 2 * 2 + odd]

    u = dot(c_ref[...], wu_ref[...])
    u_ref[...] = u
    z, _ = gelu_parts(u)
    mean = rowsum(z) / z.shape[-1]
    z = z - mean
    dw = dot_nt(e_ref[...], wd_ref[...])
    dw_ref[...] = dw
    eg = dw * fn_ref[0:1, :]
    stats = [mean, rowsum(z * z), rowsum(eg), rowsum(eg * z)]
    place = lax.broadcasted_iota(jnp.int32, (BLK, 128), 1)
    tile = jnp.zeros((BLK, 128), F32)
    for i, x in enumerate(stats):
        tile = jnp.where(place == i, x, tile)
    st_ref[...] = tile.T[:8, :]


def ffn_up(c, e, fn, pieces, idx):
    rows, d = c.shape
    fl = fn.shape[1]
    rblk = lambda n: pl.BlockSpec((BLK, n), lambda s, i: (s, 0))
    return run(
        ffn_up_kernel,
        (rows // BLK,),
        [c, e, fn, *pieces],
        [rblk(d), rblk(d), full(fn.shape)] + fulls(pieces),
        [near((rows, fl), F32), near((rows, fl), F32), sds((8, rows), F32), near((d, fl), BF), far((fl, d), BF)],
        [rblk(fl), rblk(fl), pl.BlockSpec((8, BLK), lambda s, i: (0, s)), full((d, fl)), full((fl, d))],
        idx,
        "ffn_up",
        7.5,
        hbm=(1,),
    )


def rel_of(s):
    return jnp.where(s < 2, 2 * s + 1, 2 * s - 4)


def rel_block(s, i):
    return jnp.bitwise_xor(rel_of(s), i[1])


def rel_spec(n):
    return pl.BlockSpec((BLK, n), lambda s, i: (rel_block(s, i), 0))


SEND_SPEC = lambda n: pl.BlockSpec((1, BLK, n), lambda s, i: (jnp.minimum(s, 1), 0, 0))
KEEP_SPEC = lambda n: full((BLK, n))


def put_rel(send_ref, keep_ref, last_ref, value):
    @pl.when(pl.program_id(0) < 2)
    def _():
        send_ref[0] = value.astype(BF)

    @pl.when(pl.program_id(0) == 2)
    def _():
        keep_ref[...] = value

    @pl.when(pl.program_id(0) == 3)
    def _():
        last_ref[...] = value


def ffn_mid_kernel(idx, u_ref, dw_ref, st_ref, fn_ref, wu_ref, w_ref, du_ref, send_ref, keep_ref, last_ref, fg_ref):
    g = st_ref.shape[0]
    fl = u_ref.shape[1]
    n = g * fl
    st = [st_ref[k] for k in range(g)]
    mean = sum(x[0:1] for x in st) / g
    gap = [x[0:1] - mean for x in st]
    spread = sum(x[1:2] + fl * (gp * gp) for x, gp in zip(st, gap)) / n
    r = lax.rsqrt(spread + EPS)
    s_plain = sum(x[2:3] for x in st) / n
    s_norm = r * (sum(x[3:4] + gp * x[2:3] for x, gp in zip(st, gap)) / n)
    cols = jnp.concatenate([mean, r, s_plain, s_norm, jnp.zeros((124, BLK), F32)], axis=0).T
    mean, r, s_plain, s_norm = (cols[:, i : i + 1] for i in range(4))
    u = u_ref[...]
    z, t = gelu_parts(u)
    hat = (z - mean) * r
    w_ref[...] = (hat * fn_ref[0:1, :] + fn_ref[1:2, :]).astype(BF)
    dw = dw_ref[...]
    dz = r * (dw * fn_ref[0:1, :] - s_plain - hat * s_norm)
    slope = 0.5 * (1.0 + t) + 0.5 * u * (1.0 - t * t) * (GELU_A * (1.0 + (3.0 * GELU_B) * (u * u)))
    du = (dz * slope).astype(BF)
    du_ref[...] = du
    put_rel(send_ref, keep_ref, last_ref, dot_nt(du, wu_ref[...]))
    grads = jnp.concatenate([jnp.sum(dw * hat, 0, keepdims=True), jnp.sum(dw, 0, keepdims=True)], axis=0)

    @pl.when(pl.program_id(0) == 0)
    def _():
        fg_ref[...] = grads

    @pl.when(pl.program_id(0) > 0)
    def _():
        fg_ref[...] += grads


def ffn_mid(u, dw, st, fn, wu, idx):
    rows, fl = u.shape
    d = wu.shape[0]
    return run(
        ffn_mid_kernel,
        (rows // BLK,),
        [u, dw, st, fn, wu],
        [rel_spec(fl), rel_spec(fl), pl.BlockSpec((st.shape[0], 8, BLK), lambda s, i: (0, 0, rel_block(s, i)))]
        + fulls([fn, wu]),
        [far((rows, fl), BF), far((rows, fl), BF), sds((2, BLK, d), BF), far((BLK, d), F32), sds((BLK, d), F32), sds((2, fl), F32)],
        [rel_spec(fl), rel_spec(fl), SEND_SPEC(d), KEEP_SPEC(d), KEEP_SPEC(d), full((2, fl))],
        idx,
        "ffn_mid",
        6.5,
    )


def ffn_out(x, w, idx, after):
    rows, depth = x.shape
    d = w.shape[1]

    def kernel(idx, x_ref, w_ref, send_ref, keep_ref, last_ref):
        put_rel(send_ref, keep_ref, last_ref, dot(x_ref[...], w_ref[...]))

    return run(
        kernel,
        (rows // BLK,),
        [x, w],
        [rel_spec(depth), full(w.shape)],
        [sds((2, BLK, d), BF), far((BLK, d), F32), sds((BLK, d), F32)],
        [SEND_SPEC(d), KEEP_SPEC(d), KEEP_SPEC(d)],
        idx,
        "ffn_out",
        0,
        (),
        after,
        (0, 1),
    )


def put_blocks(scr, send_ref, keep_ref, first, step):
    for i, k in enumerate(ORDER):
        for odd, dest in enumerate((keep_ref, send_ref)):
            j = jnp.bitwise_xor(first, k + odd)
            value = scr[pl.ds(pl.multiple_of(j * step, step), step), :]
            dest[i, :, : value.shape[1]] = value.astype(dest.dtype)


def weight_grad(x, y, idx, name, after=()):
    rows, d = x.shape
    n = y.shape[1]
    step = d // WAYS
    steps = d // BLK

    def kernel(idx, x_ref, y_ref, send_ref, keep_ref, scr):
        s = pl.program_id(0)
        scr[pl.ds(pl.multiple_of(s * BLK, BLK), BLK), :] = dot_tn(x_ref[...], y_ref[...])

        @pl.when(s == steps - 1)
        def _():
            put_blocks(scr, send_ref, keep_ref, idx[0], step)

    return run(
        kernel,
        (steps,),
        [x, y],
        [pl.BlockSpec((rows, BLK), lambda s, i: (0, s)), full(y.shape)],
        [sds((WAYS // 2, step, n), BF), far((WAYS // 2, step, n), F32)],
        [full((WAYS // 2, step, n))] * 2,
        idx,
        name,
        3.5,
        [pltpu.VMEM((d, n), F32)],
        after,
    )


def qkv_back(a, dqkv, wq, go, idx, after=()):
    rows, d = a.shape
    n = dqkv.shape[1]
    step = d // WAYS
    hw = go[2].shape[0]
    groups = d // hw
    orows = hw // WAYS

    def kernel(idx, a_ref, d_ref, w_ref, go0_ref, go1_ref, go2_ref, gs_ref, gk_ref, send_ref, keep_ref, last_ref, scr, go_ref):
        go_ref[...] = go0_ref[...] + go1_ref[0].astype(F32) + go2_ref[...].astype(F32)
        for s in range(d // BLK):
            scr[s * BLK : (s + 1) * BLK, :] = dot_tn(a_ref[:, s * BLK : (s + 1) * BLK], d_ref[...])
        put_blocks(scr, gs_ref, gk_ref, idx[0], step)
        for i, k in enumerate(ORDER):
            for odd, dest in enumerate((gk_ref, gs_ref)):
                j = jnp.bitwise_xor(idx[0], k + odd)
                tail = pack_rows(go_ref[pl.ds(pl.multiple_of(j * orows, orows), orows), :], groups)
                dest[i, :, n:] = tail.astype(dest.dtype)
        for k in range(4):
            j = jnp.bitwise_xor(idx[1], k)
            value = dot_nt(d_ref[pl.ds(pl.multiple_of(j * BLK, BLK), BLK), :], w_ref[...])
            if k % 2:
                send_ref[k // 2] = value.astype(BF)
            else:
                (last_ref if k else keep_ref)[...] = value

    ins = [a, dqkv, wq, *go]
    lead = pl.BlockSpec((1, hw, d), lambda s, i: (0, 0, 0))
    half = (WAYS // 2, step, d)
    part = (2, BLK, d)
    outs = [sds(half, BF), far(half, F32), sds(part, BF), far(part[1:], F32), sds(part[1:], F32)]
    return run(
        kernel, (1,), ins, fulls(ins[:4]) + [lead, full(go[2].shape)], outs, fulls(outs), idx, "qkv_back", 5.5,
        [pltpu.VMEM((d, n), F32), pltpu.VMEM((hw, d), F32)],
        after=after,
        hbm=(0, 2, 3),
    )


def shard_back_kernel(idx, dc0_ref, dc1_ref, dc2_ref, h_ref, e_ref, on_ref, *refs):
    g = 4
    o_refs, w_refs = refs[:g], refs[g : 2 * g]
    dh_ref, ol_ref, ag_ref, *do_refs = refs[2 * g :]
    do_refs, (gs_ref, gk_ref, gl_ref) = do_refs[:g], do_refs[g:]
    dc = dc0_ref[...] + dc1_ref[0].astype(F32) + dc2_ref[...].astype(F32)
    hat, r = normalize(h_ref[...])
    wgt = dc * on_ref[2:3, :]
    n = dc.shape[-1]
    dh = e_ref[...].astype(F32) + r * (wgt - rowsum(wgt) / n - hat * (rowsum(wgt * hat) / n))
    dh_ref[...] = dh
    ol_ref[...] = jnp.concatenate([jnp.sum(dc * hat, 0, keepdims=True), jnp.sum(dc, 0, keepdims=True)], axis=0)
    dhb = dh.astype(BF)
    hats, r = wide_norm(o_refs)
    norms = [unpack_norm(w_refs[k]) for k in range(g)]
    dys = [dot_nt(dhb, w_refs[k][: norms[k][0].shape[1], :]) for k in range(g)]
    wgts = [dys[k] * norms[k][0] for k in range(g)]
    s_plain = sum(rowsum(x) for x in wgts) / n
    s_norm = sum(rowsum(x * y) for x, y in zip(wgts, hats)) / n
    for k in range(g):
        do_refs[k][...] = (r * (wgts[k] - s_plain - hats[k] * s_norm)).astype(BF)
        ag_ref[jnp.bitwise_xor(idx[1], k)] = jnp.concatenate(
            [jnp.sum(dys[k] * hats[k], 0, keepdims=True), jnp.sum(dys[k], 0, keepdims=True)], axis=0
        )
    for k in range(g):
        y = (hats[k] * norms[k][0] + norms[k][1]).astype(BF)
        value = dot_tn(y, dhb)
        if k % 2:
            gs_ref[k // 2] = value.astype(BF)
        else:
            (gl_ref if k else gk_ref)[...] = value


def shard_back(dc_keep, dc_one, dc_two, h, e, on, o, w, idx, after):
    rows, d = h.shape
    g = len(o)
    hw = o[0].shape[1]
    mine = lambda n: pl.BlockSpec((BLK, n), lambda s, i: (i[1], 0))
    lead = pl.BlockSpec((1, BLK, d), lambda s, i: (0, 0, 0))
    ins = [dc_keep, dc_one, dc_two, h, e, on, *o, *w]
    return run(
        shard_back_kernel,
        (1,),
        ins,
        [full((BLK, d)), lead, full((BLK, d)), mine(d), mine(d)] + fulls([on]) + [mine(hw)] * g + fulls(w),
        [far((BLK, d), F32), sds((2, d), F32), sds((g, 2, hw), F32)]
        + [sds((BLK, hw), BF)] * g
        + [sds((2, hw, d), BF), far((hw, d), F32), sds((hw, d), F32)],
        [full((BLK, d)), full((2, d)), full((g, 2, hw))]
        + [full((BLK, hw))] * g
        + [full((2, hw, d)), full((hw, d)), full((hw, d))],
        idx,
        "shard_back",
        0,
        after=after,
        hbm=(0, 3, 4) + tuple(range(6, 6 + 2 * g)),
    )


def attend_back_kernel(idx, q_ref, k_ref, v_ref, p_ref, *refs):
    d_refs = refs[:4]
    out_ref, do_scr, dq_scr, dk_scr, dv_scr = refs[4:]
    h = pl.program_id(0)
    rows, hw = q_ref.shape

    @pl.when(h == 0)
    def _():
        for k in range(4):
            j = jnp.bitwise_xor(idx[1], k)
            do_scr[pl.ds(pl.multiple_of(j * BLK, BLK), BLK), :] = d_refs[k][...]
        dk_scr[...] = jnp.zeros_like(dk_scr)
        dv_scr[...] = jnp.zeros_like(dv_scr)
        dq_scr[...] = jnp.zeros_like(dq_scr)

    lane = (lax.broadcasted_iota(jnp.int32, (1, hw), 1) // HD) == h
    for i in range(rows // BLK):
        lo, hi = i * BLK, (i + 1) * BLK
        dob = jnp.where(lane, do_scr[lo:hi, :], BF(0))
        qb = jnp.where(lane, q_ref[lo:hi, :], BF(0))
        pb = p_ref[0, lo:hi, :hi]
        p = pb.astype(F32)
        dp = dot_nt(dob, v_ref[:hi, :])
        ds = (p * (dp - rowsum(p * dp))).astype(BF)
        dq_scr[lo:hi, :] = jnp.where(lane, dot(ds, k_ref[:hi, :]), dq_scr[lo:hi, :])
        dk_scr[:hi, :] += dot_tn(ds, qb)
        dv_scr[:hi, :] += dot_tn(pb, dob)

    @pl.when(h == pl.num_programs(0) - 1)
    def _():
        out_ref[...] = jnp.concatenate([dq_scr[...] * HD ** (-0.5), dk_scr[...], dv_scr[...]], axis=1).astype(BF)


def attend_back(q, k, v, p, do, idx, after):
    rows, hw = q.shape
    heads = hw // HD
    return run(
        attend_back_kernel,
        (heads,),
        [q, k, v, p, *do],
        fulls([q, k, v]) + [pl.BlockSpec((1, rows, rows), lambda s, i: (s, 0, 0))] + fulls(do),
        [sds((rows, 3 * hw), BF)],
        [full((rows, 3 * hw))],
        idx,
        "attend_back",
        11,
        [pltpu.VMEM((rows, hw), BF)] + [pltpu.VMEM((rows, hw), F32)] * 3,
        after=after,
        hbm=range(4),
    )[0]


def shard_end_kernel(idx, da0_ref, da1_ref, da2_ref, tok_ref, on_ref, dh_ref, gt_ref, oe_ref):
    da = da0_ref[...] + da1_ref[0].astype(F32) + da2_ref[...].astype(F32)
    hat, r = normalize(tok_ref[...].astype(F32))
    wgt = da * on_ref[0:1, :]
    n = da.shape[-1]
    grad = r * (wgt - rowsum(wgt) / n - hat * (rowsum(wgt * hat) / n))
    gt_ref[...] = (dh_ref[...] + grad).astype(BF)
    oe_ref[...] = jnp.concatenate([jnp.sum(da * hat, 0, keepdims=True), jnp.sum(da, 0, keepdims=True)], axis=0)


def shard_end(da_keep, da_one, da_two, tok, on, dh, idx, after=()):
    d = tok.shape[1]
    lead = pl.BlockSpec((1, BLK, d), lambda s, i: (0, 0, 0))
    return run(
        shard_end_kernel,
        (1,),
        [da_keep, da_one, da_two, tok, on, dh],
        [full((BLK, d)), lead, full((BLK, d)), pl.BlockSpec((BLK, d), lambda s, i: (i[1], 0)), full(on.shape), full((BLK, d))],
        [sds((BLK, d), BF), sds((2, d), F32)],
        [full((BLK, d)), full((2, d))],
        idx,
        "shard_end",
        0,
        after=after,
    )


def spread_rows(parts, idx, name, after=()):
    rows, d = parts[0].shape

    def kernel(idx, *refs):
        for k, part in enumerate(refs[:-2]):
            at = pl.ds(pl.multiple_of(jnp.bitwise_xor(idx[1], k) * rows, rows), rows)
            refs[-2][at, :] = part[...]
        refs[-1][...] = jnp.zeros(refs[-1].shape, F32)

    outs = [sds((rows * len(parts), d), BF), sds((8, 128), F32)]
    return run(kernel, (1,), parts, fulls(parts), outs, fulls(outs), idx, name, 2, (), after)


def far_sum(last, got, idx, after=(), tick=TICK):
    rows, d = last.shape

    def kernel(idx, last_ref, got_ref, out_ref):
        out_ref[...] = (last_ref[...] + got_ref[0].astype(F32)).astype(BF)

    second = pl.BlockSpec((1, rows, d), lambda s, i: (1, 0, 0))
    out = [sds((rows, d), BF)]
    return run(kernel, (1,), [last, got], [full((rows, d)), second], out, fulls(out), idx, "far_sum", tick, (), after)[0]


def fold(keep, got, idx, after=(), tick=TICK):
    count, rows, d = keep.shape
    half = count // 2

    def kernel(idx, keep_ref, got_ref, stay_ref, send_ref):
        stay_ref[...] = keep_ref[:half] + got_ref[:half].astype(F32)
        send = (keep_ref[half:] + got_ref[half:].astype(F32)).astype(BF)
        send_ref[...] = send if half > 1 else send[0]

    outs = [sds((half, rows, d), F32), sds((half, rows, d) if half > 1 else (rows, d), BF)]
    return run(kernel, (1,), [keep, got], fulls([keep, got]), outs, fulls(outs), idx, "fold", tick, (), after, (0,) if half > 1 else ())


def close(own, got, idx, after=(), vec=None):
    rows, d = got[0].shape

    def kernel(idx, own_ref, *refs):
        out_ref = refs[-1]
        total = own_ref[...].reshape(rows, d)
        for ref in refs[: len(got)]:
            total = total + ref[...].astype(F32)
        out_ref[:rows, :] = total.astype(BF)
        if vec is not None:
            x = refs[len(got)][...]
            high = x.astype(BF).astype(F32)
            out_ref[rows:, :] = jnp.concatenate([high, x - high], axis=0).astype(BF)

    ins = [own, *got] + ([] if vec is None else [vec])
    out = [sds((rows if vec is None else rows + 2 * vec.shape[0], d), BF)]
    return run(kernel, (1,), ins, fulls(ins), out, fulls(out), idx, "close", TICK, (), after)[0]


def join(parts, idx, after=()):
    shapes = [x.shape if len(x.shape) == 3 else (1, *x.shape) for x in parts]

    def kernel(idx, *refs):
        at = 0
        for ref, shape in zip(refs, shapes):
            refs[-1][at : at + shape[0]] = ref[...].reshape(shape)
            at += shape[0]

    out = [sds((sum(x[0] for x in shapes), *shapes[0][1:]), BF)]
    return run(kernel, (1,), parts, fulls(parts), out, fulls(out), idx, "join", 2 * TICK, (), after)[0]


def block_end(h, keep, got, last, idx, after=()):
    rows, d = last.shape

    def kernel(idx, h_ref, keep_ref, got_ref, last_ref, out_ref):
        total = h_ref[...] + keep_ref[...] + got_ref[0].astype(F32) + last_ref[...].astype(F32)
        out_ref[...] = total.astype(BF)

    lead = pl.BlockSpec((1, rows, d), lambda s, i: (0, 0, 0))
    mine = pl.BlockSpec((rows, d), lambda s, i: (i[1], 0))
    own = full((rows, d))
    ins = [h, keep, got, last]
    out = [sds((rows, d), BF)]
    return run(
        kernel, (1,), ins, [mine, own, lead, own], out, fulls(out), idx, "block_end", TICK, (), after, (0,)
    )[0]


def vec_add(x, y, idx, after=()):
    def kernel(idx, x_ref, y_ref, out_ref):
        out_ref[...] = x_ref[...] + y_ref[...]

    out = [sds(x.shape, F32)]
    return run(kernel, (1,), [x, y], fulls([x, y]), out, fulls(out), idx, "vec_add", TICK, (), after)[0]


def one_hot(place, count, width):
    at = lax.broadcasted_iota(jnp.int32, (count, width), 1)
    want = place * count + lax.broadcasted_iota(jnp.int32, (count, width), 0)
    return jnp.where(at == want, 1.0, 0.0).astype(BF)


def precondition(idx, ins, outs, scr, total, flip):
    w_ref, l_ref, r_ref, lr_ref, rr_ref = ins
    g_ref, nl_ref, nr_ref, nw_ref, copy_ref = outs
    d, n = scr.shape
    rows, side = w_ref.shape[0], r_ref.shape[0]
    whole = scr[...]
    g_ref[...] = whole.T if flip else whole
    grad = whole.astype(BF)
    scale = 1.0 / total
    own_cols = dot_nt(one_hot(idx[2], side, n), grad).astype(BF)
    own_rows = dot(one_hot(idx[2], rows, d), grad).astype(BF)
    nr_ref[...] = DECAY * r_ref[...] + ((1.0 - DECAY) * scale * scale) * dot(own_cols, grad)
    nl_ref[...] = DECAY * l_ref[...] + ((1.0 - DECAY) * scale * scale) * dot_nt(own_rows, grad)
    part = dot(lr_ref[...].astype(BF), grad).astype(BF)
    new = w_ref[...] - (MAT_RATE * scale) * dot(part, rr_ref[...].astype(BF))
    nw_ref[...] = new
    copy_ref[...] = new.astype(BF)


def update_outs(mats):
    w, left, right = mats[:3]
    (rows, n), d, side = w.shape, left.shape[1], right.shape[0]
    flip = n % 128 != 0
    outs = [sds((n, d) if flip else (d, n), F32), sds((rows, d), F32), sds((side, n), F32)]
    return outs + [sds((rows, n), F32), sds((rows, n), BF)], flip, pltpu.VMEM((d, n), F32)


def update_one(mats, near_blocks, far_blocks, total, idx, name, after=()):
    outs, flip, scr = update_outs(mats)
    step = mats[1].shape[1] // WAYS

    def kernel(idx, *refs):
        ins, (even, odd), rest = refs[:5], refs[5:7], refs[7:]
        for i, k in enumerate(ORDER):
            for far_one, blocks in enumerate((even, odd)):
                j = jnp.bitwise_xor(idx[0], k + far_one)
                rest[6][pl.ds(pl.multiple_of(j * step, step), step), :] = blocks[i].astype(F32)
        precondition(idx, ins, rest[:5], rest[6], total, flip)
        rest[5][...] = jnp.zeros(rest[5].shape, F32)

    ins = [*mats, near_blocks, far_blocks]
    outs = outs + [sds((8, 128), F32)]
    res = run(kernel, (1,), ins, fulls(ins), outs, fulls(outs), idx, name, 4, [scr], after, range(5))
    return [res[0].T if flip else res[0], *res[1:]]


def update_pair(mats, mats2, near_blocks, far_blocks, norms, rates, total, idx, name, after=()):
    outs, flip, scr = update_outs(mats)
    outs2, flip2, scr2 = update_outs(mats2)
    step, n = mats[1].shape[1] // WAYS, mats[0].shape[1]
    step2, n2 = mats2[1].shape[1] // WAYS, mats2[0].shape[1]
    half = (near_blocks.shape[1] - step) // 2
    wide = norms[1].shape[1]

    def kernel(idx, *refs):
        ins, ins2, (even, odd), norm_refs, rest = refs[:5], refs[5:10], refs[10:12], refs[12:15], refs[15:]
        sums = 0.0
        for i, k in enumerate(ORDER):
            for far_one, blocks in enumerate((even, odd)):
                j = jnp.bitwise_xor(idx[0], k + far_one)
                block = blocks[i].astype(F32)
                rest[-2][pl.ds(pl.multiple_of(j * step, step), step), :] = block[:step, :n]
                rest[-1][pl.ds(pl.multiple_of(j * step2, step2), step2), :] = unpack_rows(block[:step, n:], n2)
                sums = sums + (block[step : step + half] + block[step + half :])
        grads = [sums[:4], jnp.concatenate([sums[4:5, :wide], sums[4:5, wide : 2 * wide]], axis=0), sums[5:7]]
        for i, (grad, rate) in enumerate(zip(grads, (rates[0], rates[0], rates[1]))):
            rest[10 + i][...] = grad
            rest[13 + i][...] = norm_refs[i][...] - rate * grad
        precondition(idx, ins2, rest[5:10], rest[-1], total, flip2)
        precondition(idx, ins, rest[:5], rest[-2], total, flip)

    all_outs = outs + outs2 + [sds(x.shape, F32) for x in [*norms, *norms]]
    ins = [*mats, *mats2, near_blocks, far_blocks, *norms]
    res = run(kernel, (1,), ins, fulls(ins), all_outs, fulls(all_outs), idx, name, 6, [scr, scr2], after, range(10))
    res = list(res)
    res[0] = res[0].T if flip else res[0]
    res[5] = res[5].T if flip2 else res[5]
    return res[:5], res[5:10], res[10:]


def body(
    tokens,
    cotangent,
    doc_lengths,
    outer_norms,
    attn_norm,
    ffn_norm,
    w_qkv,
    left_qkv,
    right_qkv,
    left_root_qkv,
    right_root_qkv,
    w_out,
    left_out,
    right_out,
    left_root_out,
    right_root_out,
    w_up,
    left_up,
    right_up,
    left_root_up,
    right_root_up,
    w_down,
    left_down,
    right_down,
    left_root_down,
    right_root_down,
):
    row_count = tokens.shape[0]
    n_dp, n_mp = lax.axis_size("dp"), lax.axis_size("mp")
    fine = n_dp // WAYS
    total = row_count * n_dp
    dp_at, mp_at = lax.axis_index("dp"), lax.axis_index("mp")
    idx = jnp.stack([dp_at // fine, mp_at, dp_at]).astype(jnp.int32)
    hw = w_qkv.shape[2] // 3

    def swap(x, axis, size, k):
        return lax.ppermute(x, axis, [(i, i ^ k) for i in range(size)])

    def dp(x, k):
        return swap(x, "dp", n_dp, k * fine)

    def mp(x, k):
        return swap(x, "mp", n_mp, k)

    def fine_rows(x):
        k = 1
        while k < fine:
            got = swap(x, "dp", n_dp, k)
            x = jnp.where((dp_at & k) == 0, jnp.concatenate([x, got], 0), jnp.concatenate([got, x], 0))
            k *= 2
        return x

    def fine_sum(x):
        k = 1
        while k < fine:
            x = x + swap(x, "dp", n_dp, k)
            k *= 2
        return x

    def gather8(own, *early):
        parts = {0: own}
        for k in (2, 4, 6):
            parts[k] = dp(own, k)
        parts[1] = dp(own, 1)
        for k in (2, 4, 6):
            parts[k ^ 1] = dp(after(parts[k], *early) if early else parts[k], 1)
        return [parts[k] for k in range(WAYS)]

    def gather4(own):
        far = mp(own, 2)
        return [own, mp(own, 1), far, mp(far, 1)]

    def scatter4(send, keep):
        got = mp(send, 1)
        return keep, got, mp((keep[1] + got[1].astype(F32)).astype(BF), 2)

    def gather8_halves(own):
        two = jnp.stack([own, dp(own, 4)])
        four = jnp.concatenate([two, dp(two, 2)])
        return four, dp(four, 1)

    def after(x, *deps):
        return lax.optimization_barrier((x, *deps))[0]

    out_rows = fine_rows(w_out[0].astype(BF))
    groups = tokens.shape[1] // hw
    first = jnp.concatenate([fine_rows(w_qkv[0].astype(BF)), pack_rows(out_rows, groups)], axis=1)
    up_own = fine_rows(w_up[0].astype(BF))
    down_own = fine_rows(w_down[0].astype(BF))
    down_two = jnp.stack([down_own, dp(down_own, 1)])
    first = gather8(first, down_two)

    ends = jnp.cumsum(doc_lengths[0])
    places = jnp.arange(row_count, dtype=jnp.int32)
    start = jnp.max(jnp.where(ends[None, :] <= places[:, None], ends[None, :], 0), axis=1, keepdims=True)
    start = start.astype(jnp.int32)
    hat, _ = normalize(tokens.astype(F32))
    a_low = (hat * outer_norms[0] + outer_norms[1]).astype(BF)

    up_go = after(up_own, first[2], first[4], first[6], down_two)
    up_z = [dp(up_go, k) for k in ORDER[1:]]
    down_z2 = dp(after(down_two, up_go), 4)
    q, k, v, wq, wo = project(a_low, attn_norm, first, hw, idx)
    wo_far = mp(wo, 2)
    o, probs = attend(start, q, k, v, idx)
    o, *up_z = lax.optimization_barrier((o, *up_z))
    up_four = jnp.stack([up_own, *up_z])
    o, wo, wo_far, up_four = lax.optimization_barrier((o, wo, wo_far, up_four))
    o_far = mp(o, 2)
    up_x = dp(up_four, 1)
    wo_near, wo_last = mp(after(wo, up_four), 1), mp(wo_far, 1)
    down_four = join([down_two, down_z2], idx, [up_four, wo_near, wo_last])
    down_z1 = dp(down_four, 2)
    o_near = mp(after(o, o_far), 1)
    o_all = [o, o_near, o_far, mp(o_far, 1)]
    wo_all = [wo, wo_near, wo_far, wo_last]
    hidden, c_low = outproj(outer_norms, tokens, o_all, wo_all, idx, [up_x])
    u, dw, stats, wu, wd = ffn_up(c_low, cotangent, ffn_norm, [up_four, up_x, down_four, down_z1], idx)
    stats = lax.all_gather(stats, "mp")
    w_low, du, dc_send, dc_keep, dc_last, ffn_grads = ffn_mid(u, dw, stats, ffn_norm, wu, idx)
    dc_got = mp(dc_send, 1)
    dc_sum = far_sum(dc_last, dc_got, idx)
    down_send, down_keep = weight_grad(w_low, cotangent, idx, "grad_down", [dc_sum])
    down_x = dp(down_send, 1)
    up_send, up_keep = weight_grad(c_low, du, idx, "grad_up", [down_send])
    up_x2 = dp(after(up_send, down_send), 1)
    dh, outer_late, attn_grads, *rest = shard_back(
        dc_keep, dc_got, mp(dc_sum, 2), hidden, cotangent, outer_norms, o_all, wo_all, idx, [up_send]
    )
    do, (go_send, go_keep, go_last) = rest[:n_mp], rest[n_mp:]
    do = [do[0]] + [mp(do[k], k) for k in range(1, n_mp)]
    go_got = mp(go_send, 1)
    bo_send, bo_keep, bo_last = ffn_out(w_low, wd, idx, [do[1]])
    bo_got = mp(bo_send, 1)
    down_t, down_low = fold(down_keep, down_x, idx, [bo_send], 0)
    go_sum = far_sum(go_last, go_got, idx, [down_low], 0)
    dqkv = attend_back(q, k, v, probs, do, idx, [go_sum])
    down_z1 = dp(down_low, 2)
    go_far = mp(go_sum, 2)
    down_t, down_low = fold(down_t, down_z1, idx, [dqkv])
    up_t, up_low = fold(up_keep, up_x2, idx, [down_low])
    bo_sum = far_sum(bo_last, bo_got, idx, [up_low])
    bo_far = mp(bo_sum, 2)
    qkv_send, qkv_keep, da_send, da_keep, da_last = qkv_back(a_low, dqkv, wq, [go_keep, go_got, go_far], idx, [bo_sum])

    down_z2, up_z1 = dp(down_low, 4), dp(up_low, 2)
    qkv_x = dp(qkv_send, 1)
    da_got = mp(da_send, 1)
    da_sum = far_sum(da_last, da_got, idx)
    da_far = mp(da_sum, 2)
    down_done = fine_sum(close(down_t, [down_z2], idx, [da_sum]))
    down_r4 = dp(down_done, 4)
    up_t, up_low = fold(up_t, up_z1, idx, [down_done])
    up_z2 = dp(up_low, 4)
    qkv_t, qkv_low = fold(qkv_keep, qkv_x, idx, [up_low], 0)
    qkv_z1 = dp(qkv_low, 2)
    out_own = block_end(hidden, bo_keep, bo_got, bo_far, idx, [qkv_low])
    out_far = mp(out_own, 2)
    gt, outer_early = shard_end(da_keep, da_got, da_far, tokens, outer_norms, dh, idx, [out_own])
    gt_far = mp(gt, 2)
    lanes = outer_late.shape[1]
    vec = jnp.concatenate([outer_early, outer_late, attn_grads.reshape(-1, lanes)])
    vec_got = mp(vec, 1)
    down_two = join([down_done, down_r4], idx, [gt])
    down_r2 = dp(down_two, 2)
    up_done = fine_sum(close(up_t, [up_z2], idx, [down_two]))
    up_r4 = dp(up_done, 4)
    qkv_t, qkv_low = fold(qkv_t, qkv_z1, idx, [up_done])
    qkv_z2 = dp(qkv_low, 4)
    gt_far = after(gt_far, qkv_low)
    gt_all = [gt, mp(after(gt, gt_far), 1), gt_far, mp(gt_far, 1)]
    down_four = join([down_two, down_r2], idx, [qkv_low])
    down_other = dp(down_four, 1)
    vec = vec_add(vec, vec_got, idx, [down_four])
    vec_got = mp(vec, 2)
    up_two = join([up_done, up_r4], idx, [vec])
    vec = vec_add(vec, vec_got, idx, [up_two])
    up_r2 = dp(up_two, 2)
    grad_tokens, token = spread_rows(gt_all, idx, "spread_tokens", [vec])
    out_far = after(out_far, vec)
    out_all = [out_own, mp(after(out_own, out_far), 1), out_far, mp(out_far, 1)]
    block_out, token = spread_rows(out_all, idx, "spread_out", [token])
    attn_own = lax.dynamic_slice_in_dim(vec[4:].reshape(n_mp, -1), mp_at, 1, 0)
    attn_own = jnp.pad(attn_own, ((0, 0), (0, lanes - attn_own.shape[1])))
    vec = jnp.concatenate([vec[:4], attn_own, ffn_grads, jnp.zeros((1, lanes), F32)])
    vec = fine_sum(vec)
    qkv_own = close(qkv_t, [qkv_z2], idx, [token], None if fine > 1 else vec)
    if fine > 1:
        high = vec.astype(BF)
        qkv_own = jnp.concatenate([fine_sum(qkv_own), high, (vec - high.astype(F32)).astype(BF)])
    qkv_z = [dp(qkv_own, k) for k in ORDER[1:]]
    up_four = join([up_two, up_r2], idx, [qkv_own])
    up_other = dp(up_four, 1)
    down_mats = [x[0] for x in (w_down, left_down, right_down, left_root_down, right_root_down)]
    *down_res, token = update_one(down_mats, down_four, down_other, total, idx, "update_down", [up_four])
    qkv_four = join([qkv_own, *qkv_z], idx, [token])
    qkv_other = dp(qkv_four, 1)
    def mats(*arrays):
        return [x[0] for x in arrays]

    up_mats = mats(w_up, left_up, right_up, left_root_up, right_root_up)
    *up_res, token = update_one(up_mats, up_four, up_other, total, idx, "update_up", [qkv_four])
    qkv_res, out_res, vecs = update_pair(
        mats(w_qkv, left_qkv, right_qkv, left_root_qkv, right_root_qkv),
        mats(w_out, left_out, right_out, left_root_out, right_root_out),
        qkv_four,
        qkv_other,
        [outer_norms, attn_norm, ffn_norm],
        (VEC_RATE / math.sqrt(total), UNIT_RATE / math.sqrt(total)),
        total,
        idx,
        "update_qkv",
        [token],
    )

    return (
        block_out,
        grad_tokens,
        *vecs,
        *(x[None] for x in qkv_res),
        *(x[None] for x in out_res),
        *(x[None] for x in up_res),
        *(x[None] for x in down_res),
    )


def solution(mesh):
    rows = P("dp", None)
    mats = (P("mp", "dp", None),) * 4 + (P("mp", None, None),)
    res = (P("mp", None, None),) + (P("mp", "dp", None),) * 4
    cols = P(None, "mp")
    return jax.shard_map(
        body,
        mesh=mesh,
        in_specs=(rows, rows, rows, P(), cols, cols) + mats * 4,
        out_specs=(rows, rows, P(), cols, cols, P(), cols, cols) + res * 4,
        check_vma=False,
    )
```

```python
import math

import jax
import jax.numpy as jnp
from jax import lax
from jax.experimental import pallas as pl
from jax.experimental.pallas import tpu as pltpu
from jax.sharding import PartitionSpec as P

HD = 64
EPS = 1e-05
DECAY = 0.5
MAT_RATE = 0.5
VEC_RATE = 0.05
UNIT_RATE = 0.3
GELU_A = math.sqrt(2.0 / math.pi)
GELU_B = 0.044715
BF = jnp.bfloat16
F32 = jnp.float32
VMEM = 22 * 1024 * 1024
WAYS = 8
RATE = 4e8
TICK = 5
BLK = 256
ORDER = (0, 4, 2, 6)


def full(shape):
    return pl.BlockSpec(shape, lambda *args: (0,) * len(shape))


def fulls(arrays):
    return [full(x.shape) for x in arrays]


def run(kernel, grid, ins, in_specs, outs, out_specs, idx, name, micros, scratch=(), after=(), hbm=()):
    count, kernel_in = len(ins), kernel
    ins = [pltpu.with_memory_space_constraint(x, pltpu.HBM) if i in hbm else x for i, x in enumerate(ins)]

    def kernel(idx, *refs):
        kernel_in(idx, *refs[:count], *refs[count + len(after) :])

    return pl.pallas_call(
        kernel,
        grid_spec=pltpu.PrefetchScalarGridSpec(
            num_scalar_prefetch=1,
            grid=grid,
            in_specs=list(in_specs) + [pl.BlockSpec(memory_space=pl.ANY)] * len(after),
            out_specs=out_specs,
            scratch_shapes=list(scratch),
        ),
        out_shape=outs,
        compiler_params=pltpu.CompilerParams(vmem_limit_bytes=VMEM),
        cost_estimate=pl.CostEstimate(flops=int(micros * RATE), bytes_accessed=1024, transcendentals=0),
        name=name,
    )(idx, *ins, *after)


def sds(shape, dtype):
    return jax.ShapeDtypeStruct(shape, dtype)


def near(shape, dtype):
    return pltpu.VMEM(shape, dtype)


def far(shape, dtype):
    return pltpu.HBM(shape, dtype)


def dot(x, y):
    return jnp.dot(x, y, preferred_element_type=F32)


def dot_nt(x, y):
    return lax.dot_general(x, y, (((1,), (1,)), ((), ())), preferred_element_type=F32)


def dot_tn(x, y):
    return lax.dot_general(x, y, (((0,), (0,)), ((), ())), preferred_element_type=F32)


def rowsum(x):
    return jnp.sum(x, -1, keepdims=True)


def normalize(x):
    n = x.shape[-1]
    off = x - rowsum(x) / n
    r = lax.rsqrt(rowsum(off * off) / n + EPS)
    return off * r, r


def gelu_parts(u):
    t = jnp.tanh(GELU_A * (u + GELU_B * (u * u * u)))
    return 0.5 * u * (1.0 + t), t


def unpack_rows(side, wide):
    groups = wide // side.shape[1]
    rows = side.shape[0] // groups
    return jnp.concatenate([side[i * rows : (i + 1) * rows] for i in range(groups)], axis=1)


def pack_rows(block, groups):
    n = block.shape[1] // groups
    return jnp.concatenate([block[:, i * n : (i + 1) * n] for i in range(groups)], axis=0)


def project_kernel(idx, a_ref, an_ref, *refs):
    pieces = refs[:WAYS]
    q_ref, k_ref, v_ref, wq_ref, wo_ref, scr = refs[WAYS:]
    rows = wq_ref.shape[0] // WAYS
    orows = scr.shape[0] // WAYS
    hw = q_ref.shape[1]

    @pl.when(pl.program_id(0) == 0)
    def _():
        for k in range(WAYS):
            j = jnp.bitwise_xor(idx[0], k)
            wq_ref[pl.ds(pl.multiple_of(j * rows, rows), rows), :] = pieces[k][:, : 3 * hw]
            tail = pieces[k][:, 3 * hw :].astype(F32)
            scr[pl.ds(pl.multiple_of(j * orows, orows), orows), :] = unpack_rows(tail, wo_ref.shape[1])
        wo_ref[:hw, :] = scr[...].astype(BF)
        norm = jnp.concatenate([an_ref[0:1, :], an_ref[1:2, :]], axis=1)
        high = norm.astype(BF).astype(F32)
        row = jnp.concatenate([high, norm - high], axis=1)
        pad = wo_ref.shape[0] - hw
        at = lax.broadcasted_iota(jnp.int32, (pad, row.shape[1]), 0)
        wo_ref[hw:, :] = jnp.where(at == 0, row, 0.0).astype(BF)

    res = dot(a_ref[...], wq_ref[...]).astype(BF)
    q_ref[...] = res[:, :hw] * BF(HD ** (-0.5))
    k_ref[...] = res[:, hw : 2 * hw]
    v_ref[...] = res[:, 2 * hw :]


def project(a, norm, pieces, hw, idx):
    rows, d = a.shape
    n = 3 * hw
    blk = lambda w: pl.BlockSpec((BLK, w), lambda s, i: (s, 0))
    return run(
        project_kernel,
        (rows // BLK,),
        [a, norm, *pieces],
        [blk(d), full(norm.shape)] + fulls(pieces),
        [far((rows, hw), BF)] * 3 + [far((d, n), BF), far((hw + 16, d), BF)],
        [blk(hw)] * 3 + [full((d, n)), full((hw + 16, d))],
        idx,
        "project",
        40,
        [pltpu.VMEM((hw, d), F32)],
    )


def attend_kernel(idx, start_ref, q_ref, k_ref, v_ref, o_ref, p_ref):
    h = pl.program_id(0)
    rows, hw = q_ref.shape
    lane = (lax.broadcasted_iota(jnp.int32, (1, hw), 1) // HD) == h
    for i in range(rows // BLK):
        lo, hi = i * BLK, (i + 1) * BLK
        qb = jnp.where(lane, q_ref[lo:hi, :], BF(0))
        s = dot_nt(qb, k_ref[:hi, :])
        kpos = lax.broadcasted_iota(jnp.int32, (BLK, hi), 1)
        qpos = lo + lax.broadcasted_iota(jnp.int32, (BLK, hi), 0)
        s = jnp.where((kpos >= start_ref[lo:hi, :]) & (kpos <= qpos), s, -1e30)
        p = jnp.exp(s - jnp.max(s, -1, keepdims=True))
        p = (p * (1.0 / rowsum(p))).astype(BF)
        p_ref[0, lo:hi, :hi] = p
        ob = dot(p, v_ref[:hi, :]).astype(BF)
        o_ref[lo:hi, :] = jnp.where(lane, ob, o_ref[lo:hi, :])


def attend(start, q, k, v, idx, after=()):
    rows, hw = q.shape
    heads = hw // HD
    return run(
        attend_kernel,
        (heads,),
        [start, q, k, v],
        fulls([start, q, k, v]),
        [far((rows, hw), BF), far((heads, rows, rows), BF)],
        [full((rows, hw)), pl.BlockSpec((1, rows, rows), lambda s, i: (s, 0, 0))],
        idx,
        "attend",
        10,
        after=after,
        hbm=(1, 2, 3),
    )


def wide_norm(o_refs):
    parts = [x[...].astype(F32) for x in o_refs]
    n = sum(x.shape[-1] for x in parts)
    mean = sum(rowsum(x) for x in parts) / n
    parts = [x - mean for x in parts]
    r = lax.rsqrt(sum(rowsum(x * x) for x in parts) / n + EPS)
    return [x * r for x in parts], r


def unpack_norm(w_ref):
    hw = w_ref.shape[0] - 16
    row = w_ref[hw:, :].astype(F32)[0:1, :]
    gain, bias, gain_low, bias_low = (row[:, i * hw : (i + 1) * hw] for i in range(4))
    return gain + gain_low, bias + bias_low


def outproj_kernel(idx, on_ref, tok_ref, *refs):
    g = (len(refs) - 2) // 2
    o_refs, w_refs = refs[:g], refs[g : 2 * g]
    h_ref, c_ref = refs[2 * g :]
    hats, _ = wide_norm(o_refs)
    acc = tok_ref[...].astype(F32)
    for k in range(g):
        gain, bias = unpack_norm(w_refs[k])
        y = (hats[k] * gain + bias).astype(BF)
        acc = acc + dot(y, w_refs[k][: gain.shape[1], :])
    h_ref[...] = acc
    hat, _ = normalize(acc)
    c_ref[...] = (hat * on_ref[2:3, :] + on_ref[3:4, :]).astype(BF)


def outproj(on, tok, o, w, idx, after=()):
    rows, d = tok.shape
    hw = o[0].shape[1]
    blk = lambda n: pl.BlockSpec((BLK, n), lambda s, i: (s, 0))
    return run(
        outproj_kernel,
        (rows // BLK,),
        [on, tok, *o, *w],
        fulls([on]) + [blk(d)] + [blk(hw)] * len(o) + fulls(w),
        [far((rows, d), F32), near((rows, d), BF)],
        [blk(d), blk(d)],
        idx,
        "outproj",
        0,
        after=after,
        hbm=(1,),
    )


def ffn_up_kernel(idx, c_ref, e_ref, fn_ref, *refs):
    ups, downs = refs[:2], refs[2:4]
    u_ref, dw_ref, st_ref, wu_ref, wd_ref = refs[4:]
    rows = ups[0].shape[1]

    @pl.when(pl.program_id(0) == 0)
    def _():
        for i, k in enumerate(ORDER):
            for odd in range(2):
                j = jnp.bitwise_xor(idx[0], k + odd)
                at = pl.ds(pl.multiple_of(j * rows, rows), rows)
                wu_ref[at, :] = ups[odd][i]
                wd_ref[at, :] = downs[i // 2][i % 2 * 2 + odd]

    u = dot(c_ref[...], wu_ref[...])
    u_ref[...] = u
    z, _ = gelu_parts(u)
    mean = rowsum(z) / z.shape[-1]
    z = z - mean
    dw = dot_nt(e_ref[...], wd_ref[...])
    dw_ref[...] = dw
    eg = dw * fn_ref[0:1, :]
    stats = [mean, rowsum(z * z), rowsum(eg), rowsum(eg * z)]
    place = lax.broadcasted_iota(jnp.int32, (BLK, 128), 1)
    tile = jnp.zeros((BLK, 128), F32)
    for i, x in enumerate(stats):
        tile = jnp.where(place == i, x, tile)
    st_ref[...] = tile.T[:8, :]


def ffn_up(c, e, fn, pieces, idx):
    rows, d = c.shape
    fl = fn.shape[1]
    rblk = lambda n: pl.BlockSpec((BLK, n), lambda s, i: (s, 0))
    return run(
        ffn_up_kernel,
        (rows // BLK,),
        [c, e, fn, *pieces],
        [rblk(d), rblk(d), full(fn.shape)] + fulls(pieces),
        [near((rows, fl), F32), near((rows, fl), F32), sds((8, rows), F32), near((d, fl), BF), far((fl, d), BF)],
        [rblk(fl), rblk(fl), pl.BlockSpec((8, BLK), lambda s, i: (0, s)), full((d, fl)), full((fl, d))],
        idx,
        "ffn_up",
        7.5,
        hbm=(1,),
    )


def rel_of(s):
    return jnp.where(s < 2, 2 * s + 1, 2 * s - 4)


def rel_block(s, i):
    return jnp.bitwise_xor(rel_of(s), i[1])


def rel_spec(n):
    return pl.BlockSpec((BLK, n), lambda s, i: (rel_block(s, i), 0))


SEND_SPEC = lambda n: pl.BlockSpec((1, BLK, n), lambda s, i: (jnp.minimum(s, 1), 0, 0))
KEEP_SPEC = lambda n: full((BLK, n))


def put_rel(send_ref, keep_ref, last_ref, value):
    @pl.when(pl.program_id(0) < 2)
    def _():
        send_ref[0] = value.astype(BF)

    @pl.when(pl.program_id(0) == 2)
    def _():
        keep_ref[...] = value

    @pl.when(pl.program_id(0) == 3)
    def _():
        last_ref[...] = value


def ffn_mid_kernel(idx, u_ref, dw_ref, st_ref, fn_ref, wu_ref, w_ref, du_ref, send_ref, keep_ref, last_ref, fg_ref):
    g = st_ref.shape[0]
    fl = u_ref.shape[1]
    n = g * fl
    st = [st_ref[k] for k in range(g)]
    mean = sum(x[0:1] for x in st) / g
    gap = [x[0:1] - mean for x in st]
    spread = sum(x[1:2] + fl * (gp * gp) for x, gp in zip(st, gap)) / n
    r = lax.rsqrt(spread + EPS)
    s_plain = sum(x[2:3] for x in st) / n
    s_norm = r * (sum(x[3:4] + gp * x[2:3] for x, gp in zip(st, gap)) / n)
    cols = jnp.concatenate([mean, r, s_plain, s_norm, jnp.zeros((124, BLK), F32)], axis=0).T
    mean, r, s_plain, s_norm = (cols[:, i : i + 1] for i in range(4))
    u = u_ref[...]
    z, t = gelu_parts(u)
    hat = (z - mean) * r
    w_ref[...] = (hat * fn_ref[0:1, :] + fn_ref[1:2, :]).astype(BF)
    dw = dw_ref[...]
    dz = r * (dw * fn_ref[0:1, :] - s_plain - hat * s_norm)
    slope = 0.5 * (1.0 + t) + 0.5 * u * (1.0 - t * t) * (GELU_A * (1.0 + (3.0 * GELU_B) * (u * u)))
    du = (dz * slope).astype(BF)
    du_ref[...] = du
    put_rel(send_ref, keep_ref, last_ref, dot_nt(du, wu_ref[...]))
    grads = jnp.concatenate([jnp.sum(dw * hat, 0, keepdims=True), jnp.sum(dw, 0, keepdims=True)], axis=0)

    @pl.when(pl.program_id(0) == 0)
    def _():
        fg_ref[...] = grads

    @pl.when(pl.program_id(0) > 0)
    def _():
        fg_ref[...] += grads


def ffn_mid(u, dw, st, fn, wu, idx):
    rows, fl = u.shape
    d = wu.shape[0]
    return run(
        ffn_mid_kernel,
        (rows // BLK,),
        [u, dw, st, fn, wu],
        [rel_spec(fl), rel_spec(fl), pl.BlockSpec((st.shape[0], 8, BLK), lambda s, i: (0, 0, rel_block(s, i)))]
        + fulls([fn, wu]),
        [far((rows, fl), BF), far((rows, fl), BF), sds((2, BLK, d), BF), far((BLK, d), F32), sds((BLK, d), F32), sds((2, fl), F32)],
        [rel_spec(fl), rel_spec(fl), SEND_SPEC(d), KEEP_SPEC(d), KEEP_SPEC(d), full((2, fl))],
        idx,
        "ffn_mid",
        6.5,
    )


def ffn_out(x, w, idx, after):
    rows, depth = x.shape
    d = w.shape[1]

    def kernel(idx, x_ref, w_ref, send_ref, keep_ref, last_ref):
        put_rel(send_ref, keep_ref, last_ref, dot(x_ref[...], w_ref[...]))

    return run(
        kernel,
        (rows // BLK,),
        [x, w],
        [rel_spec(depth), full(w.shape)],
        [sds((2, BLK, d), BF), far((BLK, d), F32), sds((BLK, d), F32)],
        [SEND_SPEC(d), KEEP_SPEC(d), KEEP_SPEC(d)],
        idx,
        "ffn_out",
        0,
        (),
        after,
        (0, 1),
    )


def put_blocks(scr, send_ref, keep_ref, first, step):
    for i, k in enumerate(ORDER):
        for odd, dest in enumerate((keep_ref, send_ref)):
            j = jnp.bitwise_xor(first, k + odd)
            value = scr[pl.ds(pl.multiple_of(j * step, step), step), :]
            dest[i, :, : value.shape[1]] = value.astype(dest.dtype)


def weight_grad(x, y, idx, name, after=()):
    rows, d = x.shape
    n = y.shape[1]
    step = d // WAYS
    steps = d // BLK

    def kernel(idx, x_ref, y_ref, send_ref, keep_ref, scr):
        s = pl.program_id(0)
        scr[pl.ds(pl.multiple_of(s * BLK, BLK), BLK), :] = dot_tn(x_ref[...], y_ref[...])

        @pl.when(s == steps - 1)
        def _():
            put_blocks(scr, send_ref, keep_ref, idx[0], step)

    return run(
        kernel,
        (steps,),
        [x, y],
        [pl.BlockSpec((rows, BLK), lambda s, i: (0, s)), full(y.shape)],
        [sds((WAYS // 2, step, n), BF), far((WAYS // 2, step, n), F32)],
        [full((WAYS // 2, step, n))] * 2,
        idx,
        name,
        3.5,
        [pltpu.VMEM((d, n), F32)],
        after,
    )


def qkv_back(a, dqkv, wq, go, idx, after=()):
    rows, d = a.shape
    n = dqkv.shape[1]
    step = d // WAYS
    hw = go[2].shape[0]
    groups = d // hw
    orows = hw // WAYS

    def kernel(idx, a_ref, d_ref, w_ref, go0_ref, go1_ref, go2_ref, gs_ref, gk_ref, send_ref, keep_ref, last_ref, scr, go_ref):
        go_ref[...] = go0_ref[...] + go1_ref[0].astype(F32) + go2_ref[...].astype(F32)
        for s in range(d // BLK):
            scr[s * BLK : (s + 1) * BLK, :] = dot_tn(a_ref[:, s * BLK : (s + 1) * BLK], d_ref[...])
        put_blocks(scr, gs_ref, gk_ref, idx[0], step)
        for i, k in enumerate(ORDER):
            for odd, dest in enumerate((gk_ref, gs_ref)):
                j = jnp.bitwise_xor(idx[0], k + odd)
                tail = pack_rows(go_ref[pl.ds(pl.multiple_of(j * orows, orows), orows), :], groups)
                dest[i, :, n:] = tail.astype(dest.dtype)
        for k in range(4):
            j = jnp.bitwise_xor(idx[1], k)
            value = dot_nt(d_ref[pl.ds(pl.multiple_of(j * BLK, BLK), BLK), :], w_ref[...])
            if k % 2:
                send_ref[k // 2] = value.astype(BF)
            else:
                (last_ref if k else keep_ref)[...] = value

    ins = [a, dqkv, wq, *go]
    lead = pl.BlockSpec((1, hw, d), lambda s, i: (0, 0, 0))
    half = (WAYS // 2, step, d)
    part = (2, BLK, d)
    outs = [sds(half, BF), far(half, F32), sds(part, BF), far(part[1:], F32), sds(part[1:], F32)]
    return run(
        kernel, (1,), ins, fulls(ins[:4]) + [lead, full(go[2].shape)], outs, fulls(outs), idx, "qkv_back", 40,
        [pltpu.VMEM((d, n), F32), pltpu.VMEM((hw, d), F32)],
        after=after,
        hbm=(0, 2, 3),
    )


def shard_back_kernel(idx, dc0_ref, dc1_ref, dc2_ref, h_ref, e_ref, on_ref, *refs):
    g = 4
    o_refs, w_refs = refs[:g], refs[g : 2 * g]
    dh_ref, ol_ref, ag_ref, *do_refs = refs[2 * g :]
    do_refs, (gs_ref, gk_ref, gl_ref) = do_refs[:g], do_refs[g:]
    dc = dc0_ref[...] + dc1_ref[0].astype(F32) + dc2_ref[...].astype(F32)
    hat, r = normalize(h_ref[...])
    wgt = dc * on_ref[2:3, :]
    n = dc.shape[-1]
    dh = e_ref[...].astype(F32) + r * (wgt - rowsum(wgt) / n - hat * (rowsum(wgt * hat) / n))
    dh_ref[...] = dh
    ol_ref[...] = jnp.concatenate([jnp.sum(dc * hat, 0, keepdims=True), jnp.sum(dc, 0, keepdims=True)], axis=0)
    dhb = dh.astype(BF)
    hats, r = wide_norm(o_refs)
    norms = [unpack_norm(w_refs[k]) for k in range(g)]
    dys = [dot_nt(dhb, w_refs[k][: norms[k][0].shape[1], :]) for k in range(g)]
    wgts = [dys[k] * norms[k][0] for k in range(g)]
    s_plain = sum(rowsum(x) for x in wgts) / n
    s_norm = sum(rowsum(x * y) for x, y in zip(wgts, hats)) / n
    for k in range(g):
        do_refs[k][...] = (r * (wgts[k] - s_plain - hats[k] * s_norm)).astype(BF)
        ag_ref[jnp.bitwise_xor(idx[1], k)] = jnp.concatenate(
            [jnp.sum(dys[k] * hats[k], 0, keepdims=True), jnp.sum(dys[k], 0, keepdims=True)], axis=0
        )
    for k in range(g):
        y = (hats[k] * norms[k][0] + norms[k][1]).astype(BF)
        value = dot_tn(y, dhb)
        if k % 2:
            gs_ref[k // 2] = value.astype(BF)
        else:
            (gl_ref if k else gk_ref)[...] = value


def shard_back(dc_keep, dc_one, dc_two, h, e, on, o, w, idx, after):
    rows, d = h.shape
    g = len(o)
    hw = o[0].shape[1]
    mine = lambda n: pl.BlockSpec((BLK, n), lambda s, i: (i[1], 0))
    lead = pl.BlockSpec((1, BLK, d), lambda s, i: (0, 0, 0))
    ins = [dc_keep, dc_one, dc_two, h, e, on, *o, *w]
    return run(
        shard_back_kernel,
        (1,),
        ins,
        [full((BLK, d)), lead, full((BLK, d)), mine(d), mine(d)] + fulls([on]) + [mine(hw)] * g + fulls(w),
        [far((BLK, d), F32), sds((2, d), F32), sds((g, 2, hw), F32)]
        + [sds((BLK, hw), BF)] * g
        + [sds((2, hw, d), BF), far((hw, d), F32), sds((hw, d), F32)],
        [full((BLK, d)), full((2, d)), full((g, 2, hw))]
        + [full((BLK, hw))] * g
        + [full((2, hw, d)), full((hw, d)), full((hw, d))],
        idx,
        "shard_back",
        0,
        after=after,
        hbm=(0, 3, 4) + tuple(range(6, 6 + 2 * g)),
    )


def attend_back_kernel(idx, q_ref, k_ref, v_ref, p_ref, *refs):
    d_refs = refs[:4]
    out_ref, do_scr, dq_scr, dk_scr, dv_scr = refs[4:]
    h = pl.program_id(0)
    rows, hw = q_ref.shape

    @pl.when(h == 0)
    def _():
        for k in range(4):
            j = jnp.bitwise_xor(idx[1], k)
            do_scr[pl.ds(pl.multiple_of(j * BLK, BLK), BLK), :] = d_refs[k][...]
        dk_scr[...] = jnp.zeros_like(dk_scr)
        dv_scr[...] = jnp.zeros_like(dv_scr)
        dq_scr[...] = jnp.zeros_like(dq_scr)

    lane = (lax.broadcasted_iota(jnp.int32, (1, hw), 1) // HD) == h
    for i in range(rows // BLK):
        lo, hi = i * BLK, (i + 1) * BLK
        dob = jnp.where(lane, do_scr[lo:hi, :], BF(0))
        qb = jnp.where(lane, q_ref[lo:hi, :], BF(0))
        pb = p_ref[0, lo:hi, :hi]
        p = pb.astype(F32)
        dp = dot_nt(dob, v_ref[:hi, :])
        ds = (p * (dp - rowsum(p * dp))).astype(BF)
        dq_scr[lo:hi, :] = jnp.where(lane, dot(ds, k_ref[:hi, :]), dq_scr[lo:hi, :])
        dk_scr[:hi, :] += dot_tn(ds, qb)
        dv_scr[:hi, :] += dot_tn(pb, dob)

    @pl.when(h == pl.num_programs(0) - 1)
    def _():
        out_ref[...] = jnp.concatenate([dq_scr[...] * HD ** (-0.5), dk_scr[...], dv_scr[...]], axis=1).astype(BF)


def attend_back(q, k, v, p, do, idx, after):
    rows, hw = q.shape
    heads = hw // HD
    return run(
        attend_back_kernel,
        (heads,),
        [q, k, v, p, *do],
        fulls([q, k, v]) + [pl.BlockSpec((1, rows, rows), lambda s, i: (s, 0, 0))] + fulls(do),
        [sds((rows, 3 * hw), BF)],
        [full((rows, 3 * hw))],
        idx,
        "attend_back",
        11,
        [pltpu.VMEM((rows, hw), BF)] + [pltpu.VMEM((rows, hw), F32)] * 3,
        after=after,
        hbm=range(4),
    )[0]


def shard_end_kernel(idx, da0_ref, da1_ref, da2_ref, tok_ref, on_ref, dh_ref, gt_ref, oe_ref):
    da = da0_ref[...] + da1_ref[0].astype(F32) + da2_ref[...].astype(F32)
    hat, r = normalize(tok_ref[...].astype(F32))
    wgt = da * on_ref[0:1, :]
    n = da.shape[-1]
    grad = r * (wgt - rowsum(wgt) / n - hat * (rowsum(wgt * hat) / n))
    gt_ref[...] = (dh_ref[...] + grad).astype(BF)
    oe_ref[...] = jnp.concatenate([jnp.sum(da * hat, 0, keepdims=True), jnp.sum(da, 0, keepdims=True)], axis=0)


def shard_end(da_keep, da_one, da_two, tok, on, dh, idx, after=()):
    d = tok.shape[1]
    lead = pl.BlockSpec((1, BLK, d), lambda s, i: (0, 0, 0))
    return run(
        shard_end_kernel,
        (1,),
        [da_keep, da_one, da_two, tok, on, dh],
        [full((BLK, d)), lead, full((BLK, d)), pl.BlockSpec((BLK, d), lambda s, i: (i[1], 0)), full(on.shape), full((BLK, d))],
        [sds((BLK, d), BF), sds((2, d), F32)],
        [full((BLK, d)), full((2, d))],
        idx,
        "shard_end",
        0,
        after=after,
    )


def spread_rows(parts, idx, name, after=()):
    rows, d = parts[0].shape

    def kernel(idx, *refs):
        for k, part in enumerate(refs[:-2]):
            at = pl.ds(pl.multiple_of(jnp.bitwise_xor(idx[1], k) * rows, rows), rows)
            refs[-2][at, :] = part[...]
        refs[-1][...] = jnp.zeros(refs[-1].shape, F32)

    outs = [sds((rows * len(parts), d), BF), sds((8, 128), F32)]
    return run(kernel, (1,), parts, fulls(parts), outs, fulls(outs), idx, name, 0, (), after)


def far_sum(last, got, idx, after=(), tick=TICK):
    rows, d = last.shape

    def kernel(idx, last_ref, got_ref, out_ref):
        out_ref[...] = (last_ref[...] + got_ref[0].astype(F32)).astype(BF)

    second = pl.BlockSpec((1, rows, d), lambda s, i: (1, 0, 0))
    out = [sds((rows, d), BF)]
    return run(kernel, (1,), [last, got], [full((rows, d)), second], out, fulls(out), idx, "far_sum", tick, (), after)[0]


def fold(keep, got, idx, after=(), tick=TICK):
    count, rows, d = keep.shape
    half = count // 2

    def kernel(idx, keep_ref, got_ref, stay_ref, send_ref):
        stay_ref[...] = keep_ref[:half] + got_ref[:half].astype(F32)
        send = (keep_ref[half:] + got_ref[half:].astype(F32)).astype(BF)
        send_ref[...] = send if half > 1 else send[0]

    outs = [sds((half, rows, d), F32), sds((half, rows, d) if half > 1 else (rows, d), BF)]
    return run(kernel, (1,), [keep, got], fulls([keep, got]), outs, fulls(outs), idx, "fold", tick, (), after, (0,) if half > 1 else ())


def close(own, got, idx, after=(), vec=None, tick=TICK):
    rows, d = got[0].shape

    def kernel(idx, own_ref, *refs):
        out_ref = refs[-1]
        total = own_ref[...].reshape(rows, d)
        for ref in refs[: len(got)]:
            total = total + ref[...].astype(F32)
        out_ref[:rows, :] = total.astype(BF)
        if vec is not None:
            x = refs[len(got)][...]
            high = x.astype(BF).astype(F32)
            out_ref[rows:, :] = jnp.concatenate([high, x - high], axis=0).astype(BF)

    ins = [own, *got] + ([] if vec is None else [vec])
    out = [sds((rows if vec is None else rows + 2 * vec.shape[0], d), BF)]
    return run(kernel, (1,), ins, fulls(ins), out, fulls(out), idx, "close", tick, (), after)[0]


def join(parts, idx, after=(), tick=2 * TICK):
    shapes = [x.shape if len(x.shape) == 3 else (1, *x.shape) for x in parts]

    def kernel(idx, *refs):
        at = 0
        for ref, shape in zip(refs, shapes):
            refs[-1][at : at + shape[0]] = ref[...].reshape(shape)
            at += shape[0]

    out = [sds((sum(x[0] for x in shapes), *shapes[0][1:]), BF)]
    return run(kernel, (1,), parts, fulls(parts), out, fulls(out), idx, "join", tick, (), after)[0]


def block_end(h, keep, got, last, idx, after=()):
    rows, d = last.shape

    def kernel(idx, h_ref, keep_ref, got_ref, last_ref, out_ref):
        total = h_ref[...] + keep_ref[...] + got_ref[0].astype(F32) + last_ref[...].astype(F32)
        out_ref[...] = total.astype(BF)

    lead = pl.BlockSpec((1, rows, d), lambda s, i: (0, 0, 0))
    mine = pl.BlockSpec((rows, d), lambda s, i: (i[1], 0))
    own = full((rows, d))
    ins = [h, keep, got, last]
    out = [sds((rows, d), BF)]
    return run(
        kernel, (1,), ins, [mine, own, lead, own], out, fulls(out), idx, "block_end", TICK, (), after, (0,)
    )[0]


def vec_add(x, y, idx, after=(), tick=TICK):
    def kernel(idx, x_ref, y_ref, out_ref):
        out_ref[...] = x_ref[...] + y_ref[...]

    out = [sds(x.shape, F32)]
    return run(kernel, (1,), [x, y], fulls([x, y]), out, fulls(out), idx, "vec_add", tick, (), after)[0]


def one_hot(place, count, width):
    at = lax.broadcasted_iota(jnp.int32, (count, width), 1)
    want = place * count + lax.broadcasted_iota(jnp.int32, (count, width), 0)
    return jnp.where(at == want, 1.0, 0.0).astype(BF)


def precondition(idx, ins, outs, scr, total, flip):
    w_ref, l_ref, r_ref, lr_ref, rr_ref = ins
    g_ref, nl_ref, nr_ref, nw_ref, copy_ref = outs
    d, n = scr.shape
    rows, side = w_ref.shape[0], r_ref.shape[0]
    whole = scr[...]
    g_ref[...] = whole.T if flip else whole
    grad = whole.astype(BF)
    scale = 1.0 / total
    own_cols = dot_nt(one_hot(idx[2], side, n), grad).astype(BF)
    own_rows = dot(one_hot(idx[2], rows, d), grad).astype(BF)
    nr_ref[...] = DECAY * r_ref[...] + ((1.0 - DECAY) * scale * scale) * dot(own_cols, grad)
    nl_ref[...] = DECAY * l_ref[...] + ((1.0 - DECAY) * scale * scale) * dot_nt(own_rows, grad)
    part = dot(lr_ref[...].astype(BF), grad).astype(BF)
    new = w_ref[...] - (MAT_RATE * scale) * dot(part, rr_ref[...].astype(BF))
    nw_ref[...] = new
    copy_ref[...] = new.astype(BF)


def update_outs(mats):
    w, left, right = mats[:3]
    (rows, n), d, side = w.shape, left.shape[1], right.shape[0]
    flip = n % 128 != 0
    outs = [sds((n, d) if flip else (d, n), F32), sds((rows, d), F32), sds((side, n), F32)]
    return outs + [sds((rows, n), F32), sds((rows, n), BF)], flip, pltpu.VMEM((d, n), F32)


def update_one(mats, near_blocks, far_blocks, total, idx, name, after=(), tick=0):
    outs, flip, scr = update_outs(mats)
    step = mats[1].shape[1] // WAYS

    def kernel(idx, *refs):
        ins, (even, odd), rest = refs[:5], refs[5:7], refs[7:]
        for i, k in enumerate(ORDER):
            for far_one, blocks in enumerate((even, odd)):
                j = jnp.bitwise_xor(idx[0], k + far_one)
                rest[6][pl.ds(pl.multiple_of(j * step, step), step), :] = blocks[i].astype(F32)
        precondition(idx, ins, rest[:5], rest[6], total, flip)
        rest[5][...] = jnp.zeros(rest[5].shape, F32)

    ins = [*mats, near_blocks, far_blocks]
    outs = outs + [sds((8, 128), F32)]
    res = run(kernel, (1,), ins, fulls(ins), outs, fulls(outs), idx, name, tick, [scr], after, range(5))
    return [res[0].T if flip else res[0], *res[1:]]


def update_pair(mats, mats2, near_blocks, far_blocks, norms, rates, total, idx, name, after=()):
    outs, flip, scr = update_outs(mats)
    outs2, flip2, scr2 = update_outs(mats2)
    step, n = mats[1].shape[1] // WAYS, mats[0].shape[1]
    step2, n2 = mats2[1].shape[1] // WAYS, mats2[0].shape[1]
    half = (near_blocks.shape[1] - step) // 2
    wide = norms[1].shape[1]

    def kernel(idx, *refs):
        ins, ins2, (even, odd), norm_refs, rest = refs[:5], refs[5:10], refs[10:12], refs[12:15], refs[15:]
        sums = 0.0
        for i, k in enumerate(ORDER):
            for far_one, blocks in enumerate((even, odd)):
                j = jnp.bitwise_xor(idx[0], k + far_one)
                block = blocks[i].astype(F32)
                rest[-2][pl.ds(pl.multiple_of(j * step, step), step), :] = block[:step, :n]
                rest[-1][pl.ds(pl.multiple_of(j * step2, step2), step2), :] = unpack_rows(block[:step, n:], n2)
                sums = sums + (block[step : step + half] + block[step + half :])
        grads = [sums[:4], jnp.concatenate([sums[4:5, :wide], sums[4:5, wide : 2 * wide]], axis=0), sums[5:7]]
        for i, (grad, rate) in enumerate(zip(grads, (rates[0], rates[0], rates[1]))):
            rest[10 + i][...] = grad
            rest[13 + i][...] = norm_refs[i][...] - rate * grad
        precondition(idx, ins2, rest[5:10], rest[-1], total, flip2)
        precondition(idx, ins, rest[:5], rest[-2], total, flip)

    all_outs = outs + outs2 + [sds(x.shape, F32) for x in [*norms, *norms]]
    ins = [*mats, *mats2, near_blocks, far_blocks, *norms]
    res = run(kernel, (1,), ins, fulls(ins), all_outs, fulls(all_outs), idx, name, 6, [scr, scr2], after, range(10))
    res = list(res)
    res[0] = res[0].T if flip else res[0]
    res[5] = res[5].T if flip2 else res[5]
    return res[:5], res[5:10], res[10:]


def body(
    tokens,
    cotangent,
    doc_lengths,
    outer_norms,
    attn_norm,
    ffn_norm,
    w_qkv,
    left_qkv,
    right_qkv,
    left_root_qkv,
    right_root_qkv,
    w_out,
    left_out,
    right_out,
    left_root_out,
    right_root_out,
    w_up,
    left_up,
    right_up,
    left_root_up,
    right_root_up,
    w_down,
    left_down,
    right_down,
    left_root_down,
    right_root_down,
):
    row_count = tokens.shape[0]
    n_dp, n_mp = lax.axis_size("dp"), lax.axis_size("mp")
    fine = n_dp // WAYS
    total = row_count * n_dp
    dp_at, mp_at = lax.axis_index("dp"), lax.axis_index("mp")
    idx = jnp.stack([dp_at // fine, mp_at, dp_at]).astype(jnp.int32)
    hw = w_qkv.shape[2] // 3

    def swap(x, axis, size, k):
        return lax.ppermute(x, axis, [(i, i ^ k) for i in range(size)])

    def dp(x, k):
        return swap(x, "dp", n_dp, k * fine)

    def mp(x, k):
        return swap(x, "mp", n_mp, k)

    def fine_rows(x):
        k = 1
        while k < fine:
            got = swap(x, "dp", n_dp, k)
            x = jnp.where((dp_at & k) == 0, jnp.concatenate([x, got], 0), jnp.concatenate([got, x], 0))
            k *= 2
        return x

    def fine_sum(x):
        k = 1
        while k < fine:
            x = x + swap(x, "dp", n_dp, k)
            k *= 2
        return x

    def gather8(own, *early):
        parts = {0: own}
        for k in (2, 4, 6):
            parts[k] = dp(own, k)
        parts[1] = dp(own, 1)
        for k in (2, 4, 6):
            parts[k ^ 1] = dp(after(parts[k], *early) if early else parts[k], 1)
        return [parts[k] for k in range(WAYS)]

    def gather4(own):
        far = mp(own, 2)
        return [own, mp(own, 1), far, mp(far, 1)]

    def scatter4(send, keep):
        got = mp(send, 1)
        return keep, got, mp((keep[1] + got[1].astype(F32)).astype(BF), 2)

    def gather8_halves(own):
        two = jnp.stack([own, dp(own, 4)])
        four = jnp.concatenate([two, dp(two, 2)])
        return four, dp(four, 1)

    def after(x, *deps):
        return lax.optimization_barrier((x, *deps))[0]

    out_rows = fine_rows(w_out[0].astype(BF))
    groups = tokens.shape[1] // hw
    first = jnp.concatenate([fine_rows(w_qkv[0].astype(BF)), pack_rows(out_rows, groups)], axis=1)
    up_own = fine_rows(w_up[0].astype(BF))
    down_own = fine_rows(w_down[0].astype(BF))
    down_two = jnp.stack([down_own, dp(down_own, 1)])
    first = gather8(first, down_two)

    ends = jnp.cumsum(doc_lengths[0])
    places = jnp.arange(row_count, dtype=jnp.int32)
    start = jnp.max(jnp.where(ends[None, :] <= places[:, None], ends[None, :], 0), axis=1, keepdims=True)
    start = start.astype(jnp.int32)
    hat, _ = normalize(tokens.astype(F32))
    a_low = (hat * outer_norms[0] + outer_norms[1]).astype(BF)

    up_go = after(up_own, first[2], first[4], first[6], down_two)
    up_z = [dp(up_go, k) for k in ORDER[1:]]
    down_z2 = dp(after(down_two, up_go), 4)
    q, k, v, wq, wo = project(a_low, attn_norm, first, hw, idx)
    wo_far = mp(wo, 2)
    o, probs = attend(start, q, k, v, idx)
    o, *up_z = lax.optimization_barrier((o, *up_z))
    up_four = jnp.stack([up_own, *up_z])
    o, wo, wo_far, up_four = lax.optimization_barrier((o, wo, wo_far, up_four))
    o_far = mp(o, 2)
    up_x = dp(up_four, 1)
    wo_near, wo_last = mp(after(wo, up_four), 1), mp(wo_far, 1)
    down_four = join([down_two, down_z2], idx, [up_four, wo_near, wo_last])
    down_z1 = dp(down_four, 2)
    o_near = mp(after(o, o_far), 1)
    o_all = [o, o_near, o_far, mp(o_far, 1)]
    wo_all = [wo, wo_near, wo_far, wo_last]
    hidden, c_low = outproj(outer_norms, tokens, o_all, wo_all, idx, [up_x])
    u, dw, stats, wu, wd = ffn_up(c_low, cotangent, ffn_norm, [up_four, up_x, down_four, down_z1], idx)
    stats = lax.all_gather(stats, "mp")
    w_low, du, dc_send, dc_keep, dc_last, ffn_grads = ffn_mid(u, dw, stats, ffn_norm, wu, idx)
    dc_got = mp(dc_send, 1)
    dc_sum = far_sum(dc_last, dc_got, idx)
    down_send, down_keep = weight_grad(w_low, cotangent, idx, "grad_down", [dc_sum])
    down_x = dp(down_send, 1)
    up_send, up_keep = weight_grad(c_low, du, idx, "grad_up", [down_send])
    up_x2 = dp(after(up_send, down_send), 1)
    dh, outer_late, attn_grads, *rest = shard_back(
        dc_keep, dc_got, mp(dc_sum, 2), hidden, cotangent, outer_norms, o_all, wo_all, idx, [up_send]
    )
    do, (go_send, go_keep, go_last) = rest[:n_mp], rest[n_mp:]
    do = [do[0]] + [mp(do[k], k) for k in range(1, n_mp)]
    go_got = mp(go_send, 1)
    bo_send, bo_keep, bo_last = ffn_out(w_low, wd, idx, [do[1]])
    down_t, down_low = fold(down_keep, down_x, idx, [bo_send], 0)
    go_sum = far_sum(go_last, go_got, idx, [down_low], 0)
    dqkv = attend_back(q, k, v, probs, do, idx, [go_sum])
    down_z1 = dp(down_low, 2)
    go_far = mp(go_sum, 2)
    bo_got = mp(after(bo_send, dqkv), 1)
    down_t, down_low = fold(down_t, down_z1, idx, [dqkv])
    up_t, up_low = fold(up_keep, up_x2, idx, [down_low])
    qkv_send, qkv_keep, da_send, da_keep, da_last = qkv_back(
        a_low, dqkv, wq, [go_keep, go_got, go_far], idx, [up_low]
    )

    down_z2, up_z1 = dp(down_low, 4), dp(up_low, 2)
    qkv_x = dp(qkv_send, 1)
    da_got = mp(da_send, 1)
    bo_sum = far_sum(bo_last, bo_got, idx, [qkv_send], 0)
    bo_far = mp(bo_sum, 2)
    da_sum = far_sum(da_last, da_got, idx, [bo_sum])
    da_far = mp(da_sum, 2)
    down_done = fine_sum(close(down_t, [down_z2], idx, [da_sum]))
    down_r4 = dp(down_done, 4)
    qkv_t, qkv_low = fold(qkv_keep, qkv_x, idx, [down_done], 0)
    qkv_z1 = dp(qkv_low, 2)
    up_t, up_low = fold(up_t, up_z1, idx, [qkv_low])
    up_z2 = dp(up_low, 4)
    down_two = join([down_done, down_r4], idx, [up_low])
    down_r2 = dp(down_two, 2)
    out_own = block_end(hidden, bo_keep, bo_got, bo_far, idx, [down_two])
    out_far = mp(out_own, 2)
    gt, outer_early = shard_end(da_keep, da_got, da_far, tokens, outer_norms, dh, idx, [out_own])
    gt_far = mp(gt, 2)
    lanes = outer_late.shape[1]
    vec = jnp.concatenate([outer_early, outer_late, attn_grads.reshape(-1, lanes)])
    vec_got = mp(vec, 1)
    up_done = fine_sum(close(up_t, [up_z2], idx, [gt]))
    up_r4 = dp(up_done, 4)
    qkv_t, qkv_low = fold(qkv_t, qkv_z1, idx, [up_done])
    qkv_z2 = dp(qkv_low, 4)
    vec = vec_add(vec, vec_got, idx, [qkv_low])
    vec_got = mp(vec, 2)
    down_four = join([down_two, down_r2], idx, [vec])
    down_other = dp(down_four, 1)
    up_two = join([up_done, up_r4], idx, [down_four, gt_far, out_far])
    up_r2 = dp(up_two, 2)
    vec = vec_add(vec, vec_got, idx, [up_two])
    attn_own = lax.dynamic_slice_in_dim(vec[4:].reshape(n_mp, -1), mp_at, 1, 0)
    attn_own = jnp.pad(attn_own, ((0, 0), (0, lanes - attn_own.shape[1])))
    vec = jnp.concatenate([vec[:4], attn_own, ffn_grads, jnp.zeros((1, lanes), F32)])
    vec = fine_sum(vec)
    qkv_own = close(qkv_t, [qkv_z2], idx, [up_two], None if fine > 1 else vec)
    if fine > 1:
        high = vec.astype(BF)
        qkv_own = jnp.concatenate([fine_sum(qkv_own), high, (vec - high.astype(F32)).astype(BF)])
    qkv_z = [dp(qkv_own, k) for k in ORDER[1:]]
    up_four = join([up_two, up_r2], idx, [qkv_own])
    up_other = dp(up_four, 1)
    down_mats = [x[0] for x in (w_down, left_down, right_down, left_root_down, right_root_down)]
    *down_res, token = update_one(down_mats, down_four, down_other, total, idx, "update_down", [up_four])
    qkv_four = join([qkv_own, *qkv_z], idx, [token], 10)
    qkv_other = dp(qkv_four, 1)

    def mats(*arrays):
        return [x[0] for x in arrays]

    up_mats = mats(w_up, left_up, right_up, left_root_up, right_root_up)
    *up_res, token = update_one(up_mats, up_four, up_other, total, idx, "update_up", [qkv_four], 0)
    gt_far, out_far = after(gt_far, token), after(out_far, token)
    gt_all = [gt, mp(after(gt, gt_far), 1), gt_far, mp(gt_far, 1)]
    grad_tokens, token = spread_rows(gt_all, idx, "spread_tokens", [token])
    out_all = [out_own, mp(after(out_own, out_far), 1), out_far, mp(out_far, 1)]
    block_out, token = spread_rows(out_all, idx, "spread_out", [token])
    qkv_res, out_res, vecs = update_pair(
        mats(w_qkv, left_qkv, right_qkv, left_root_qkv, right_root_qkv),
        mats(w_out, left_out, right_out, left_root_out, right_root_out),
        qkv_four,
        qkv_other,
        [outer_norms, attn_norm, ffn_norm],
        (VEC_RATE / math.sqrt(total), UNIT_RATE / math.sqrt(total)),
        total,
        idx,
        "update_qkv",
        [token],
    )

    return (
        block_out,
        grad_tokens,
        *vecs,
        *(x[None] for x in qkv_res),
        *(x[None] for x in out_res),
        *(x[None] for x in up_res),
        *(x[None] for x in down_res),
    )


def solution(mesh):
    rows = P("dp", None)
    mats = (P("mp", "dp", None),) * 4 + (P("mp", None, None),)
    res = (P("mp", None, None),) + (P("mp", "dp", None),) * 4
    cols = P(None, "mp")
    return jax.shard_map(
        body,
        mesh=mesh,
        in_specs=(rows, rows, rows, P(), cols, cols) + mats * 4,
        out_specs=(rows, rows, P(), cols, cols, P(), cols, cols) + res * 4,
        check_vma=False,
    )
```

```python
import math

import jax
import jax.numpy as jnp
from jax import lax
from jax.experimental import pallas as pl
from jax.experimental.pallas import tpu as pltpu
from jax.sharding import PartitionSpec as P

HD = 64
EPS = 1e-05
DECAY = 0.5
MAT_RATE = 0.5
VEC_RATE = 0.05
UNIT_RATE = 0.3
GELU_A = math.sqrt(2.0 / math.pi)
GELU_B = 0.044715
BF = jnp.bfloat16
F32 = jnp.float32
VMEM = 22 * 1024 * 1024
WAYS = 8
RATE = 4e8
TICK = 5
BLK = 256
WIDE = 512
ORDER = (0, 4, 2, 6)


def full(shape):
    return pl.BlockSpec(shape, lambda *args: (0,) * len(shape))


def fulls(arrays):
    return [full(x.shape) for x in arrays]


def run(kernel, grid, ins, in_specs, outs, out_specs, idx, name, micros, scratch=(), after=(), hbm=()):
    count, kernel_in = len(ins), kernel
    ins = [pltpu.with_memory_space_constraint(x, pltpu.HBM) if i in hbm else x for i, x in enumerate(ins)]

    def kernel(idx, *refs):
        kernel_in(idx, *refs[:count], *refs[count + len(after) :])

    return pl.pallas_call(
        kernel,
        grid_spec=pltpu.PrefetchScalarGridSpec(
            num_scalar_prefetch=1,
            grid=grid,
            in_specs=list(in_specs) + [pl.BlockSpec(memory_space=pl.ANY)] * len(after),
            out_specs=out_specs,
            scratch_shapes=list(scratch),
        ),
        out_shape=outs,
        compiler_params=pltpu.CompilerParams(vmem_limit_bytes=VMEM),
        cost_estimate=pl.CostEstimate(flops=int(micros * RATE), bytes_accessed=1024, transcendentals=0),
        name=name,
    )(idx, *ins, *after)


def sds(shape, dtype):
    return jax.ShapeDtypeStruct(shape, dtype)


def near(shape, dtype):
    return pltpu.VMEM(shape, dtype)


def far(shape, dtype):
    return pltpu.HBM(shape, dtype)


def dot(x, y):
    return jnp.dot(x, y, preferred_element_type=F32)


def dot_nt(x, y):
    return lax.dot_general(x, y, (((1,), (1,)), ((), ())), preferred_element_type=F32)


def dot_tn(x, y):
    return lax.dot_general(x, y, (((0,), (0,)), ((), ())), preferred_element_type=F32)


def rowsum(x):
    return jnp.sum(x, -1, keepdims=True)


def normalize(x):
    n = x.shape[-1]
    off = x - rowsum(x) / n
    r = lax.rsqrt(rowsum(off * off) / n + EPS)
    return off * r, r


def gelu_parts(u):
    t = jnp.tanh(GELU_A * (u + GELU_B * (u * u * u)))
    return 0.5 * u * (1.0 + t), t


def unpack_rows(side, wide):
    groups = wide // side.shape[1]
    rows = side.shape[0] // groups
    return jnp.concatenate([side[i * rows : (i + 1) * rows] for i in range(groups)], axis=1)


def pack_rows(block, groups):
    n = block.shape[1] // groups
    return jnp.concatenate([block[:, i * n : (i + 1) * n] for i in range(groups)], axis=0)


def project_kernel(idx, a_ref, an_ref, *refs):
    pieces = refs[:WAYS]
    q_ref, k_ref, v_ref, wq_ref, wo_ref, scr = refs[WAYS:]
    rows = wq_ref.shape[0] // WAYS
    orows = scr.shape[0] // WAYS
    hw = q_ref.shape[1]

    @pl.when(pl.program_id(0) == 0)
    def _():
        for k in range(WAYS):
            j = jnp.bitwise_xor(idx[0], k)
            wq_ref[pl.ds(pl.multiple_of(j * rows, rows), rows), :] = pieces[k][:, : 3 * hw]
            tail = pieces[k][:, 3 * hw :].astype(F32)
            scr[pl.ds(pl.multiple_of(j * orows, orows), orows), :] = unpack_rows(tail, wo_ref.shape[1])
        wo_ref[:hw, :] = scr[...].astype(BF)
        norm = jnp.concatenate([an_ref[0:1, :], an_ref[1:2, :]], axis=1)
        high = norm.astype(BF).astype(F32)
        row = jnp.concatenate([high, norm - high], axis=1)
        pad = wo_ref.shape[0] - hw
        at = lax.broadcasted_iota(jnp.int32, (pad, row.shape[1]), 0)
        wo_ref[hw:, :] = jnp.where(at == 0, row, 0.0).astype(BF)

    res = dot(a_ref[...], wq_ref[...]).astype(BF)
    q_ref[...] = res[:, :hw] * BF(HD ** (-0.5))
    k_ref[...] = res[:, hw : 2 * hw]
    v_ref[...] = res[:, 2 * hw :]


def project(a, norm, pieces, hw, idx):
    rows, d = a.shape
    n = 3 * hw
    blk = lambda w: pl.BlockSpec((BLK, w), lambda s, i: (s, 0))
    return run(
        project_kernel,
        (rows // BLK,),
        [a, norm, *pieces],
        [blk(d), full(norm.shape)] + fulls(pieces),
        [far((rows, hw), BF)] * 3 + [far((d, n), BF), far((hw + 16, d), BF)],
        [blk(hw)] * 3 + [full((d, n)), full((hw + 16, d))],
        idx,
        "project",
        40,
        [pltpu.VMEM((hw, d), F32)],
    )


def attend_kernel(idx, start_ref, q_ref, k_ref, v_ref, o_ref, *p_refs):
    h = pl.program_id(0)
    rows, hw = q_ref.shape
    lane = (lax.broadcasted_iota(jnp.int32, (1, hw), 1) // HD) == h
    for i in range(rows // BLK):
        lo, hi = i * BLK, (i + 1) * BLK
        qb = jnp.where(lane, q_ref[lo:hi, :], BF(0))
        s = dot_nt(qb, k_ref[:hi, :])
        kpos = lax.broadcasted_iota(jnp.int32, (BLK, hi), 1)
        qpos = lo + lax.broadcasted_iota(jnp.int32, (BLK, hi), 0)
        s = jnp.where((kpos >= start_ref[lo:hi, :]) & (kpos <= qpos), s, -1e30)
        p = jnp.exp(s - jnp.max(s, -1, keepdims=True))
        p = (p * (1.0 / rowsum(p))).astype(BF)
        p_refs[i][0] = p
        ob = dot(p, v_ref[:hi, :]).astype(BF)
        o_ref[lo:hi, :] = jnp.where(lane, ob, o_ref[lo:hi, :])


def widths(rows):
    return range(BLK, rows + BLK, BLK)


def head_spec(width):
    return pl.BlockSpec((1, BLK, width), lambda s, i: (s, 0, 0))


def attend(start, q, k, v, idx, after=()):
    rows, hw = q.shape
    heads = hw // HD
    return run(
        attend_kernel,
        (heads,),
        [start, q, k, v],
        fulls([start, q, k, v]),
        [far((rows, hw), BF)] + [far((heads, BLK, w), BF) for w in widths(rows)],
        [full((rows, hw))] + [head_spec(w) for w in widths(rows)],
        idx,
        "attend",
        10,
        after=after,
        hbm=(1, 2, 3),
    )


def wide_norm(o_refs):
    parts = [x[...].astype(F32) for x in o_refs]
    n = sum(x.shape[-1] for x in parts)
    mean = sum(rowsum(x) for x in parts) / n
    parts = [x - mean for x in parts]
    r = lax.rsqrt(sum(rowsum(x * x) for x in parts) / n + EPS)
    return [x * r for x in parts], r


def unpack_norm(w_ref):
    hw = w_ref.shape[0] - 16
    row = w_ref[hw:, :].astype(F32)[0:1, :]
    gain, bias, gain_low, bias_low = (row[:, i * hw : (i + 1) * hw] for i in range(4))
    return gain + gain_low, bias + bias_low


def outproj_kernel(idx, on_ref, tok_ref, *refs):
    g = (len(refs) - 2) // 2
    o_refs, w_refs = refs[:g], refs[g : 2 * g]
    h_ref, c_ref = refs[2 * g :]
    hats, _ = wide_norm(o_refs)
    acc = tok_ref[...].astype(F32)
    for k in range(g):
        gain, bias = unpack_norm(w_refs[k])
        y = (hats[k] * gain + bias).astype(BF)
        acc = acc + dot(y, w_refs[k][: gain.shape[1], :])
    h_ref[...] = acc
    hat, _ = normalize(acc)
    c_ref[...] = (hat * on_ref[2:3, :] + on_ref[3:4, :]).astype(BF)


def outproj(on, tok, o, w, idx, after=()):
    rows, d = tok.shape
    hw = o[0].shape[1]
    blk = lambda n: pl.BlockSpec((WIDE, n), lambda s, i: (s, 0))
    return run(
        outproj_kernel,
        (rows // WIDE,),
        [on, tok, *o, *w],
        fulls([on]) + [blk(d)] + [blk(hw)] * len(o) + fulls(w),
        [far((rows, d), F32), near((rows, d), BF)],
        [blk(d), blk(d)],
        idx,
        "outproj",
        0,
        after=after,
        hbm=(1,),
    )


def ffn_up_kernel(idx, c_ref, e_ref, fn_ref, *refs):
    ups, downs = refs[:2], refs[2:4]
    z_ref, slope_ref, dw_ref, st_ref, wu_ref, wd_ref = refs[4:]
    rows = ups[0].shape[1]

    @pl.when(pl.program_id(0) == 0)
    def _():
        for i, k in enumerate(ORDER):
            for odd in range(2):
                j = jnp.bitwise_xor(idx[0], k + odd)
                at = pl.ds(pl.multiple_of(j * rows, rows), rows)
                wu_ref[at, :] = ups[odd][i]
                wd_ref[at, :] = downs[i // 2][i % 2 * 2 + odd]

    u = dot(c_ref[...], wu_ref[...])
    z, t = gelu_parts(u)
    z_ref[...] = z
    slope_ref[...] = 0.5 * (1.0 + t) + 0.5 * u * (1.0 - t * t) * (GELU_A * (1.0 + (3.0 * GELU_B) * (u * u)))
    mean = rowsum(z) / z.shape[-1]
    z = z - mean
    dw = dot_nt(e_ref[...], wd_ref[...])
    dw_ref[...] = dw
    eg = dw * fn_ref[0:1, :]
    stats = [mean, rowsum(z * z), rowsum(eg), rowsum(eg * z)]
    place = lax.broadcasted_iota(jnp.int32, (WIDE, 128), 1)
    tile = jnp.zeros((WIDE, 128), F32)
    for i, x in enumerate(stats):
        tile = jnp.where(place == i, x, tile)
    st_ref[...] = tile.T[:8, :]


def ffn_up(c, e, fn, pieces, idx):
    rows, d = c.shape
    fl = fn.shape[1]
    rblk = lambda n: pl.BlockSpec((WIDE, n), lambda s, i: (s, 0))
    return run(
        ffn_up_kernel,
        (rows // WIDE,),
        [c, e, fn, *pieces],
        [rblk(d), rblk(d), full(fn.shape)] + fulls(pieces),
        [near((rows, fl), F32)] * 3 + [sds((8, rows), F32), near((d, fl), BF), far((fl, d), BF)],
        [rblk(fl)] * 3 + [pl.BlockSpec((8, WIDE), lambda s, i: (0, s)), full((d, fl)), full((fl, d))],
        idx,
        "ffn_up",
        7.5,
        hbm=(1,),
    )


def rel_of(s):
    return jnp.where(s < 2, 2 * s + 1, 2 * s - 4)


def rel_block(s, i):
    return jnp.bitwise_xor(rel_of(s), i[1])


def rel_spec(n):
    return pl.BlockSpec((BLK, n), lambda s, i: (rel_block(s, i), 0))


SEND_SPEC = lambda n: pl.BlockSpec((1, BLK, n), lambda s, i: (jnp.minimum(s, 1), 0, 0))
KEEP_SPEC = lambda n: full((BLK, n))


def put_rel(send_ref, keep_ref, last_ref, value):
    @pl.when(pl.program_id(0) < 2)
    def _():
        send_ref[0] = value.astype(BF)

    @pl.when(pl.program_id(0) == 2)
    def _():
        keep_ref[...] = value

    @pl.when(pl.program_id(0) == 3)
    def _():
        last_ref[...] = value


def ffn_mid_kernel(idx, z_ref, slope_ref, dw_ref, st_ref, fn_ref, wu_ref, w_ref, du_ref, send_ref, keep_ref, last_ref, fg_ref):
    g = st_ref.shape[0]
    fl = z_ref.shape[1]
    n = g * fl
    st = [st_ref[k] for k in range(g)]
    mean = sum(x[0:1] for x in st) / g
    gap = [x[0:1] - mean for x in st]
    spread = sum(x[1:2] + fl * (gp * gp) for x, gp in zip(st, gap)) / n
    r = lax.rsqrt(spread + EPS)
    s_plain = sum(x[2:3] for x in st) / n
    s_norm = r * (sum(x[3:4] + gp * x[2:3] for x, gp in zip(st, gap)) / n)
    cols = jnp.concatenate([mean, r, s_plain, s_norm, jnp.zeros((124, BLK), F32)], axis=0).T
    mean, r, s_plain, s_norm = (cols[:, i : i + 1] for i in range(4))
    hat = (z_ref[...] - mean) * r
    w_ref[...] = (hat * fn_ref[0:1, :] + fn_ref[1:2, :]).astype(BF)
    dw = dw_ref[...]
    dz = r * (dw * fn_ref[0:1, :] - s_plain - hat * s_norm)
    du = (dz * slope_ref[...]).astype(BF)
    du_ref[...] = du
    put_rel(send_ref, keep_ref, last_ref, dot_nt(du, wu_ref[...]))
    grads = jnp.concatenate([jnp.sum(dw * hat, 0, keepdims=True), jnp.sum(dw, 0, keepdims=True)], axis=0)

    @pl.when(pl.program_id(0) == 0)
    def _():
        fg_ref[...] = grads

    @pl.when(pl.program_id(0) > 0)
    def _():
        fg_ref[...] += grads


def ffn_mid(z, slope, dw, st, fn, wu, idx):
    rows, fl = z.shape
    d = wu.shape[0]
    return run(
        ffn_mid_kernel,
        (rows // BLK,),
        [z, slope, dw, st, fn, wu],
        [rel_spec(fl)] * 3 + [pl.BlockSpec((st.shape[0], 8, BLK), lambda s, i: (0, 0, rel_block(s, i)))]
        + fulls([fn, wu]),
        [far((rows, fl), BF), far((rows, fl), BF), sds((2, BLK, d), BF), far((BLK, d), F32), sds((BLK, d), F32), sds((2, fl), F32)],
        [rel_spec(fl), rel_spec(fl), SEND_SPEC(d), KEEP_SPEC(d), KEEP_SPEC(d), full((2, fl))],
        idx,
        "ffn_mid",
        6.5,
    )


def ffn_out(x, w, idx, after):
    rows, depth = x.shape
    d = w.shape[1]

    def kernel(idx, x_ref, w_ref, send_ref, keep_ref, last_ref):
        put_rel(send_ref, keep_ref, last_ref, dot(x_ref[...], w_ref[...]))

    return run(
        kernel,
        (rows // BLK,),
        [x, w],
        [rel_spec(depth), full(w.shape)],
        [sds((2, BLK, d), BF), far((BLK, d), F32), sds((BLK, d), F32)],
        [SEND_SPEC(d), KEEP_SPEC(d), KEEP_SPEC(d)],
        idx,
        "ffn_out",
        0,
        (),
        after,
        (0, 1),
    )


def put_blocks(scr, send_ref, keep_ref, first, step):
    for i, k in enumerate(ORDER):
        for odd, dest in enumerate((keep_ref, send_ref)):
            j = jnp.bitwise_xor(first, k + odd)
            value = scr[pl.ds(pl.multiple_of(j * step, step), step), :]
            dest[i, :, : value.shape[1]] = value.astype(dest.dtype)


def weight_grad(x, y, idx, name, after=()):
    rows, d = x.shape
    n = y.shape[1]
    step = d // WAYS
    steps = d // BLK

    def kernel(idx, x_ref, y_ref, send_ref, keep_ref, scr):
        s = pl.program_id(0)
        scr[pl.ds(pl.multiple_of(s * BLK, BLK), BLK), :] = dot_tn(x_ref[...], y_ref[...])

        @pl.when(s == steps - 1)
        def _():
            put_blocks(scr, send_ref, keep_ref, idx[0], step)

    return run(
        kernel,
        (steps,),
        [x, y],
        [pl.BlockSpec((rows, BLK), lambda s, i: (0, s)), full(y.shape)],
        [sds((WAYS // 2, step, n), BF), far((WAYS // 2, step, n), BF)],
        [full((WAYS // 2, step, n))] * 2,
        idx,
        name,
        3.5,
        [pltpu.VMEM((d, n), F32)],
        after,
    )


def qkv_back(a, dqkv, wq, go, idx, after=()):
    rows, d = a.shape
    n = dqkv.shape[1]
    step = d // WAYS
    hw = go[2].shape[0]
    groups = d // hw
    orows = hw // WAYS

    def kernel(idx, a_ref, d_ref, w_ref, go0_ref, go1_ref, go2_ref, gs_ref, gk_ref, send_ref, keep_ref, last_ref, scr, go_ref):
        go_ref[...] = go0_ref[...] + go1_ref[0].astype(F32) + go2_ref[...].astype(F32)
        for s in range(d // BLK):
            scr[s * BLK : (s + 1) * BLK, :] = dot_tn(a_ref[:, s * BLK : (s + 1) * BLK], d_ref[...])
        put_blocks(scr, gs_ref, gk_ref, idx[0], step)
        for i, k in enumerate(ORDER):
            for odd, dest in enumerate((gk_ref, gs_ref)):
                j = jnp.bitwise_xor(idx[0], k + odd)
                tail = pack_rows(go_ref[pl.ds(pl.multiple_of(j * orows, orows), orows), :], groups)
                dest[i, :, n:] = tail.astype(dest.dtype)
        for k in range(4):
            j = jnp.bitwise_xor(idx[1], k)
            value = dot_nt(d_ref[pl.ds(pl.multiple_of(j * BLK, BLK), BLK), :], w_ref[...])
            if k % 2:
                send_ref[k // 2] = value.astype(BF)
            else:
                (last_ref if k else keep_ref)[...] = value

    ins = [a, dqkv, wq, *go]
    lead = pl.BlockSpec((1, hw, d), lambda s, i: (0, 0, 0))
    half = (WAYS // 2, step, d)
    part = (2, BLK, d)
    outs = [sds(half, BF), far(half, BF), sds(part, BF), far(part[1:], F32), sds(part[1:], F32)]
    return run(
        kernel, (1,), ins, fulls(ins[:4]) + [lead, full(go[2].shape)], outs, fulls(outs), idx, "qkv_back", 40,
        [pltpu.VMEM((d, n), F32), pltpu.VMEM((hw, d), F32)],
        after=after,
        hbm=(0, 2, 3),
    )


def shard_back_kernel(idx, dc0_ref, dc1_ref, dc2_ref, h_ref, e_ref, on_ref, *refs):
    g = 4
    o_refs, w_refs = refs[:g], refs[g : 2 * g]
    dh_ref, ol_ref, ag_ref, *do_refs = refs[2 * g :]
    do_refs, (gs_ref, gk_ref, gl_ref) = do_refs[:g], do_refs[g:]
    dc = dc0_ref[...] + dc1_ref[0].astype(F32) + dc2_ref[...].astype(F32)
    hat, r = normalize(h_ref[...])
    wgt = dc * on_ref[2:3, :]
    n = dc.shape[-1]
    dh = e_ref[...].astype(F32) + r * (wgt - rowsum(wgt) / n - hat * (rowsum(wgt * hat) / n))
    dh_ref[...] = dh
    ol_ref[...] = jnp.concatenate([jnp.sum(dc * hat, 0, keepdims=True), jnp.sum(dc, 0, keepdims=True)], axis=0)
    dhb = dh.astype(BF)
    hats, r = wide_norm(o_refs)
    norms = [unpack_norm(w_refs[k]) for k in range(g)]
    dys = [dot_nt(dhb, w_refs[k][: norms[k][0].shape[1], :]) for k in range(g)]
    wgts = [dys[k] * norms[k][0] for k in range(g)]
    s_plain = sum(rowsum(x) for x in wgts) / n
    s_norm = sum(rowsum(x * y) for x, y in zip(wgts, hats)) / n
    for k in range(g):
        do_refs[k][...] = (r * (wgts[k] - s_plain - hats[k] * s_norm)).astype(BF)
        ag_ref[jnp.bitwise_xor(idx[1], k)] = jnp.concatenate(
            [jnp.sum(dys[k] * hats[k], 0, keepdims=True), jnp.sum(dys[k], 0, keepdims=True)], axis=0
        )
    for k in range(g):
        y = (hats[k] * norms[k][0] + norms[k][1]).astype(BF)
        value = dot_tn(y, dhb)
        if k % 2:
            gs_ref[k // 2] = value.astype(BF)
        else:
            (gl_ref if k else gk_ref)[...] = value


def shard_back(dc_keep, dc_one, dc_two, h, e, on, o, w, idx, after):
    rows, d = h.shape
    g = len(o)
    hw = o[0].shape[1]
    mine = lambda n: pl.BlockSpec((BLK, n), lambda s, i: (i[1], 0))
    lead = pl.BlockSpec((1, BLK, d), lambda s, i: (0, 0, 0))
    ins = [dc_keep, dc_one, dc_two, h, e, on, *o, *w]
    return run(
        shard_back_kernel,
        (1,),
        ins,
        [full((BLK, d)), lead, full((BLK, d)), mine(d), mine(d)] + fulls([on]) + [mine(hw)] * g + fulls(w),
        [far((BLK, d), F32), sds((2, d), F32), sds((g, 2, hw), F32)]
        + [sds((BLK, hw), BF)] * g
        + [sds((2, hw, d), BF), far((hw, d), F32), sds((hw, d), F32)],
        [full((BLK, d)), full((2, d)), full((g, 2, hw))]
        + [full((BLK, hw))] * g
        + [full((2, hw, d)), full((hw, d)), full((hw, d))],
        idx,
        "shard_back",
        0,
        after=after,
        hbm=(0, 3, 4) + tuple(range(6, 6 + 2 * g)),
    )


def attend_back_kernel(idx, q_ref, k_ref, v_ref, *refs):
    h = pl.program_id(0)
    rows, hw = q_ref.shape
    count = rows // BLK
    p_refs, d_refs = refs[:count], refs[count : count + 4]
    out_ref, do_scr, dq_scr, dk_scr, dv_scr = refs[count + 4 :]

    @pl.when(h == 0)
    def _():
        for k in range(4):
            j = jnp.bitwise_xor(idx[1], k)
            do_scr[pl.ds(pl.multiple_of(j * BLK, BLK), BLK), :] = d_refs[k][...]
        dk_scr[...] = jnp.zeros_like(dk_scr)
        dv_scr[...] = jnp.zeros_like(dv_scr)
        dq_scr[...] = jnp.zeros_like(dq_scr)

    lane = (lax.broadcasted_iota(jnp.int32, (1, hw), 1) // HD) == h
    for i in range(rows // BLK):
        lo, hi = i * BLK, (i + 1) * BLK
        dob = jnp.where(lane, do_scr[lo:hi, :], BF(0))
        qb = jnp.where(lane, q_ref[lo:hi, :], BF(0))
        pb = p_refs[i][0]
        p = pb.astype(F32)
        dp = dot_nt(dob, v_ref[:hi, :])
        ds = (p * (dp - rowsum(p * dp))).astype(BF)
        dq_scr[lo:hi, :] = jnp.where(lane, dot(ds, k_ref[:hi, :]), dq_scr[lo:hi, :])
        dk_scr[:hi, :] += dot_tn(ds, qb)
        dv_scr[:hi, :] += dot_tn(pb, dob)

    @pl.when(h == pl.num_programs(0) - 1)
    def _():
        out_ref[...] = jnp.concatenate([dq_scr[...] * HD ** (-0.5), dk_scr[...], dv_scr[...]], axis=1).astype(BF)


def attend_back(q, k, v, p, do, idx, after):
    rows, hw = q.shape
    heads = hw // HD
    return run(
        attend_back_kernel,
        (heads,),
        [q, k, v, *p, *do],
        fulls([q, k, v]) + [head_spec(w) for w in widths(rows)] + fulls(do),
        [sds((rows, 3 * hw), BF)],
        [full((rows, 3 * hw))],
        idx,
        "attend_back",
        11,
        [pltpu.VMEM((rows, hw), BF)] + [pltpu.VMEM((rows, hw), F32)] * 3,
        after=after,
        hbm=range(3 + len(p)),
    )[0]


def shard_end_kernel(idx, da0_ref, da1_ref, da2_ref, tok_ref, on_ref, dh_ref, gt_ref, oe_ref):
    da = da0_ref[...] + da1_ref[0].astype(F32) + da2_ref[...].astype(F32)
    hat, r = normalize(tok_ref[...].astype(F32))
    wgt = da * on_ref[0:1, :]
    n = da.shape[-1]
    grad = r * (wgt - rowsum(wgt) / n - hat * (rowsum(wgt * hat) / n))
    gt_ref[...] = (dh_ref[...] + grad).astype(BF)
    oe_ref[...] = jnp.concatenate([jnp.sum(da * hat, 0, keepdims=True), jnp.sum(da, 0, keepdims=True)], axis=0)


def shard_end(da_keep, da_one, da_two, tok, on, dh, idx, after=()):
    d = tok.shape[1]
    lead = pl.BlockSpec((1, BLK, d), lambda s, i: (0, 0, 0))
    return run(
        shard_end_kernel,
        (1,),
        [da_keep, da_one, da_two, tok, on, dh],
        [full((BLK, d)), lead, full((BLK, d)), pl.BlockSpec((BLK, d), lambda s, i: (i[1], 0)), full(on.shape), full((BLK, d))],
        [sds((BLK, d), BF), sds((2, d), F32)],
        [full((BLK, d)), full((2, d))],
        idx,
        "shard_end",
        0,
        after=after,
    )


def spread_rows(parts, idx, name, after=()):
    rows, d = parts[0].shape

    def kernel(idx, *refs):
        for k, part in enumerate(refs[:-2]):
            at = pl.ds(pl.multiple_of(jnp.bitwise_xor(idx[1], k) * rows, rows), rows)
            refs[-2][at, :] = part[...]
        refs[-1][...] = jnp.zeros(refs[-1].shape, F32)

    outs = [sds((rows * len(parts), d), BF), sds((8, 128), F32)]
    return run(kernel, (1,), parts, fulls(parts), outs, fulls(outs), idx, name, 0, (), after)


def far_sum(last, got, idx, after=(), tick=TICK):
    rows, d = last.shape

    def kernel(idx, last_ref, got_ref, out_ref):
        out_ref[...] = (last_ref[...] + got_ref[0].astype(F32)).astype(BF)

    second = pl.BlockSpec((1, rows, d), lambda s, i: (1, 0, 0))
    out = [sds((rows, d), BF)]
    return run(kernel, (1,), [last, got], [full((rows, d)), second], out, fulls(out), idx, "far_sum", tick, (), after)[0]


def fold(keep, got, idx, after=(), tick=TICK):
    count, rows, d = keep.shape
    half = count // 2

    def kernel(idx, keep_ref, got_ref, stay_ref, send_ref):
        stay_ref[...] = keep_ref[:half].astype(F32) + got_ref[:half].astype(F32)
        send = (keep_ref[half:].astype(F32) + got_ref[half:].astype(F32)).astype(BF)
        send_ref[...] = send if half > 1 else send[0]

    outs = [sds((half, rows, d), F32), sds((half, rows, d) if half > 1 else (rows, d), BF)]
    return run(kernel, (1,), [keep, got], fulls([keep, got]), outs, fulls(outs), idx, "fold", tick, (), after, (0,) if half > 1 else ())


def close(own, got, idx, after=(), vec=None, tick=TICK):
    rows, d = got[0].shape

    def kernel(idx, own_ref, *refs):
        out_ref = refs[-1]
        total = own_ref[...].reshape(rows, d)
        for ref in refs[: len(got)]:
            total = total + ref[...].astype(F32)
        out_ref[:rows, :] = total.astype(BF)
        if vec is not None:
            x = refs[len(got)][...]
            high = x.astype(BF).astype(F32)
            out_ref[rows:, :] = jnp.concatenate([high, x - high], axis=0).astype(BF)

    ins = [own, *got] + ([] if vec is None else [vec])
    out = [sds((rows if vec is None else rows + 2 * vec.shape[0], d), BF)]
    return run(kernel, (1,), ins, fulls(ins), out, fulls(out), idx, "close", tick, (), after)[0]


def join(parts, idx, after=(), tick=2 * TICK):
    shapes = [x.shape if len(x.shape) == 3 else (1, *x.shape) for x in parts]

    def kernel(idx, *refs):
        at = 0
        for ref, shape in zip(refs, shapes):
            refs[-1][at : at + shape[0]] = ref[...].reshape(shape)
            at += shape[0]

    out = [sds((sum(x[0] for x in shapes), *shapes[0][1:]), BF)]
    return run(kernel, (1,), parts, fulls(parts), out, fulls(out), idx, "join", tick, (), after)[0]


def block_end(h, keep, got, last, idx, after=()):
    rows, d = last.shape

    def kernel(idx, h_ref, keep_ref, got_ref, last_ref, out_ref):
        total = h_ref[...] + keep_ref[...] + got_ref[0].astype(F32) + last_ref[...].astype(F32)
        out_ref[...] = total.astype(BF)

    lead = pl.BlockSpec((1, rows, d), lambda s, i: (0, 0, 0))
    mine = pl.BlockSpec((rows, d), lambda s, i: (i[1], 0))
    own = full((rows, d))
    ins = [h, keep, got, last]
    out = [sds((rows, d), BF)]
    return run(
        kernel, (1,), ins, [mine, own, lead, own], out, fulls(out), idx, "block_end", TICK, (), after, (0,)
    )[0]


def vec_add(x, y, idx, after=(), tick=TICK):
    def kernel(idx, x_ref, y_ref, out_ref):
        out_ref[...] = x_ref[...] + y_ref[...]

    out = [sds(x.shape, F32)]
    return run(kernel, (1,), [x, y], fulls([x, y]), out, fulls(out), idx, "vec_add", tick, (), after)[0]


def pack_weights(w, w2, groups, idx):
    rows, n = w.shape

    def kernel(idx, w_ref, w2_ref, out_ref):
        out_ref[:, :n] = w_ref[...].astype(BF)
        out_ref[:, n:] = pack_rows(w2_ref[...], groups).astype(BF)

    out = [sds((rows, n + w2.shape[1] // groups), BF)]
    return run(kernel, (1,), [w, w2], fulls([w, w2]), out, fulls(out), idx, "pack_weights", 1, hbm=(0, 1))[0]


def cast_pair(x, y, idx):
    def kernel(idx, x_ref, y_ref, x_out, y_out):
        x_out[...] = x_ref[...].astype(BF)
        y_out[...] = y_ref[...].astype(BF)

    outs = [sds(x.shape, BF), sds(y.shape, BF)]
    return run(kernel, (1,), [x, y], fulls([x, y]), outs, fulls(outs), idx, "cast_pair", 1, hbm=(0, 1))


def warm(arrays, idx, after=()):
    count = len(arrays)

    def kernel(idx, *refs):
        for x, y in zip(refs[:count], refs[count:]):
            y[...] = x[...]

    outs = [near(x.shape, x.dtype) for x in arrays]
    return run(kernel, (1,), arrays, fulls(arrays), outs, fulls(outs), idx, "warm", 0, (), after, range(count))


def one_hot(place, count, width):
    at = lax.broadcasted_iota(jnp.int32, (count, width), 1)
    want = place * count + lax.broadcasted_iota(jnp.int32, (count, width), 0)
    return jnp.where(at == want, 1.0, 0.0).astype(BF)


def precondition(idx, ins, outs, scr, total, flip):
    w_ref, l_ref, r_ref, lr_ref, rr_ref = ins
    g_ref, nl_ref, nr_ref, nw_ref, copy_ref = outs
    d, n = scr.shape
    rows, side = w_ref.shape[0], r_ref.shape[0]
    whole = scr[...]
    g_ref[...] = whole.T if flip else whole
    grad = whole.astype(BF)
    scale = 1.0 / total
    own_cols = dot_nt(one_hot(idx[2], side, n), grad).astype(BF)
    own_rows = dot(one_hot(idx[2], rows, d), grad).astype(BF)
    nr_ref[...] = DECAY * r_ref[...] + ((1.0 - DECAY) * scale * scale) * dot(own_cols, grad)
    nl_ref[...] = DECAY * l_ref[...] + ((1.0 - DECAY) * scale * scale) * dot_nt(own_rows, grad)
    part = dot(lr_ref[...].astype(BF), grad).astype(BF)
    new = w_ref[...] - (MAT_RATE * scale) * dot(part, rr_ref[...].astype(BF))
    nw_ref[...] = new
    copy_ref[...] = new.astype(BF)


def update_outs(mats):
    w, left, right = mats[:3]
    (rows, n), d, side = w.shape, left.shape[1], right.shape[0]
    flip = n % 128 != 0
    outs = [sds((n, d) if flip else (d, n), F32), sds((rows, d), F32), sds((side, n), F32)]
    return outs + [sds((rows, n), F32), sds((rows, n), BF)], flip, pltpu.VMEM((d, n), F32)


def update_one(mats, near_blocks, far_blocks, total, idx, name, after=(), tick=0):
    outs, flip, scr = update_outs(mats)
    step = mats[1].shape[1] // WAYS

    def kernel(idx, *refs):
        ins, (even, odd), rest = refs[:5], refs[5:7], refs[7:]
        for i, k in enumerate(ORDER):
            for far_one, blocks in enumerate((even, odd)):
                j = jnp.bitwise_xor(idx[0], k + far_one)
                rest[6][pl.ds(pl.multiple_of(j * step, step), step), :] = blocks[i].astype(F32)
        precondition(idx, ins, rest[:5], rest[6], total, flip)
        rest[5][...] = jnp.zeros(rest[5].shape, F32)

    ins = [*mats, near_blocks, far_blocks]
    outs = outs + [sds((8, 128), F32)]
    res = run(kernel, (1,), ins, fulls(ins), outs, fulls(outs), idx, name, tick, [scr], after, range(5))
    return [res[0].T if flip else res[0], *res[1:]]


def update_pair(mats, mats2, near_blocks, far_blocks, norms, rates, total, idx, name, after=()):
    outs, flip, scr = update_outs(mats)
    outs2, flip2, scr2 = update_outs(mats2)
    step, n = mats[1].shape[1] // WAYS, mats[0].shape[1]
    step2, n2 = mats2[1].shape[1] // WAYS, mats2[0].shape[1]
    half = (near_blocks.shape[1] - step) // 2
    wide = norms[1].shape[1]

    def kernel(idx, *refs):
        ins, ins2, (even, odd), norm_refs, rest = refs[:5], refs[5:10], refs[10:12], refs[12:15], refs[15:]
        sums = 0.0
        for i, k in enumerate(ORDER):
            for far_one, blocks in enumerate((even, odd)):
                j = jnp.bitwise_xor(idx[0], k + far_one)
                block = blocks[i].astype(F32)
                rest[-2][pl.ds(pl.multiple_of(j * step, step), step), :] = block[:step, :n]
                rest[-1][pl.ds(pl.multiple_of(j * step2, step2), step2), :] = unpack_rows(block[:step, n:], n2)
                sums = sums + (block[step : step + half] + block[step + half :])
        grads = [sums[:4], jnp.concatenate([sums[4:5, :wide], sums[4:5, wide : 2 * wide]], axis=0), sums[5:7]]
        for i, (grad, rate) in enumerate(zip(grads, (rates[0], rates[0], rates[1]))):
            rest[10 + i][...] = grad
            rest[13 + i][...] = norm_refs[i][...] - rate * grad
        precondition(idx, ins2, rest[5:10], rest[-1], total, flip2)
        precondition(idx, ins, rest[:5], rest[-2], total, flip)

    all_outs = outs + outs2 + [sds(x.shape, F32) for x in [*norms, *norms]]
    ins = [*mats, *mats2, near_blocks, far_blocks, *norms]
    res = run(kernel, (1,), ins, fulls(ins), all_outs, fulls(all_outs), idx, name, 6, [scr, scr2], after)
    res = list(res)
    res[0] = res[0].T if flip else res[0]
    res[5] = res[5].T if flip2 else res[5]
    return res[:5], res[5:10], res[10:]


def body(
    tokens,
    cotangent,
    doc_lengths,
    outer_norms,
    attn_norm,
    ffn_norm,
    w_qkv,
    left_qkv,
    right_qkv,
    left_root_qkv,
    right_root_qkv,
    w_out,
    left_out,
    right_out,
    left_root_out,
    right_root_out,
    w_up,
    left_up,
    right_up,
    left_root_up,
    right_root_up,
    w_down,
    left_down,
    right_down,
    left_root_down,
    right_root_down,
):
    row_count = tokens.shape[0]
    n_dp, n_mp = lax.axis_size("dp"), lax.axis_size("mp")
    fine = n_dp // WAYS
    total = row_count * n_dp
    dp_at, mp_at = lax.axis_index("dp"), lax.axis_index("mp")
    idx = jnp.stack([dp_at // fine, mp_at, dp_at]).astype(jnp.int32)
    hw = w_qkv.shape[2] // 3

    def swap(x, axis, size, k):
        return lax.ppermute(x, axis, [(i, i ^ k) for i in range(size)])

    def dp(x, k):
        return swap(x, "dp", n_dp, k * fine)

    def mp(x, k):
        return swap(x, "mp", n_mp, k)

    def fine_rows(x):
        k = 1
        while k < fine:
            got = swap(x, "dp", n_dp, k)
            x = jnp.where((dp_at & k) == 0, jnp.concatenate([x, got], 0), jnp.concatenate([got, x], 0))
            k *= 2
        return x

    def fine_sum(x):
        k = 1
        while k < fine:
            x = x + swap(x, "dp", n_dp, k)
            k *= 2
        return x

    def gather8(own, *early):
        parts = {0: own}
        for k in (2, 4, 6):
            parts[k] = dp(own, k)
        parts[1] = dp(own, 1)
        for k in (2, 4, 6):
            parts[k ^ 1] = dp(after(parts[k], *early) if early else parts[k], 1)
        return [parts[k] for k in range(WAYS)]

    def gather4(own):
        far = mp(own, 2)
        return [own, mp(own, 1), far, mp(far, 1)]

    def scatter4(send, keep):
        got = mp(send, 1)
        return keep, got, mp((keep[1] + got[1].astype(F32)).astype(BF), 2)

    def gather8_halves(own):
        two = jnp.stack([own, dp(own, 4)])
        four = jnp.concatenate([two, dp(two, 2)])
        return four, dp(four, 1)

    def after(x, *deps):
        return lax.optimization_barrier((x, *deps))[0]

    groups = tokens.shape[1] // hw
    if fine == 1:
        first = pack_weights(w_qkv[0], w_out[0], groups, idx)
    else:
        out_rows = fine_rows(w_out[0].astype(BF))
        first = jnp.concatenate([fine_rows(w_qkv[0].astype(BF)), pack_rows(out_rows, groups)], axis=1)
    up_own, down_own = (fine_rows(x) for x in cast_pair(w_up[0], w_down[0], idx))
    down_two = jnp.stack([down_own, dp(down_own, 1)])
    first = gather8(first, down_two)

    ends = jnp.cumsum(doc_lengths[0])
    places = jnp.arange(row_count, dtype=jnp.int32)
    start = jnp.max(jnp.where(ends[None, :] <= places[:, None], ends[None, :], 0), axis=1, keepdims=True)
    start = start.astype(jnp.int32)
    hat, _ = normalize(tokens.astype(F32))
    a_low = (hat * outer_norms[0] + outer_norms[1]).astype(BF)

    up_go = after(up_own, first[2], first[4], first[6], down_two)
    up_z = [dp(up_go, k) for k in ORDER[1:]]
    down_z2 = dp(after(down_two, up_go), 4)
    q, k, v, wq, wo = project(a_low, attn_norm, first, hw, idx)
    wo_far = mp(wo, 2)
    o, *probs = attend(start, q, k, v, idx)
    o, *up_z = lax.optimization_barrier((o, *up_z))
    o_far = mp(o, 2)
    up_four = jnp.stack([up_own, *lax.optimization_barrier((*up_z, down_z2))[:-1]])
    up_x = dp(up_four, 1)
    wo_near, wo_last = mp(after(wo, up_four), 1), mp(after(wo_far, up_four), 1)
    down_four = join([down_two, down_z2], idx, [up_four, wo_near, wo_last])
    down_z1 = dp(down_four, 2)
    o_near = mp(after(o, o_far), 1)
    o_all = [o, o_near, o_far, mp(o_far, 1)]
    wo_all = [wo, wo_near, wo_far, wo_last]
    hidden, c_low = outproj(outer_norms, tokens, o_all, wo_all, idx, [up_x])
    z, slope, dw, stats, wu, wd = ffn_up(c_low, cotangent, ffn_norm, [up_four, up_x, down_four, down_z1], idx)
    stats = lax.all_gather(stats, "mp")
    w_low, du, dc_send, dc_keep, dc_last, ffn_grads = ffn_mid(z, slope, dw, stats, ffn_norm, wu, idx)
    dc_got = mp(dc_send, 1)
    dc_sum = far_sum(dc_last, dc_got, idx)
    down_send, down_keep = weight_grad(w_low, cotangent, idx, "grad_down", [dc_sum])
    down_x = dp(down_send, 1)
    up_send, up_keep = weight_grad(c_low, du, idx, "grad_up", [down_send])
    up_x2 = dp(after(up_send, down_send), 1)
    dh, outer_late, attn_grads, *rest = shard_back(
        dc_keep, dc_got, mp(dc_sum, 2), hidden, cotangent, outer_norms, o_all, wo_all, idx, [up_send]
    )
    do, (go_send, go_keep, go_last) = rest[:n_mp], rest[n_mp:]
    do = [do[0]] + [mp(do[k], k) for k in range(1, n_mp)]
    go_got = mp(go_send, 1)
    bo_send, bo_keep, bo_last = ffn_out(w_low, wd, idx, [do[1]])
    down_t, down_low = fold(down_keep, down_x, idx, [bo_send], 0)
    go_sum = far_sum(go_last, go_got, idx, [down_low], 0)
    dqkv = attend_back(q, k, v, probs, do, idx, [go_sum])
    down_z1 = dp(down_low, 2)
    go_far = mp(go_sum, 2)
    bo_got = mp(after(bo_send, dqkv), 1)
    down_t, down_low = fold(down_t, down_z1, idx, [dqkv])
    up_t, up_low = fold(up_keep, up_x2, idx, [down_low])
    qkv_send, qkv_keep, da_send, da_keep, da_last = qkv_back(
        a_low, dqkv, wq, [go_keep, go_got, go_far], idx, [up_low]
    )

    down_z2, up_z1 = dp(down_low, 4), dp(up_low, 2)
    qkv_x = dp(qkv_send, 1)
    da_got = mp(da_send, 1)
    bo_sum = far_sum(bo_last, bo_got, idx, [qkv_send], 0)
    bo_far = mp(bo_sum, 2)
    da_sum = far_sum(da_last, da_got, idx, [bo_sum])
    da_far = mp(da_sum, 2)
    down_done = fine_sum(close(down_t, [down_z2], idx, [da_sum]))
    down_r4 = dp(down_done, 4)
    qkv_t, qkv_low = fold(qkv_keep, qkv_x, idx, [down_done], 0)
    qkv_z1 = dp(qkv_low, 2)
    up_t, up_low = fold(up_t, up_z1, idx, [qkv_low])
    up_z2 = dp(up_low, 4)
    down_two = join([down_done, down_r4], idx, [up_low])
    down_r2 = dp(down_two, 2)
    out_own = block_end(hidden, bo_keep, bo_got, bo_far, idx, [down_two])
    out_far = mp(out_own, 2)
    gt, outer_early = shard_end(da_keep, da_got, da_far, tokens, outer_norms, dh, idx, [out_own])
    gt_far = mp(gt, 2)
    lanes = outer_late.shape[1]
    vec = jnp.concatenate([outer_early, outer_late, attn_grads.reshape(-1, lanes)])
    vec_got = mp(vec, 1)
    up_done = fine_sum(close(up_t, [up_z2], idx, [gt]))
    up_r4 = dp(up_done, 4)
    qkv_t, qkv_low = fold(qkv_t, qkv_z1, idx, [up_done])
    qkv_z2 = dp(qkv_low, 4)
    vec = vec_add(vec, vec_got, idx, [qkv_low])
    vec_got = mp(vec, 2)
    down_four = join([down_two, down_r2], idx, [vec])
    down_other = dp(down_four, 1)
    up_two = join([up_done, up_r4], idx, [down_four, gt_far, out_far])
    up_r2 = dp(up_two, 2)
    vec = vec_add(vec, vec_got, idx, [up_two])
    attn_own = lax.dynamic_slice_in_dim(vec[4:].reshape(n_mp, -1), mp_at, 1, 0)
    attn_own = jnp.pad(attn_own, ((0, 0), (0, lanes - attn_own.shape[1])))
    vec = jnp.concatenate([vec[:4], attn_own, ffn_grads, jnp.zeros((1, lanes), F32)])
    vec = fine_sum(vec)
    qkv_own = close(qkv_t, [qkv_z2], idx, [up_two], None if fine > 1 else vec)
    if fine > 1:
        high = vec.astype(BF)
        qkv_own = jnp.concatenate([fine_sum(qkv_own), high, (vec - high.astype(F32)).astype(BF)])
    qkv_z = [dp(qkv_own, k) for k in ORDER[1:]]
    up_four = join([up_two, up_r2], idx, [qkv_own])
    up_other = dp(up_four, 1)
    down_mats = [x[0] for x in (w_down, left_down, right_down, left_root_down, right_root_down)]
    *down_res, token = update_one(down_mats, down_four, down_other, total, idx, "update_down", [up_four])
    qkv_four = join([qkv_own, *qkv_z], idx, [token], 10)
    qkv_other = dp(qkv_four, 1)

    def mats(*arrays):
        return [x[0] for x in arrays]

    ready = warm(
        mats(w_qkv, left_qkv, right_qkv, left_root_qkv, right_root_qkv)
        + mats(w_out, left_out, right_out, left_root_out, right_root_out),
        idx,
        [qkv_four],
    )
    up_mats = mats(w_up, left_up, right_up, left_root_up, right_root_up)
    *up_res, token = update_one(up_mats, up_four, up_other, total, idx, "update_up", [ready[0]], 0)
    gt_far, out_far = after(gt_far, token), after(out_far, token)
    gt_all = [gt, mp(after(gt, gt_far), 1), gt_far, mp(gt_far, 1)]
    grad_tokens, token = spread_rows(gt_all, idx, "spread_tokens", [token])
    out_all = [out_own, mp(after(out_own, out_far), 1), out_far, mp(out_far, 1)]
    block_out, token = spread_rows(out_all, idx, "spread_out", [token])
    qkv_res, out_res, vecs = update_pair(
        ready[:5],
        ready[5:],
        qkv_four,
        qkv_other,
        [outer_norms, attn_norm, ffn_norm],
        (VEC_RATE / math.sqrt(total), UNIT_RATE / math.sqrt(total)),
        total,
        idx,
        "update_qkv",
        [token],
    )

    return (
        block_out,
        grad_tokens,
        *vecs,
        *(x[None] for x in qkv_res),
        *(x[None] for x in out_res),
        *(x[None] for x in up_res),
        *(x[None] for x in down_res),
    )


def solution(mesh):
    rows = P("dp", None)
    mats = (P("mp", "dp", None),) * 4 + (P("mp", None, None),)
    res = (P("mp", None, None),) + (P("mp", "dp", None),) * 4
    cols = P(None, "mp")
    return jax.shard_map(
        body,
        mesh=mesh,
        in_specs=(rows, rows, rows, P(), cols, cols) + mats * 4,
        out_specs=(rows, rows, P(), cols, cols, P(), cols, cols) + res * 4,
        check_vma=False,
    )
```

```python
import math

import jax
import jax.numpy as jnp
from jax import lax
from jax.experimental import pallas as pl
from jax.experimental.pallas import tpu as pltpu
from jax.sharding import PartitionSpec as P

HD = 64
EPS = 1e-05
DECAY = 0.5
MAT_RATE = 0.5
VEC_RATE = 0.05
UNIT_RATE = 0.3
GELU_A = math.sqrt(2.0 / math.pi)
GELU_B = 0.044715
BF = jnp.bfloat16
F32 = jnp.float32
VMEM = 22 * 1024 * 1024
WAYS = 8
RATE = 4e8
TICK = 5
BLK = 256
WIDE = 512
ORDER = (0, 4, 2, 6)


def full(shape):
    return pl.BlockSpec(shape, lambda *args: (0,) * len(shape))


def fulls(arrays):
    return [full(x.shape) for x in arrays]


def run(kernel, grid, ins, in_specs, outs, out_specs, idx, name, micros, scratch=(), after=(), hbm=()):
    count, kernel_in = len(ins), kernel
    ins = [pltpu.with_memory_space_constraint(x, pltpu.HBM) if i in hbm else x for i, x in enumerate(ins)]

    def kernel(idx, *refs):
        kernel_in(idx, *refs[:count], *refs[count + len(after) :])

    return pl.pallas_call(
        kernel,
        grid_spec=pltpu.PrefetchScalarGridSpec(
            num_scalar_prefetch=1,
            grid=grid,
            in_specs=list(in_specs) + [pl.BlockSpec(memory_space=pl.ANY)] * len(after),
            out_specs=out_specs,
            scratch_shapes=list(scratch),
        ),
        out_shape=outs,
        compiler_params=pltpu.CompilerParams(vmem_limit_bytes=VMEM),
        cost_estimate=pl.CostEstimate(flops=int(micros * RATE), bytes_accessed=1024, transcendentals=0),
        name=name,
    )(idx, *ins, *after)


def sds(shape, dtype):
    return jax.ShapeDtypeStruct(shape, dtype)


def near(shape, dtype):
    return pltpu.VMEM(shape, dtype)


def far(shape, dtype):
    return pltpu.HBM(shape, dtype)


def dot(x, y):
    return jnp.dot(x, y, preferred_element_type=F32)


def dot_nt(x, y):
    return lax.dot_general(x, y, (((1,), (1,)), ((), ())), preferred_element_type=F32)


def dot_tn(x, y):
    return lax.dot_general(x, y, (((0,), (0,)), ((), ())), preferred_element_type=F32)


def rowsum(x):
    return jnp.sum(x, -1, keepdims=True)


def normalize(x):
    n = x.shape[-1]
    off = x - rowsum(x) / n
    r = lax.rsqrt(rowsum(off * off) / n + EPS)
    return off * r, r


def gelu_parts(u):
    t = jnp.tanh(GELU_A * (u + GELU_B * (u * u * u)))
    return 0.5 * u * (1.0 + t), t


def unpack_rows(side, wide):
    groups = wide // side.shape[1]
    rows = side.shape[0] // groups
    return jnp.concatenate([side[i * rows : (i + 1) * rows] for i in range(groups)], axis=1)


def pack_rows(block, groups):
    n = block.shape[1] // groups
    return jnp.concatenate([block[:, i * n : (i + 1) * n] for i in range(groups)], axis=0)


def project_kernel(idx, a_ref, an_ref, *refs):
    pieces = refs[:WAYS]
    q_ref, k_ref, v_ref, wq_ref, wo_ref, scr = refs[WAYS:]
    rows = wq_ref.shape[0] // WAYS
    orows = scr.shape[0] // WAYS
    hw = q_ref.shape[1]

    @pl.when(pl.program_id(0) == 0)
    def _():
        for k in range(WAYS):
            j = jnp.bitwise_xor(idx[0], k)
            wq_ref[pl.ds(pl.multiple_of(j * rows, rows), rows), :] = pieces[k][:, : 3 * hw]
            tail = pieces[k][:, 3 * hw :].astype(F32)
            scr[pl.ds(pl.multiple_of(j * orows, orows), orows), :] = unpack_rows(tail, wo_ref.shape[1])
        wo_ref[:hw, :] = scr[...].astype(BF)
        norm = jnp.concatenate([an_ref[0:1, :], an_ref[1:2, :]], axis=1)
        high = norm.astype(BF).astype(F32)
        row = jnp.concatenate([high, norm - high], axis=1)
        pad = wo_ref.shape[0] - hw
        at = lax.broadcasted_iota(jnp.int32, (pad, row.shape[1]), 0)
        wo_ref[hw:, :] = jnp.where(at == 0, row, 0.0).astype(BF)

    res = dot(a_ref[...], wq_ref[...]).astype(BF)
    q_ref[...] = res[:, :hw] * BF(HD ** (-0.5))
    k_ref[...] = res[:, hw : 2 * hw]
    v_ref[...] = res[:, 2 * hw :]


def project(a, norm, pieces, hw, idx):
    rows, d = a.shape
    n = 3 * hw
    blk = lambda w: pl.BlockSpec((BLK, w), lambda s, i: (s, 0))
    return run(
        project_kernel,
        (rows // BLK,),
        [a, norm, *pieces],
        [blk(d), full(norm.shape)] + fulls(pieces),
        [far((rows, hw), BF)] * 3 + [far((d, n), BF), far((hw + 16, d), BF)],
        [blk(hw)] * 3 + [full((d, n)), full((hw + 16, d))],
        idx,
        "project",
        40,
        [pltpu.VMEM((hw, d), F32)],
    )


def attend_kernel(idx, start_ref, q_ref, k_ref, v_ref, o_ref, *p_refs):
    h = pl.program_id(0)
    rows, hw = q_ref.shape
    lane = (lax.broadcasted_iota(jnp.int32, (1, hw), 1) // HD) == h
    for i in range(rows // BLK):
        lo, hi = i * BLK, (i + 1) * BLK
        qb = jnp.where(lane, q_ref[lo:hi, :], BF(0))
        s = dot_nt(qb, k_ref[:hi, :])
        kpos = lax.broadcasted_iota(jnp.int32, (BLK, hi), 1)
        qpos = lo + lax.broadcasted_iota(jnp.int32, (BLK, hi), 0)
        s = jnp.where((kpos >= start_ref[lo:hi, :]) & (kpos <= qpos), s, -1e30)
        p = jnp.exp(s - jnp.max(s, -1, keepdims=True))
        p = (p * (1.0 / rowsum(p))).astype(BF)
        p_refs[i][0] = p
        ob = dot(p, v_ref[:hi, :]).astype(BF)
        o_ref[lo:hi, :] = jnp.where(lane, ob, o_ref[lo:hi, :])


def widths(rows):
    return range(BLK, rows + BLK, BLK)


def head_spec(width):
    return pl.BlockSpec((1, BLK, width), lambda s, i: (s, 0, 0))


def attend(start, q, k, v, idx, after=()):
    rows, hw = q.shape
    heads = hw // HD
    return run(
        attend_kernel,
        (heads,),
        [start, q, k, v],
        fulls([start, q, k, v]),
        [far((rows, hw), BF)] + [far((heads, BLK, w), BF) for w in widths(rows)],
        [full((rows, hw))] + [head_spec(w) for w in widths(rows)],
        idx,
        "attend",
        10,
        after=after,
        hbm=(1, 2, 3),
    )


def wide_norm(o_refs):
    parts = [x[...].astype(F32) for x in o_refs]
    n = sum(x.shape[-1] for x in parts)
    mean = sum(rowsum(x) for x in parts) / n
    parts = [x - mean for x in parts]
    r = lax.rsqrt(sum(rowsum(x * x) for x in parts) / n + EPS)
    return [x * r for x in parts], r


def unpack_norm(w_ref):
    hw = w_ref.shape[0] - 16
    row = w_ref[hw:, :].astype(F32)[0:1, :]
    gain, bias, gain_low, bias_low = (row[:, i * hw : (i + 1) * hw] for i in range(4))
    return gain + gain_low, bias + bias_low


def outproj_kernel(idx, on_ref, tok_ref, *refs):
    g = (len(refs) - 2) // 2
    o_refs, w_refs = refs[:g], refs[g : 2 * g]
    h_ref, c_ref = refs[2 * g :]
    hats, _ = wide_norm(o_refs)
    acc = tok_ref[...].astype(F32)
    for k in range(g):
        gain, bias = unpack_norm(w_refs[k])
        y = (hats[k] * gain + bias).astype(BF)
        acc = acc + dot(y, w_refs[k][: gain.shape[1], :])
    h_ref[...] = acc
    hat, _ = normalize(acc)
    c_ref[...] = (hat * on_ref[2:3, :] + on_ref[3:4, :]).astype(BF)


def outproj(on, tok, o, w, idx, after=()):
    rows, d = tok.shape
    hw = o[0].shape[1]
    blk = lambda n: pl.BlockSpec((WIDE, n), lambda s, i: (s, 0))
    return run(
        outproj_kernel,
        (rows // WIDE,),
        [on, tok, *o, *w],
        fulls([on]) + [blk(d)] + [blk(hw)] * len(o) + fulls(w),
        [far((rows, d), F32), near((rows, d), BF)],
        [blk(d), blk(d)],
        idx,
        "outproj",
        0,
        after=after,
        hbm=(1,),
    )


def ffn_up_kernel(idx, c_ref, e_ref, fn_ref, *refs):
    ups, downs = refs[:2], refs[2:4]
    z_ref, slope_ref, dw_ref, st_ref, wu_ref, wd_ref = refs[4:]
    rows = ups[0].shape[1]

    @pl.when(pl.program_id(0) == 0)
    def _():
        for i, k in enumerate(ORDER):
            for odd in range(2):
                j = jnp.bitwise_xor(idx[0], k + odd)
                at = pl.ds(pl.multiple_of(j * rows, rows), rows)
                wu_ref[at, :] = ups[odd][i]
                wd_ref[at, :] = downs[i // 2][i % 2 * 2 + odd]

    u = dot(c_ref[...], wu_ref[...])
    z, t = gelu_parts(u)
    z_ref[...] = z
    slope_ref[...] = 0.5 * (1.0 + t) + 0.5 * u * (1.0 - t * t) * (GELU_A * (1.0 + (3.0 * GELU_B) * (u * u)))
    mean = rowsum(z) / z.shape[-1]
    z = z - mean
    dw = dot_nt(e_ref[...], wd_ref[...])
    dw_ref[...] = dw
    eg = dw * fn_ref[0:1, :]
    stats = [mean, rowsum(z * z), rowsum(eg), rowsum(eg * z)]
    place = lax.broadcasted_iota(jnp.int32, (WIDE, 128), 1)
    tile = jnp.zeros((WIDE, 128), F32)
    for i, x in enumerate(stats):
        tile = jnp.where(place == i, x, tile)
    st_ref[...] = tile.T[:8, :]


def ffn_up(c, e, fn, pieces, idx):
    rows, d = c.shape
    fl = fn.shape[1]
    rblk = lambda n: pl.BlockSpec((WIDE, n), lambda s, i: (s, 0))
    return run(
        ffn_up_kernel,
        (rows // WIDE,),
        [c, e, fn, *pieces],
        [rblk(d), rblk(d), full(fn.shape)] + fulls(pieces),
        [near((rows, fl), F32)] * 3 + [sds((8, rows), F32), near((d, fl), BF), far((fl, d), BF)],
        [rblk(fl)] * 3 + [pl.BlockSpec((8, WIDE), lambda s, i: (0, s)), full((d, fl)), full((fl, d))],
        idx,
        "ffn_up",
        7.5,
        hbm=(1,),
    )


def rel_of(s):
    return jnp.where(s < 2, 2 * s + 1, 2 * s - 4)


def rel_block(s, i):
    return jnp.bitwise_xor(rel_of(s), i[1])


def rel_spec(n):
    return pl.BlockSpec((BLK, n), lambda s, i: (rel_block(s, i), 0))


SEND_SPEC = lambda n: pl.BlockSpec((1, BLK, n), lambda s, i: (jnp.minimum(s, 1), 0, 0))
KEEP_SPEC = lambda n: full((BLK, n))


def put_rel(send_ref, keep_ref, last_ref, value):
    @pl.when(pl.program_id(0) < 2)
    def _():
        send_ref[0] = value.astype(BF)

    @pl.when(pl.program_id(0) == 2)
    def _():
        keep_ref[...] = value

    @pl.when(pl.program_id(0) == 3)
    def _():
        last_ref[...] = value


def ffn_mid_kernel(idx, z_ref, slope_ref, dw_ref, st_ref, fn_ref, wu_ref, w_ref, du_ref, send_ref, keep_ref, last_ref, fg_ref):
    g = st_ref.shape[0]
    fl = z_ref.shape[1]
    n = g * fl
    st = [st_ref[k] for k in range(g)]
    mean = sum(x[0:1] for x in st) / g
    gap = [x[0:1] - mean for x in st]
    spread = sum(x[1:2] + fl * (gp * gp) for x, gp in zip(st, gap)) / n
    r = lax.rsqrt(spread + EPS)
    s_plain = sum(x[2:3] for x in st) / n
    s_norm = r * (sum(x[3:4] + gp * x[2:3] for x, gp in zip(st, gap)) / n)
    cols = jnp.concatenate([mean, r, s_plain, s_norm, jnp.zeros((124, BLK), F32)], axis=0).T
    mean, r, s_plain, s_norm = (cols[:, i : i + 1] for i in range(4))
    hat = (z_ref[...] - mean) * r
    w_ref[...] = (hat * fn_ref[0:1, :] + fn_ref[1:2, :]).astype(BF)
    dw = dw_ref[...]
    dz = r * (dw * fn_ref[0:1, :] - s_plain - hat * s_norm)
    du = (dz * slope_ref[...]).astype(BF)
    du_ref[...] = du
    put_rel(send_ref, keep_ref, last_ref, dot_nt(du, wu_ref[...]))
    grads = jnp.concatenate([jnp.sum(dw * hat, 0, keepdims=True), jnp.sum(dw, 0, keepdims=True)], axis=0)

    @pl.when(pl.program_id(0) == 0)
    def _():
        fg_ref[...] = grads

    @pl.when(pl.program_id(0) > 0)
    def _():
        fg_ref[...] += grads


def ffn_mid(z, slope, dw, st, fn, wu, idx):
    rows, fl = z.shape
    d = wu.shape[0]
    return run(
        ffn_mid_kernel,
        (rows // BLK,),
        [z, slope, dw, st, fn, wu],
        [rel_spec(fl)] * 3 + [pl.BlockSpec((st.shape[0], 8, BLK), lambda s, i: (0, 0, rel_block(s, i)))]
        + fulls([fn, wu]),
        [far((rows, fl), BF), far((rows, fl), BF), sds((2, BLK, d), BF), far((BLK, d), F32), sds((BLK, d), F32), sds((2, fl), F32)],
        [rel_spec(fl), rel_spec(fl), SEND_SPEC(d), KEEP_SPEC(d), KEEP_SPEC(d), full((2, fl))],
        idx,
        "ffn_mid",
        6.5,
    )


def ffn_out(x, w, idx, after):
    rows, depth = x.shape
    d = w.shape[1]

    def kernel(idx, x_ref, w_ref, send_ref, keep_ref, last_ref):
        put_rel(send_ref, keep_ref, last_ref, dot(x_ref[...], w_ref[...]))

    return run(
        kernel,
        (rows // BLK,),
        [x, w],
        [rel_spec(depth), full(w.shape)],
        [sds((2, BLK, d), BF), far((BLK, d), F32), sds((BLK, d), F32)],
        [SEND_SPEC(d), KEEP_SPEC(d), KEEP_SPEC(d)],
        idx,
        "ffn_out",
        0,
        (),
        after,
        (0, 1),
    )


def put_blocks(scr, send_ref, keep_ref, first, step):
    for i, k in enumerate(ORDER):
        for odd, dest in enumerate((keep_ref, send_ref)):
            j = jnp.bitwise_xor(first, k + odd)
            value = scr[pl.ds(pl.multiple_of(j * step, step), step), :]
            dest[i, :, : value.shape[1]] = value.astype(dest.dtype)


def weight_grad(x, y, idx, name, after=()):
    rows, d = x.shape
    n = y.shape[1]
    step = d // WAYS
    steps = d // BLK

    def kernel(idx, x_ref, y_ref, send_ref, keep_ref, scr):
        s = pl.program_id(0)
        scr[pl.ds(pl.multiple_of(s * BLK, BLK), BLK), :] = dot_tn(x_ref[...], y_ref[...])

        @pl.when(s == steps - 1)
        def _():
            put_blocks(scr, send_ref, keep_ref, idx[0], step)

    return run(
        kernel,
        (steps,),
        [x, y],
        [pl.BlockSpec((rows, BLK), lambda s, i: (0, s)), full(y.shape)],
        [sds((WAYS // 2, step, n), BF), far((WAYS // 2, step, n), BF)],
        [full((WAYS // 2, step, n))] * 2,
        idx,
        name,
        3.5,
        [pltpu.VMEM((d, n), F32)],
        after,
    )


def qkv_back(a, dqkv, wq, go, idx, after=()):
    rows, d = a.shape
    n = dqkv.shape[1]
    step = d // WAYS
    hw = go[2].shape[0]
    groups = d // hw
    orows = hw // WAYS

    def kernel(idx, a_ref, d_ref, w_ref, go0_ref, go1_ref, go2_ref, gs_ref, gk_ref, send_ref, keep_ref, last_ref, scr, go_ref):
        go_ref[...] = go0_ref[...] + go1_ref[0].astype(F32) + go2_ref[...].astype(F32)
        for s in range(d // BLK):
            scr[s * BLK : (s + 1) * BLK, :] = dot_tn(a_ref[:, s * BLK : (s + 1) * BLK], d_ref[...])
        put_blocks(scr, gs_ref, gk_ref, idx[0], step)
        for i, k in enumerate(ORDER):
            for odd, dest in enumerate((gk_ref, gs_ref)):
                j = jnp.bitwise_xor(idx[0], k + odd)
                tail = pack_rows(go_ref[pl.ds(pl.multiple_of(j * orows, orows), orows), :], groups)
                dest[i, :, n:] = tail.astype(dest.dtype)
        for k in range(4):
            j = jnp.bitwise_xor(idx[1], k)
            value = dot_nt(d_ref[pl.ds(pl.multiple_of(j * BLK, BLK), BLK), :], w_ref[...])
            if k % 2:
                send_ref[k // 2] = value.astype(BF)
            else:
                (last_ref if k else keep_ref)[...] = value

    ins = [a, dqkv, wq, *go]
    lead = pl.BlockSpec((1, hw, d), lambda s, i: (0, 0, 0))
    half = (WAYS // 2, step, d)
    part = (2, BLK, d)
    outs = [sds(half, BF), far(half, BF), sds(part, BF), far(part[1:], F32), sds(part[1:], F32)]
    return run(
        kernel, (1,), ins, fulls(ins[:4]) + [lead, full(go[2].shape)], outs, fulls(outs), idx, "qkv_back", 40,
        [pltpu.VMEM((d, n), F32), pltpu.VMEM((hw, d), F32)],
        after=after,
        hbm=(0, 2, 3),
    )


def shard_back_kernel(idx, dc0_ref, dc1_ref, dc2_ref, h_ref, e_ref, on_ref, *refs):
    g = 4
    o_refs, w_refs = refs[:g], refs[g : 2 * g]
    dh_ref, ol_ref, ag_ref, *do_refs = refs[2 * g :]
    do_refs, (gs_ref, gk_ref, gl_ref) = do_refs[:g], do_refs[g:]
    dc = dc0_ref[...] + dc1_ref[0].astype(F32) + dc2_ref[...].astype(F32)
    hat, r = normalize(h_ref[...])
    wgt = dc * on_ref[2:3, :]
    n = dc.shape[-1]
    dh = e_ref[...].astype(F32) + r * (wgt - rowsum(wgt) / n - hat * (rowsum(wgt * hat) / n))
    dh_ref[...] = dh
    ol_ref[...] = jnp.concatenate([jnp.sum(dc * hat, 0, keepdims=True), jnp.sum(dc, 0, keepdims=True)], axis=0)
    dhb = dh.astype(BF)
    hats, r = wide_norm(o_refs)
    norms = [unpack_norm(w_refs[k]) for k in range(g)]
    dys = [dot_nt(dhb, w_refs[k][: norms[k][0].shape[1], :]) for k in range(g)]
    wgts = [dys[k] * norms[k][0] for k in range(g)]
    s_plain = sum(rowsum(x) for x in wgts) / n
    s_norm = sum(rowsum(x * y) for x, y in zip(wgts, hats)) / n
    for k in range(g):
        do_refs[k][...] = (r * (wgts[k] - s_plain - hats[k] * s_norm)).astype(BF)
        ag_ref[jnp.bitwise_xor(idx[1], k)] = jnp.concatenate(
            [jnp.sum(dys[k] * hats[k], 0, keepdims=True), jnp.sum(dys[k], 0, keepdims=True)], axis=0
        )
    for k in range(g):
        y = (hats[k] * norms[k][0] + norms[k][1]).astype(BF)
        value = dot_tn(y, dhb)
        if k % 2:
            gs_ref[k // 2] = value.astype(BF)
        else:
            (gl_ref if k else gk_ref)[...] = value


def shard_back(dc_keep, dc_one, dc_two, h, e, on, o, w, idx, after):
    rows, d = h.shape
    g = len(o)
    hw = o[0].shape[1]
    mine = lambda n: pl.BlockSpec((BLK, n), lambda s, i: (i[1], 0))
    lead = pl.BlockSpec((1, BLK, d), lambda s, i: (0, 0, 0))
    ins = [dc_keep, dc_one, dc_two, h, e, on, *o, *w]
    return run(
        shard_back_kernel,
        (1,),
        ins,
        [full((BLK, d)), lead, full((BLK, d)), mine(d), mine(d)] + fulls([on]) + [mine(hw)] * g + fulls(w),
        [far((BLK, d), F32), sds((2, d), F32), sds((g, 2, hw), F32)]
        + [sds((BLK, hw), BF)] * g
        + [sds((2, hw, d), BF), far((hw, d), F32), sds((hw, d), F32)],
        [full((BLK, d)), full((2, d)), full((g, 2, hw))]
        + [full((BLK, hw))] * g
        + [full((2, hw, d)), full((hw, d)), full((hw, d))],
        idx,
        "shard_back",
        0,
        after=after,
        hbm=(0, 3, 4) + tuple(range(6, 6 + 2 * g)),
    )


def attend_back_kernel(idx, q_ref, k_ref, v_ref, *refs):
    h = pl.program_id(0)
    rows, hw = q_ref.shape
    count = rows // BLK
    p_refs, d_refs = refs[:count], refs[count : count + 4]
    out_ref, do_scr, dq_scr, dk_scr, dv_scr = refs[count + 4 :]

    @pl.when(h == 0)
    def _():
        for k in range(4):
            j = jnp.bitwise_xor(idx[1], k)
            do_scr[pl.ds(pl.multiple_of(j * BLK, BLK), BLK), :] = d_refs[k][...]
        dk_scr[...] = jnp.zeros_like(dk_scr)
        dv_scr[...] = jnp.zeros_like(dv_scr)
        dq_scr[...] = jnp.zeros_like(dq_scr)

    lane = (lax.broadcasted_iota(jnp.int32, (1, hw), 1) // HD) == h
    for i in range(rows // BLK):
        lo, hi = i * BLK, (i + 1) * BLK
        dob = jnp.where(lane, do_scr[lo:hi, :], BF(0))
        qb = jnp.where(lane, q_ref[lo:hi, :], BF(0))
        pb = p_refs[i][0]
        p = pb.astype(F32)
        dp = dot_nt(dob, v_ref[:hi, :])
        ds = (p * (dp - rowsum(p * dp))).astype(BF)
        dq_scr[lo:hi, :] = jnp.where(lane, dot(ds, k_ref[:hi, :]), dq_scr[lo:hi, :])
        dk_scr[:hi, :] += dot_tn(ds, qb)
        dv_scr[:hi, :] += dot_tn(pb, dob)

    @pl.when(h == pl.num_programs(0) - 1)
    def _():
        out_ref[...] = jnp.concatenate([dq_scr[...] * HD ** (-0.5), dk_scr[...], dv_scr[...]], axis=1).astype(BF)


def attend_back(q, k, v, p, do, idx, after):
    rows, hw = q.shape
    heads = hw // HD
    return run(
        attend_back_kernel,
        (heads,),
        [q, k, v, *p, *do],
        fulls([q, k, v]) + [head_spec(w) for w in widths(rows)] + fulls(do),
        [sds((rows, 3 * hw), BF)],
        [full((rows, 3 * hw))],
        idx,
        "attend_back",
        11,
        [pltpu.VMEM((rows, hw), BF)] + [pltpu.VMEM((rows, hw), F32)] * 3,
        after=after,
        hbm=range(3 + len(p)),
    )[0]


def shard_end_kernel(idx, da0_ref, da1_ref, da2_ref, tok_ref, on_ref, dh_ref, gt_ref, oe_ref):
    da = da0_ref[...] + da1_ref[0].astype(F32) + da2_ref[...].astype(F32)
    hat, r = normalize(tok_ref[...].astype(F32))
    wgt = da * on_ref[0:1, :]
    n = da.shape[-1]
    grad = r * (wgt - rowsum(wgt) / n - hat * (rowsum(wgt * hat) / n))
    gt_ref[...] = (dh_ref[...] + grad).astype(BF)
    oe_ref[...] = jnp.concatenate([jnp.sum(da * hat, 0, keepdims=True), jnp.sum(da, 0, keepdims=True)], axis=0)


def shard_end(da_keep, da_one, da_two, tok, on, dh, idx, after=()):
    d = tok.shape[1]
    lead = pl.BlockSpec((1, BLK, d), lambda s, i: (0, 0, 0))
    return run(
        shard_end_kernel,
        (1,),
        [da_keep, da_one, da_two, tok, on, dh],
        [full((BLK, d)), lead, full((BLK, d)), pl.BlockSpec((BLK, d), lambda s, i: (i[1], 0)), full(on.shape), full((BLK, d))],
        [sds((BLK, d), BF), sds((2, d), F32)],
        [full((BLK, d)), full((2, d))],
        idx,
        "shard_end",
        0,
        after=after,
    )


def spread_rows(parts, idx, name, after=()):
    rows, d = parts[0].shape

    def kernel(idx, *refs):
        for k, part in enumerate(refs[:-2]):
            at = pl.ds(pl.multiple_of(jnp.bitwise_xor(idx[1], k) * rows, rows), rows)
            refs[-2][at, :] = part[...]
        refs[-1][...] = jnp.zeros(refs[-1].shape, F32)

    outs = [sds((rows * len(parts), d), BF), sds((8, 128), F32)]
    return run(kernel, (1,), parts, fulls(parts), outs, fulls(outs), idx, name, 0, (), after)


def far_sum(last, got, idx, after=(), tick=TICK):
    rows, d = last.shape

    def kernel(idx, last_ref, got_ref, out_ref):
        out_ref[...] = (last_ref[...] + got_ref[0].astype(F32)).astype(BF)

    second = pl.BlockSpec((1, rows, d), lambda s, i: (1, 0, 0))
    out = [sds((rows, d), BF)]
    return run(kernel, (1,), [last, got], [full((rows, d)), second], out, fulls(out), idx, "far_sum", tick, (), after)[0]


def fold(keep, got, idx, after=(), tick=TICK):
    count, rows, d = keep.shape
    half = count // 2

    def kernel(idx, keep_ref, got_ref, stay_ref, send_ref):
        stay_ref[...] = keep_ref[:half].astype(F32) + got_ref[:half].astype(F32)
        send = (keep_ref[half:].astype(F32) + got_ref[half:].astype(F32)).astype(BF)
        send_ref[...] = send if half > 1 else send[0]

    outs = [sds((half, rows, d), F32), sds((half, rows, d) if half > 1 else (rows, d), BF)]
    return run(kernel, (1,), [keep, got], fulls([keep, got]), outs, fulls(outs), idx, "fold", tick, (), after, (0,) if half > 1 else ())


def close(own, got, idx, after=(), vec=None, tick=TICK):
    rows, d = got[0].shape

    def kernel(idx, own_ref, *refs):
        out_ref = refs[-1]
        total = own_ref[...].reshape(rows, d)
        for ref in refs[: len(got)]:
            total = total + ref[...].astype(F32)
        out_ref[:rows, :] = total.astype(BF)
        if vec is not None:
            x = refs[len(got)][...]
            high = x.astype(BF).astype(F32)
            out_ref[rows:, :] = jnp.concatenate([high, x - high], axis=0).astype(BF)

    ins = [own, *got] + ([] if vec is None else [vec])
    out = [sds((rows if vec is None else rows + 2 * vec.shape[0], d), BF)]
    return run(kernel, (1,), ins, fulls(ins), out, fulls(out), idx, "close", tick, (), after)[0]


def join(parts, idx, after=(), tick=2 * TICK, hbm=()):
    shapes = [x.shape if len(x.shape) == 3 else (1, *x.shape) for x in parts]

    def kernel(idx, *refs):
        at = 0
        for ref, shape in zip(refs, shapes):
            refs[-1][at : at + shape[0]] = ref[...].reshape(shape)
            at += shape[0]

    out = [sds((sum(x[0] for x in shapes), *shapes[0][1:]), BF)]
    return run(kernel, (1,), parts, fulls(parts), out, fulls(out), idx, "join", tick, (), after, hbm)[0]


def block_end(h, keep, got, last, idx, after=()):
    rows, d = last.shape

    def kernel(idx, h_ref, keep_ref, got_ref, last_ref, out_ref):
        total = h_ref[...] + keep_ref[...] + got_ref[0].astype(F32) + last_ref[...].astype(F32)
        out_ref[...] = total.astype(BF)

    lead = pl.BlockSpec((1, rows, d), lambda s, i: (0, 0, 0))
    mine = pl.BlockSpec((rows, d), lambda s, i: (i[1], 0))
    own = full((rows, d))
    ins = [h, keep, got, last]
    out = [sds((rows, d), BF)]
    return run(
        kernel, (1,), ins, [mine, own, lead, own], out, fulls(out), idx, "block_end", TICK, (), after, (0,)
    )[0]


def vec_add(x, y, idx, after=(), tick=TICK):
    def kernel(idx, x_ref, y_ref, out_ref):
        out_ref[...] = x_ref[...] + y_ref[...]

    out = [sds(x.shape, F32)]
    return run(kernel, (1,), [x, y], fulls([x, y]), out, fulls(out), idx, "vec_add", tick, (), after)[0]


def pack_weights(w, w2, groups, idx):
    rows, n = w.shape

    def kernel(idx, w_ref, w2_ref, out_ref):
        out_ref[:, :n] = w_ref[...].astype(BF)
        out_ref[:, n:] = pack_rows(w2_ref[...], groups).astype(BF)

    out = [sds((rows, n + w2.shape[1] // groups), BF)]
    return run(kernel, (1,), [w, w2], fulls([w, w2]), out, fulls(out), idx, "pack_weights", 1, hbm=(0, 1))[0]


def cast_pair(x, y, idx):
    def kernel(idx, x_ref, y_ref, x_out, y_out):
        x_out[...] = x_ref[...].astype(BF)
        y_out[...] = y_ref[...].astype(BF)

    outs = [sds(x.shape, BF), sds(y.shape, BF)]
    return run(kernel, (1,), [x, y], fulls([x, y]), outs, fulls(outs), idx, "cast_pair", 1, hbm=(0, 1))


def warm(arrays, idx, after=()):
    count = len(arrays)

    def kernel(idx, *refs):
        for x, y in zip(refs[:count], refs[count:]):
            y[...] = x[...]

    outs = [near(x.shape, x.dtype) for x in arrays]
    return run(kernel, (1,), arrays, fulls(arrays), outs, fulls(outs), idx, "warm", 0, (), after, range(count))


def one_hot(place, count, width):
    at = lax.broadcasted_iota(jnp.int32, (count, width), 1)
    want = place * count + lax.broadcasted_iota(jnp.int32, (count, width), 0)
    return jnp.where(at == want, 1.0, 0.0).astype(BF)


def precondition(idx, ins, outs, scr, total, flip):
    w_ref, l_ref, r_ref, lr_ref, rr_ref = ins
    g_ref, nl_ref, nr_ref, nw_ref, copy_ref = outs
    d, n = scr.shape
    rows, side = w_ref.shape[0], r_ref.shape[0]
    whole = scr[...]
    g_ref[...] = whole.T if flip else whole
    grad = whole.astype(BF)
    scale = 1.0 / total
    own_cols = dot_nt(one_hot(idx[2], side, n), grad).astype(BF)
    own_rows = dot(one_hot(idx[2], rows, d), grad).astype(BF)
    nr_ref[...] = DECAY * r_ref[...] + ((1.0 - DECAY) * scale * scale) * dot(own_cols, grad)
    nl_ref[...] = DECAY * l_ref[...] + ((1.0 - DECAY) * scale * scale) * dot_nt(own_rows, grad)
    part = dot(lr_ref[...].astype(BF), grad).astype(BF)
    new = w_ref[...] - (MAT_RATE * scale) * dot(part, rr_ref[...].astype(BF))
    nw_ref[...] = new
    copy_ref[...] = new.astype(BF)


def update_outs(mats):
    w, left, right = mats[:3]
    (rows, n), d, side = w.shape, left.shape[1], right.shape[0]
    flip = n % 128 != 0
    outs = [sds((n, d) if flip else (d, n), F32), sds((rows, d), F32), sds((side, n), F32)]
    return outs + [sds((rows, n), F32), sds((rows, n), BF)], flip, pltpu.VMEM((d, n), F32)


def update_one(mats, near_blocks, far_blocks, total, idx, name, after=(), tick=0):
    outs, flip, scr = update_outs(mats)
    step = mats[1].shape[1] // WAYS

    def kernel(idx, *refs):
        ins, (even, odd), rest = refs[:5], refs[5:7], refs[7:]
        for i, k in enumerate(ORDER):
            for far_one, blocks in enumerate((even, odd)):
                j = jnp.bitwise_xor(idx[0], k + far_one)
                rest[6][pl.ds(pl.multiple_of(j * step, step), step), :] = blocks[i].astype(F32)
        precondition(idx, ins, rest[:5], rest[6], total, flip)
        rest[5][...] = jnp.zeros(rest[5].shape, F32)

    ins = [*mats, near_blocks, far_blocks]
    outs = outs + [sds((8, 128), F32)]
    res = run(kernel, (1,), ins, fulls(ins), outs, fulls(outs), idx, name, tick, [scr], after, range(5))
    return [res[0].T if flip else res[0], *res[1:]]


def update_pair(mats, mats2, near_blocks, far_blocks, norms, rates, total, idx, name, after=()):
    outs, flip, scr = update_outs(mats)
    outs2, flip2, scr2 = update_outs(mats2)
    step, n = mats[1].shape[1] // WAYS, mats[0].shape[1]
    step2, n2 = mats2[1].shape[1] // WAYS, mats2[0].shape[1]
    half = (near_blocks.shape[1] - step) // 2
    wide = norms[1].shape[1]

    def kernel(idx, *refs):
        ins, ins2, (even, odd), norm_refs, rest = refs[:5], refs[5:10], refs[10:12], refs[12:15], refs[15:]
        sums = 0.0
        for i, k in enumerate(ORDER):
            for far_one, blocks in enumerate((even, odd)):
                j = jnp.bitwise_xor(idx[0], k + far_one)
                block = blocks[i].astype(F32)
                rest[-2][pl.ds(pl.multiple_of(j * step, step), step), :] = block[:step, :n]
                rest[-1][pl.ds(pl.multiple_of(j * step2, step2), step2), :] = unpack_rows(block[:step, n:], n2)
                sums = sums + (block[step : step + half] + block[step + half :])
        grads = [sums[:4], jnp.concatenate([sums[4:5, :wide], sums[4:5, wide : 2 * wide]], axis=0), sums[5:7]]
        for i, (grad, rate) in enumerate(zip(grads, (rates[0], rates[0], rates[1]))):
            rest[10 + i][...] = grad
            rest[13 + i][...] = norm_refs[i][...] - rate * grad
        precondition(idx, ins2, rest[5:10], rest[-1], total, flip2)
        precondition(idx, ins, rest[:5], rest[-2], total, flip)

    all_outs = outs + outs2 + [sds(x.shape, F32) for x in [*norms, *norms]]
    ins = [*mats, *mats2, near_blocks, far_blocks, *norms]
    res = run(kernel, (1,), ins, fulls(ins), all_outs, fulls(all_outs), idx, name, 6, [scr, scr2], after)
    res = list(res)
    res[0] = res[0].T if flip else res[0]
    res[5] = res[5].T if flip2 else res[5]
    return res[:5], res[5:10], res[10:]


def body(
    tokens,
    cotangent,
    doc_lengths,
    outer_norms,
    attn_norm,
    ffn_norm,
    w_qkv,
    left_qkv,
    right_qkv,
    left_root_qkv,
    right_root_qkv,
    w_out,
    left_out,
    right_out,
    left_root_out,
    right_root_out,
    w_up,
    left_up,
    right_up,
    left_root_up,
    right_root_up,
    w_down,
    left_down,
    right_down,
    left_root_down,
    right_root_down,
):
    row_count = tokens.shape[0]
    n_dp, n_mp = lax.axis_size("dp"), lax.axis_size("mp")
    fine = n_dp // WAYS
    total = row_count * n_dp
    dp_at, mp_at = lax.axis_index("dp"), lax.axis_index("mp")
    idx = jnp.stack([dp_at // fine, mp_at, dp_at]).astype(jnp.int32)
    hw = w_qkv.shape[2] // 3

    def swap(x, axis, size, k):
        return lax.ppermute(x, axis, [(i, i ^ k) for i in range(size)])

    def dp(x, k):
        return swap(x, "dp", n_dp, k * fine)

    def mp(x, k):
        return swap(x, "mp", n_mp, k)

    def fine_rows(x):
        k = 1
        while k < fine:
            got = swap(x, "dp", n_dp, k)
            x = jnp.where((dp_at & k) == 0, jnp.concatenate([x, got], 0), jnp.concatenate([got, x], 0))
            k *= 2
        return x

    def fine_sum(x):
        k = 1
        while k < fine:
            x = x + swap(x, "dp", n_dp, k)
            k *= 2
        return x

    def gather8(own, *early):
        parts = {0: own}
        for k in (2, 4, 6):
            parts[k] = dp(own, k)
        parts[1] = dp(own, 1)
        for k in (2, 4, 6):
            parts[k ^ 1] = dp(after(parts[k], *early) if early else parts[k], 1)
        return [parts[k] for k in range(WAYS)]

    def gather4(own):
        far = mp(own, 2)
        return [own, mp(own, 1), far, mp(far, 1)]

    def scatter4(send, keep):
        got = mp(send, 1)
        return keep, got, mp((keep[1] + got[1].astype(F32)).astype(BF), 2)

    def gather8_halves(own):
        two = jnp.stack([own, dp(own, 4)])
        four = jnp.concatenate([two, dp(two, 2)])
        return four, dp(four, 1)

    def after(x, *deps):
        return lax.optimization_barrier((x, *deps))[0]

    groups = tokens.shape[1] // hw
    if fine == 1:
        first = pack_weights(w_qkv[0], w_out[0], groups, idx)
    else:
        out_rows = fine_rows(w_out[0].astype(BF))
        first = jnp.concatenate([fine_rows(w_qkv[0].astype(BF)), pack_rows(out_rows, groups)], axis=1)
    up_own, down_own = (fine_rows(x) for x in cast_pair(w_up[0], w_down[0], idx))
    down_two = jnp.stack([down_own, dp(down_own, 1)])
    first = gather8(first, down_two)

    ends = jnp.cumsum(doc_lengths[0])
    places = jnp.arange(row_count, dtype=jnp.int32)
    start = jnp.max(jnp.where(ends[None, :] <= places[:, None], ends[None, :], 0), axis=1, keepdims=True)
    start = start.astype(jnp.int32)
    hat, _ = normalize(tokens.astype(F32))
    a_low = (hat * outer_norms[0] + outer_norms[1]).astype(BF)

    up_go = after(up_own, first[2], first[4], first[6], down_two)
    up_z = [dp(up_go, k) for k in ORDER[1:]]
    down_z2 = dp(after(down_two, up_go), 4)
    q, k, v, wq, wo = project(a_low, attn_norm, first, hw, idx)
    wo_far = mp(wo, 2)
    o, *probs = attend(start, q, k, v, idx)
    o, *up_z = lax.optimization_barrier((o, *up_z))
    o_far = mp(o, 2)
    up_four = jnp.stack([up_own, *lax.optimization_barrier((*up_z, down_z2))[:-1]])
    up_x = dp(up_four, 1)
    wo_near, wo_last = mp(after(wo, up_four), 1), mp(after(wo_far, up_four), 1)
    down_four = join([down_two, down_z2], idx, [up_four, wo_near, wo_last])
    down_z1 = dp(down_four, 2)
    o_near = mp(after(o, o_far), 1)
    o_all = [o, o_near, o_far, mp(o_far, 1)]
    wo_all = [wo, wo_near, wo_far, wo_last]
    hidden, c_low = outproj(outer_norms, tokens, o_all, wo_all, idx, [up_x])
    z, slope, dw, stats, wu, wd = ffn_up(c_low, cotangent, ffn_norm, [up_four, up_x, down_four, down_z1], idx)
    stats = lax.all_gather(stats, "mp")
    w_low, du, dc_send, dc_keep, dc_last, ffn_grads = ffn_mid(z, slope, dw, stats, ffn_norm, wu, idx)
    dc_got = mp(dc_send, 1)
    dc_sum = far_sum(dc_last, dc_got, idx)
    down_send, down_keep = weight_grad(w_low, cotangent, idx, "grad_down", [dc_sum])
    down_x = dp(down_send, 1)
    up_send, up_keep = weight_grad(c_low, du, idx, "grad_up", [down_send])
    up_x2 = dp(after(up_send, down_send), 1)
    dh, outer_late, attn_grads, *rest = shard_back(
        dc_keep, dc_got, mp(dc_sum, 2), hidden, cotangent, outer_norms, o_all, wo_all, idx, [up_send]
    )
    do, (go_send, go_keep, go_last) = rest[:n_mp], rest[n_mp:]
    do = [do[0]] + [mp(do[k], k) for k in range(1, n_mp)]
    go_got = mp(go_send, 1)
    bo_send, bo_keep, bo_last = ffn_out(w_low, wd, idx, [do[1]])
    down_t, down_low = fold(down_keep, down_x, idx, [bo_send], 0)
    go_sum = far_sum(go_last, go_got, idx, [down_low], 0)
    dqkv = attend_back(q, k, v, probs, do, idx, [go_sum])
    down_z1 = dp(down_low, 2)
    go_far = mp(go_sum, 2)
    bo_got = mp(after(bo_send, dqkv), 1)
    down_t, down_low = fold(down_t, down_z1, idx, [dqkv])
    up_t, up_low = fold(up_keep, up_x2, idx, [down_low])
    qkv_send, qkv_keep, da_send, da_keep, da_last = qkv_back(
        a_low, dqkv, wq, [go_keep, go_got, go_far], idx, [up_low]
    )

    down_z2, up_z1 = dp(down_low, 4), dp(up_low, 2)
    qkv_x = dp(qkv_send, 1)
    da_got = mp(da_send, 1)
    down_done = fine_sum(close(down_t, [down_z2], idx, [qkv_send], tick=20))
    down_r4 = dp(down_done, 4)
    up_t, up_low = fold(up_t, up_z1, idx, [down_done], 20)
    up_z2 = dp(up_low, 4)
    da_sum = far_sum(da_last, da_got, idx, [up_low])
    da_far = mp(da_sum, 2)
    bo_sum = far_sum(bo_last, bo_got, idx, [da_sum], 0)
    down_two = join([down_done, down_r4], idx, [bo_sum])
    down_r2 = dp(down_two, 2)
    qkv_t, qkv_low = fold(qkv_keep, qkv_x, idx, [down_two], 0)
    qkv_z1 = dp(qkv_low, 2)
    gt, outer_early = shard_end(da_keep, da_got, da_far, tokens, outer_norms, dh, idx, [qkv_low])
    lanes = outer_late.shape[1]
    vec = jnp.concatenate([outer_early, outer_late, attn_grads.reshape(-1, lanes)])
    vec_got = mp(vec, 1)
    up_done = fine_sum(close(up_t, [up_z2], idx, [gt]))
    up_r4 = dp(up_done, 4)
    vec = vec_add(vec, vec_got, idx, [up_done])
    vec_got = mp(vec, 2)
    gt_far = mp(after(gt, vec), 2)
    down_four = join([down_two, down_r2], idx, [vec])
    down_other = dp(down_four, 1)
    vec = vec_add(vec, vec_got, idx, [down_four])
    bo_far = mp(after(bo_sum, vec), 2)
    qkv_t, qkv_low = fold(qkv_t, qkv_z1, idx, [vec])
    qkv_z2 = dp(qkv_low, 4)
    up_two = join([up_done, up_r4], idx, [qkv_low], hbm=(0, 1))
    up_r2 = dp(up_two, 2)
    attn_own = lax.dynamic_slice_in_dim(vec[4:].reshape(n_mp, -1), mp_at, 1, 0)
    attn_own = jnp.pad(attn_own, ((0, 0), (0, lanes - attn_own.shape[1])))
    vec = jnp.concatenate([vec[:4], attn_own, ffn_grads, jnp.zeros((1, lanes), F32)])
    vec = fine_sum(vec)
    qkv_own = close(qkv_t, [qkv_z2], idx, [up_two, down_other, gt_far], None if fine > 1 else vec)
    if fine > 1:
        high = vec.astype(BF)
        qkv_own = jnp.concatenate([fine_sum(qkv_own), high, (vec - high.astype(F32)).astype(BF)])
    qkv_z = [dp(qkv_own, k) for k in ORDER[1:]]
    up_four = join([up_two, up_r2], idx, [qkv_own])
    out_own = block_end(hidden, bo_keep, bo_got, bo_far, idx, [up_four])
    out_far = mp(out_own, 2)
    up_other = dp(up_four, 1)
    down_mats = [x[0] for x in (w_down, left_down, right_down, left_root_down, right_root_down)]
    *down_res, token = update_one(down_mats, down_four, down_other, total, idx, "update_down", [up_four])
    qkv_four = join([qkv_own, *qkv_z], idx, [token], 10)
    qkv_other = dp(qkv_four, 1)

    def mats(*arrays):
        return [x[0] for x in arrays]

    ready = warm(
        mats(w_qkv, left_qkv, right_qkv, left_root_qkv, right_root_qkv)
        + mats(w_out, left_out, right_out, left_root_out, right_root_out),
        idx,
        [qkv_four],
    )
    up_mats = mats(w_up, left_up, right_up, left_root_up, right_root_up)
    *up_res, token = update_one(up_mats, up_four, up_other, total, idx, "update_up", [ready[0]], 0)
    gt_far, out_far = after(gt_far, token), after(out_far, token)
    gt_all = [gt, mp(after(gt, gt_far), 1), gt_far, mp(gt_far, 1)]
    grad_tokens, token = spread_rows(gt_all, idx, "spread_tokens", [token])
    out_all = [out_own, mp(after(out_own, out_far), 1), out_far, mp(out_far, 1)]
    block_out, token = spread_rows(out_all, idx, "spread_out", [token])
    qkv_res, out_res, vecs = update_pair(
        ready[:5],
        ready[5:],
        qkv_four,
        qkv_other,
        [outer_norms, attn_norm, ffn_norm],
        (VEC_RATE / math.sqrt(total), UNIT_RATE / math.sqrt(total)),
        total,
        idx,
        "update_qkv",
        [token],
    )

    return (
        block_out,
        grad_tokens,
        *vecs,
        *(x[None] for x in qkv_res),
        *(x[None] for x in out_res),
        *(x[None] for x in up_res),
        *(x[None] for x in down_res),
    )


def solution(mesh):
    rows = P("dp", None)
    mats = (P("mp", "dp", None),) * 4 + (P("mp", None, None),)
    res = (P("mp", None, None),) + (P("mp", "dp", None),) * 4
    cols = P(None, "mp")
    return jax.shard_map(
        body,
        mesh=mesh,
        in_specs=(rows, rows, rows, P(), cols, cols) + mats * 4,
        out_specs=(rows, rows, P(), cols, cols, P(), cols, cols) + res * 4,
        check_vma=False,
    )
```

```python
import math

import jax
import jax.numpy as jnp
from jax import lax
from jax.experimental import pallas as pl
from jax.experimental.pallas import tpu as pltpu
from jax.sharding import PartitionSpec as P

HD = 64
EPS = 1e-05
DECAY = 0.5
MAT_RATE = 0.5
VEC_RATE = 0.05
UNIT_RATE = 0.3
GELU_A = math.sqrt(2.0 / math.pi)
GELU_B = 0.044715
BF = jnp.bfloat16
F32 = jnp.float32
VMEM = 22 * 1024 * 1024
WAYS = 8
RATE = 4e8
TICK = 5
BLK = 256
WIDE = 512
ORDER = (0, 4, 2, 6)


def full(shape):
    return pl.BlockSpec(shape, lambda *args: (0,) * len(shape))


def fulls(arrays):
    return [full(x.shape) for x in arrays]


def run(kernel, grid, ins, in_specs, outs, out_specs, idx, name, micros, scratch=(), after=(), hbm=()):
    count, kernel_in = len(ins), kernel
    ins = [pltpu.with_memory_space_constraint(x, pltpu.HBM) if i in hbm else x for i, x in enumerate(ins)]

    def kernel(idx, *refs):
        kernel_in(idx, *refs[:count], *refs[count + len(after) :])

    return pl.pallas_call(
        kernel,
        grid_spec=pltpu.PrefetchScalarGridSpec(
            num_scalar_prefetch=1,
            grid=grid,
            in_specs=list(in_specs) + [pl.BlockSpec(memory_space=pl.ANY)] * len(after),
            out_specs=out_specs,
            scratch_shapes=list(scratch),
        ),
        out_shape=outs,
        compiler_params=pltpu.CompilerParams(vmem_limit_bytes=VMEM),
        cost_estimate=pl.CostEstimate(flops=int(micros * RATE), bytes_accessed=1024, transcendentals=0),
        name=name,
    )(idx, *ins, *after)


def sds(shape, dtype):
    return jax.ShapeDtypeStruct(shape, dtype)


def near(shape, dtype):
    return pltpu.VMEM(shape, dtype)


def far(shape, dtype):
    return pltpu.HBM(shape, dtype)


def dot(x, y):
    return jnp.dot(x, y, preferred_element_type=F32)


def dot_nt(x, y):
    return lax.dot_general(x, y, (((1,), (1,)), ((), ())), preferred_element_type=F32)


def dot_tn(x, y):
    return lax.dot_general(x, y, (((0,), (0,)), ((), ())), preferred_element_type=F32)


def rowsum(x):
    return jnp.sum(x, -1, keepdims=True)


def normalize(x):
    n = x.shape[-1]
    off = x - rowsum(x) / n
    r = lax.rsqrt(rowsum(off * off) / n + EPS)
    return off * r, r


def gelu_parts(u):
    t = jnp.tanh(GELU_A * (u + GELU_B * (u * u * u)))
    return 0.5 * u * (1.0 + t), t


def unpack_rows(side, wide):
    groups = wide // side.shape[1]
    rows = side.shape[0] // groups
    return jnp.concatenate([side[i * rows : (i + 1) * rows] for i in range(groups)], axis=1)


def pack_rows(block, groups):
    n = block.shape[1] // groups
    return jnp.concatenate([block[:, i * n : (i + 1) * n] for i in range(groups)], axis=0)


def project_kernel(idx, a_ref, an_ref, *refs):
    pieces = refs[:WAYS]
    q_ref, k_ref, v_ref, wq_ref, wo_ref, scr = refs[WAYS:]
    rows = wq_ref.shape[0] // WAYS
    orows = scr.shape[0] // WAYS
    hw = q_ref.shape[1]

    @pl.when(pl.program_id(0) == 0)
    def _():
        for k in range(WAYS):
            j = jnp.bitwise_xor(idx[0], k)
            wq_ref[pl.ds(pl.multiple_of(j * rows, rows), rows), :] = pieces[k][:, : 3 * hw]
            tail = pieces[k][:, 3 * hw :].astype(F32)
            scr[pl.ds(pl.multiple_of(j * orows, orows), orows), :] = unpack_rows(tail, wo_ref.shape[1])
        wo_ref[:hw, :] = scr[...].astype(BF)
        norm = jnp.concatenate([an_ref[0:1, :], an_ref[1:2, :]], axis=1)
        high = norm.astype(BF).astype(F32)
        row = jnp.concatenate([high, norm - high], axis=1)
        pad = wo_ref.shape[0] - hw
        at = lax.broadcasted_iota(jnp.int32, (pad, row.shape[1]), 0)
        wo_ref[hw:, :] = jnp.where(at == 0, row, 0.0).astype(BF)

    res = dot(a_ref[...], wq_ref[...]).astype(BF)
    q_ref[...] = res[:, :hw] * BF(HD ** (-0.5))
    k_ref[...] = res[:, hw : 2 * hw]
    v_ref[...] = res[:, 2 * hw :]


def project(a, norm, pieces, hw, idx):
    rows, d = a.shape
    n = 3 * hw
    blk = lambda w: pl.BlockSpec((BLK, w), lambda s, i: (s, 0))
    return run(
        project_kernel,
        (rows // BLK,),
        [a, norm, *pieces],
        [blk(d), full(norm.shape)] + fulls(pieces),
        [far((rows, hw), BF)] * 3 + [far((d, n), BF), far((hw + 16, d), BF)],
        [blk(hw)] * 3 + [full((d, n)), full((hw + 16, d))],
        idx,
        "project",
        40,
        [pltpu.VMEM((hw, d), F32)],
    )


def attend_kernel(idx, start_ref, q_ref, k_ref, v_ref, o_ref, *p_refs):
    h = pl.program_id(0)
    rows, hw = q_ref.shape
    lane = (lax.broadcasted_iota(jnp.int32, (1, hw), 1) // HD) == h
    for i in range(rows // BLK):
        lo, hi = i * BLK, (i + 1) * BLK
        qb = jnp.where(lane, q_ref[lo:hi, :], BF(0))
        s = dot_nt(qb, k_ref[:hi, :])
        kpos = lax.broadcasted_iota(jnp.int32, (BLK, hi), 1)
        qpos = lo + lax.broadcasted_iota(jnp.int32, (BLK, hi), 0)
        s = jnp.where((kpos >= start_ref[lo:hi, :]) & (kpos <= qpos), s, -1e30)
        p = jnp.exp(s - jnp.max(s, -1, keepdims=True))
        p = (p * (1.0 / rowsum(p))).astype(BF)
        p_refs[i][0] = p
        ob = dot(p, v_ref[:hi, :]).astype(BF)
        o_ref[lo:hi, :] = jnp.where(lane, ob, o_ref[lo:hi, :])


def widths(rows):
    return range(BLK, rows + BLK, BLK)


def head_spec(width):
    return pl.BlockSpec((1, BLK, width), lambda s, i: (s, 0, 0))


def attend(start, q, k, v, idx, after=()):
    rows, hw = q.shape
    heads = hw // HD
    return run(
        attend_kernel,
        (heads,),
        [start, q, k, v],
        fulls([start, q, k, v]),
        [far((rows, hw), BF)] + [far((heads, BLK, w), BF) for w in widths(rows)],
        [full((rows, hw))] + [head_spec(w) for w in widths(rows)],
        idx,
        "attend",
        10,
        after=after,
        hbm=(1, 2, 3),
    )


def wide_norm(o_refs):
    parts = [x[...].astype(F32) for x in o_refs]
    n = sum(x.shape[-1] for x in parts)
    mean = sum(rowsum(x) for x in parts) / n
    parts = [x - mean for x in parts]
    r = lax.rsqrt(sum(rowsum(x * x) for x in parts) / n + EPS)
    return [x * r for x in parts], r


def unpack_norm(w_ref):
    hw = w_ref.shape[0] - 16
    row = w_ref[hw:, :].astype(F32)[0:1, :]
    gain, bias, gain_low, bias_low = (row[:, i * hw : (i + 1) * hw] for i in range(4))
    return gain + gain_low, bias + bias_low


def outproj_kernel(idx, on_ref, tok_ref, *refs):
    g = (len(refs) - 2) // 2
    o_refs, w_refs = refs[:g], refs[g : 2 * g]
    h_ref, c_ref = refs[2 * g :]
    hats, _ = wide_norm(o_refs)
    acc = tok_ref[...].astype(F32)
    for k in range(g):
        gain, bias = unpack_norm(w_refs[k])
        y = (hats[k] * gain + bias).astype(BF)
        acc = acc + dot(y, w_refs[k][: gain.shape[1], :])
    h_ref[...] = acc
    hat, _ = normalize(acc)
    c_ref[...] = (hat * on_ref[2:3, :] + on_ref[3:4, :]).astype(BF)


def outproj(on, tok, o, w, idx, after=()):
    rows, d = tok.shape
    hw = o[0].shape[1]
    blk = lambda n: pl.BlockSpec((WIDE, n), lambda s, i: (s, 0))
    return run(
        outproj_kernel,
        (rows // WIDE,),
        [on, tok, *o, *w],
        fulls([on]) + [blk(d)] + [blk(hw)] * len(o) + fulls(w),
        [far((rows, d), F32), near((rows, d), BF)],
        [blk(d), blk(d)],
        idx,
        "outproj",
        0,
        after=after,
        hbm=(1,),
    )


def ffn_up_kernel(idx, c_ref, e_ref, fn_ref, *refs):
    ups, downs = refs[:2], refs[2:4]
    z_ref, slope_ref, dw_ref, st_ref, wu_ref, wd_ref = refs[4:]
    rows = ups[0].shape[1]

    @pl.when(pl.program_id(0) == 0)
    def _():
        for i, k in enumerate(ORDER):
            for odd in range(2):
                j = jnp.bitwise_xor(idx[0], k + odd)
                at = pl.ds(pl.multiple_of(j * rows, rows), rows)
                wu_ref[at, :] = ups[odd][i]
                wd_ref[at, :] = downs[i // 2][i % 2 * 2 + odd]

    u = dot(c_ref[...], wu_ref[...])
    z, t = gelu_parts(u)
    z_ref[...] = z
    slope_ref[...] = 0.5 * (1.0 + t) + 0.5 * u * (1.0 - t * t) * (GELU_A * (1.0 + (3.0 * GELU_B) * (u * u)))
    mean = rowsum(z) / z.shape[-1]
    z = z - mean
    dw = dot_nt(e_ref[...], wd_ref[...])
    dw_ref[...] = dw
    eg = dw * fn_ref[0:1, :]
    stats = [mean, rowsum(z * z), rowsum(eg), rowsum(eg * z)]
    place = lax.broadcasted_iota(jnp.int32, (WIDE, 128), 1)
    tile = jnp.zeros((WIDE, 128), F32)
    for i, x in enumerate(stats):
        tile = jnp.where(place == i, x, tile)
    st_ref[...] = tile.T[:8, :]


def ffn_up(c, e, fn, pieces, idx):
    rows, d = c.shape
    fl = fn.shape[1]
    rblk = lambda n: pl.BlockSpec((WIDE, n), lambda s, i: (s, 0))
    return run(
        ffn_up_kernel,
        (rows // WIDE,),
        [c, e, fn, *pieces],
        [rblk(d), rblk(d), full(fn.shape)] + fulls(pieces),
        [near((rows, fl), F32)] * 3 + [sds((8, rows), F32), near((d, fl), BF), far((fl, d), BF)],
        [rblk(fl)] * 3 + [pl.BlockSpec((8, WIDE), lambda s, i: (0, s)), full((d, fl)), full((fl, d))],
        idx,
        "ffn_up",
        7.5,
        hbm=(1,),
    )


def rel_of(s):
    return jnp.where(s < 2, 2 * s + 1, 2 * s - 4)


def rel_block(s, i):
    return jnp.bitwise_xor(rel_of(s), i[1])


def rel_spec(n):
    return pl.BlockSpec((BLK, n), lambda s, i: (rel_block(s, i), 0))


SEND_SPEC = lambda n: pl.BlockSpec((1, BLK, n), lambda s, i: (jnp.minimum(s, 1), 0, 0))
KEEP_SPEC = lambda n: full((BLK, n))


def put_rel(send_ref, keep_ref, last_ref, value):
    @pl.when(pl.program_id(0) < 2)
    def _():
        send_ref[0] = value.astype(BF)

    @pl.when(pl.program_id(0) == 2)
    def _():
        keep_ref[...] = value

    @pl.when(pl.program_id(0) == 3)
    def _():
        last_ref[...] = value


def ffn_mid_kernel(idx, z_ref, slope_ref, dw_ref, st_ref, fn_ref, wu_ref, w_ref, du_ref, send_ref, keep_ref, last_ref, fg_ref):
    g = st_ref.shape[0]
    fl = z_ref.shape[1]
    n = g * fl
    st = [st_ref[k] for k in range(g)]
    mean = sum(x[0:1] for x in st) / g
    gap = [x[0:1] - mean for x in st]
    spread = sum(x[1:2] + fl * (gp * gp) for x, gp in zip(st, gap)) / n
    r = lax.rsqrt(spread + EPS)
    s_plain = sum(x[2:3] for x in st) / n
    s_norm = r * (sum(x[3:4] + gp * x[2:3] for x, gp in zip(st, gap)) / n)
    cols = jnp.concatenate([mean, r, s_plain, s_norm, jnp.zeros((124, BLK), F32)], axis=0).T
    mean, r, s_plain, s_norm = (cols[:, i : i + 1] for i in range(4))
    hat = (z_ref[...] - mean) * r
    w_ref[...] = (hat * fn_ref[0:1, :] + fn_ref[1:2, :]).astype(BF)
    dw = dw_ref[...]
    dz = r * (dw * fn_ref[0:1, :] - s_plain - hat * s_norm)
    du = (dz * slope_ref[...]).astype(BF)
    du_ref[...] = du
    put_rel(send_ref, keep_ref, last_ref, dot_nt(du, wu_ref[...]))
    grads = jnp.concatenate([jnp.sum(dw * hat, 0, keepdims=True), jnp.sum(dw, 0, keepdims=True)], axis=0)

    @pl.when(pl.program_id(0) == 0)
    def _():
        fg_ref[...] = grads

    @pl.when(pl.program_id(0) > 0)
    def _():
        fg_ref[...] += grads


def ffn_mid(z, slope, dw, st, fn, wu, idx):
    rows, fl = z.shape
    d = wu.shape[0]
    return run(
        ffn_mid_kernel,
        (rows // BLK,),
        [z, slope, dw, st, fn, wu],
        [rel_spec(fl)] * 3 + [pl.BlockSpec((st.shape[0], 8, BLK), lambda s, i: (0, 0, rel_block(s, i)))]
        + fulls([fn, wu]),
        [far((rows, fl), BF), far((rows, fl), BF), sds((2, BLK, d), BF), far((BLK, d), F32), sds((BLK, d), F32), sds((2, fl), F32)],
        [rel_spec(fl), rel_spec(fl), SEND_SPEC(d), KEEP_SPEC(d), KEEP_SPEC(d), full((2, fl))],
        idx,
        "ffn_mid",
        6.5,
    )


def ffn_out(x, w, idx, after):
    rows, depth = x.shape
    d = w.shape[1]

    def kernel(idx, x_ref, w_ref, send_ref, keep_ref, last_ref):
        put_rel(send_ref, keep_ref, last_ref, dot(x_ref[...], w_ref[...]))

    return run(
        kernel,
        (rows // BLK,),
        [x, w],
        [rel_spec(depth), full(w.shape)],
        [sds((2, BLK, d), BF), far((BLK, d), F32), sds((BLK, d), F32)],
        [SEND_SPEC(d), KEEP_SPEC(d), KEEP_SPEC(d)],
        idx,
        "ffn_out",
        0,
        (),
        after,
        (0, 1),
    )


def put_blocks(scr, send_ref, keep_ref, first, step):
    for i, k in enumerate(ORDER):
        for odd, dest in enumerate((keep_ref, send_ref)):
            j = jnp.bitwise_xor(first, k + odd)
            value = scr[pl.ds(pl.multiple_of(j * step, step), step), :]
            dest[i, :, : value.shape[1]] = value.astype(dest.dtype)


def weight_grad(x, y, idx, name, after=()):
    rows, d = x.shape
    n = y.shape[1]
    step = d // WAYS
    steps = d // BLK

    def kernel(idx, x_ref, y_ref, send_ref, keep_ref, scr):
        s = pl.program_id(0)
        scr[pl.ds(pl.multiple_of(s * BLK, BLK), BLK), :] = dot_tn(x_ref[...], y_ref[...])

        @pl.when(s == steps - 1)
        def _():
            put_blocks(scr, send_ref, keep_ref, idx[0], step)

    return run(
        kernel,
        (steps,),
        [x, y],
        [pl.BlockSpec((rows, BLK), lambda s, i: (0, s)), full(y.shape)],
        [sds((WAYS // 2, step, n), BF), far((WAYS // 2, step, n), BF)],
        [full((WAYS // 2, step, n))] * 2,
        idx,
        name,
        3.5,
        [pltpu.VMEM((d, n), F32)],
        after,
    )


def qkv_back(a, dqkv, wq, go, idx, after=()):
    rows, d = a.shape
    n = dqkv.shape[1]
    step = d // WAYS
    hw = go[2].shape[0]
    groups = d // hw
    orows = hw // WAYS

    def kernel(idx, a_ref, d_ref, w_ref, go0_ref, go1_ref, go2_ref, gs_ref, gk_ref, send_ref, keep_ref, last_ref, scr, go_ref):
        go_ref[...] = go0_ref[...] + go1_ref[0].astype(F32) + go2_ref[...].astype(F32)
        for s in range(d // BLK):
            scr[s * BLK : (s + 1) * BLK, :] = dot_tn(a_ref[:, s * BLK : (s + 1) * BLK], d_ref[...])
        put_blocks(scr, gs_ref, gk_ref, idx[0], step)
        for i, k in enumerate(ORDER):
            for odd, dest in enumerate((gk_ref, gs_ref)):
                j = jnp.bitwise_xor(idx[0], k + odd)
                tail = pack_rows(go_ref[pl.ds(pl.multiple_of(j * orows, orows), orows), :], groups)
                dest[i, :, n:] = tail.astype(dest.dtype)
        for k in range(4):
            j = jnp.bitwise_xor(idx[1], k)
            value = dot_nt(d_ref[pl.ds(pl.multiple_of(j * BLK, BLK), BLK), :], w_ref[...])
            if k % 2:
                send_ref[k // 2] = value.astype(BF)
            else:
                (last_ref if k else keep_ref)[...] = value

    ins = [a, dqkv, wq, *go]
    lead = pl.BlockSpec((1, hw, d), lambda s, i: (0, 0, 0))
    half = (WAYS // 2, step, d)
    part = (2, BLK, d)
    outs = [sds(half, BF), far(half, BF), sds(part, BF), far(part[1:], F32), sds(part[1:], F32)]
    return run(
        kernel, (1,), ins, fulls(ins[:4]) + [lead, full(go[2].shape)], outs, fulls(outs), idx, "qkv_back", 40,
        [pltpu.VMEM((d, n), F32), pltpu.VMEM((hw, d), F32)],
        after=after,
        hbm=(0, 2, 3),
    )


def shard_back_kernel(idx, dc0_ref, dc1_ref, dc2_ref, h_ref, e_ref, on_ref, *refs):
    g = 4
    o_refs, w_refs = refs[:g], refs[g : 2 * g]
    dh_ref, ol_ref, ag_ref, *do_refs = refs[2 * g :]
    do_refs, (gs_ref, gk_ref, gl_ref) = do_refs[:g], do_refs[g:]
    dc = dc0_ref[...] + dc1_ref[0].astype(F32) + dc2_ref[...].astype(F32)
    hat, r = normalize(h_ref[...])
    wgt = dc * on_ref[2:3, :]
    n = dc.shape[-1]
    dh = e_ref[...].astype(F32) + r * (wgt - rowsum(wgt) / n - hat * (rowsum(wgt * hat) / n))
    dh_ref[...] = dh
    ol_ref[...] = jnp.concatenate([jnp.sum(dc * hat, 0, keepdims=True), jnp.sum(dc, 0, keepdims=True)], axis=0)
    dhb = dh.astype(BF)
    hats, r = wide_norm(o_refs)
    norms = [unpack_norm(w_refs[k]) for k in range(g)]
    dys = [dot_nt(dhb, w_refs[k][: norms[k][0].shape[1], :]) for k in range(g)]
    wgts = [dys[k] * norms[k][0] for k in range(g)]
    s_plain = sum(rowsum(x) for x in wgts) / n
    s_norm = sum(rowsum(x * y) for x, y in zip(wgts, hats)) / n
    for k in range(g):
        do_refs[k][...] = (r * (wgts[k] - s_plain - hats[k] * s_norm)).astype(BF)
        ag_ref[jnp.bitwise_xor(idx[1], k)] = jnp.concatenate(
            [jnp.sum(dys[k] * hats[k], 0, keepdims=True), jnp.sum(dys[k], 0, keepdims=True)], axis=0
        )
    for k in range(g):
        y = (hats[k] * norms[k][0] + norms[k][1]).astype(BF)
        value = dot_tn(y, dhb)
        if k % 2:
            gs_ref[k // 2] = value.astype(BF)
        else:
            (gl_ref if k else gk_ref)[...] = value


def shard_back(dc_keep, dc_one, dc_two, h, e, on, o, w, idx, after):
    rows, d = h.shape
    g = len(o)
    hw = o[0].shape[1]
    mine = lambda n: pl.BlockSpec((BLK, n), lambda s, i: (i[1], 0))
    lead = pl.BlockSpec((1, BLK, d), lambda s, i: (0, 0, 0))
    ins = [dc_keep, dc_one, dc_two, h, e, on, *o, *w]
    return run(
        shard_back_kernel,
        (1,),
        ins,
        [full((BLK, d)), lead, full((BLK, d)), mine(d), mine(d)] + fulls([on]) + [mine(hw)] * g + fulls(w),
        [far((BLK, d), F32), sds((2, d), F32), sds((g, 2, hw), F32)]
        + [sds((BLK, hw), BF)] * g
        + [sds((2, hw, d), BF), far((hw, d), F32), sds((hw, d), F32)],
        [full((BLK, d)), full((2, d)), full((g, 2, hw))]
        + [full((BLK, hw))] * g
        + [full((2, hw, d)), full((hw, d)), full((hw, d))],
        idx,
        "shard_back",
        0,
        after=after,
        hbm=(0, 3, 4) + tuple(range(6, 6 + 2 * g)),
    )


def attend_back_kernel(idx, q_ref, k_ref, v_ref, *refs):
    h = pl.program_id(0)
    rows, hw = q_ref.shape
    count = rows // BLK
    p_refs, d_refs = refs[:count], refs[count : count + 4]
    out_ref, do_scr, dq_scr, dk_scr, dv_scr = refs[count + 4 :]

    @pl.when(h == 0)
    def _():
        for k in range(4):
            j = jnp.bitwise_xor(idx[1], k)
            do_scr[pl.ds(pl.multiple_of(j * BLK, BLK), BLK), :] = d_refs[k][...]
        dk_scr[...] = jnp.zeros_like(dk_scr)
        dv_scr[...] = jnp.zeros_like(dv_scr)
        dq_scr[...] = jnp.zeros_like(dq_scr)

    lane = (lax.broadcasted_iota(jnp.int32, (1, hw), 1) // HD) == h
    for i in range(rows // BLK):
        lo, hi = i * BLK, (i + 1) * BLK
        dob = jnp.where(lane, do_scr[lo:hi, :], BF(0))
        qb = jnp.where(lane, q_ref[lo:hi, :], BF(0))
        pb = p_refs[i][0]
        p = pb.astype(F32)
        dp = dot_nt(dob, v_ref[:hi, :])
        ds = (p * (dp - rowsum(p * dp))).astype(BF)
        dq_scr[lo:hi, :] = jnp.where(lane, dot(ds, k_ref[:hi, :]), dq_scr[lo:hi, :])
        dk_scr[:hi, :] += dot_tn(ds, qb)
        dv_scr[:hi, :] += dot_tn(pb, dob)

    @pl.when(h == pl.num_programs(0) - 1)
    def _():
        out_ref[...] = jnp.concatenate([dq_scr[...] * HD ** (-0.5), dk_scr[...], dv_scr[...]], axis=1).astype(BF)


def attend_back(q, k, v, p, do, idx, after):
    rows, hw = q.shape
    heads = hw // HD
    return run(
        attend_back_kernel,
        (heads,),
        [q, k, v, *p, *do],
        fulls([q, k, v]) + [head_spec(w) for w in widths(rows)] + fulls(do),
        [sds((rows, 3 * hw), BF)],
        [full((rows, 3 * hw))],
        idx,
        "attend_back",
        11,
        [pltpu.VMEM((rows, hw), BF)] + [pltpu.VMEM((rows, hw), F32)] * 3,
        after=after,
        hbm=range(3 + len(p)),
    )[0]


def shard_end_kernel(idx, da0_ref, da1_ref, da2_ref, tok_ref, on_ref, dh_ref, gt_ref, oe_ref):
    da = da0_ref[...] + da1_ref[0].astype(F32) + da2_ref[...].astype(F32)
    hat, r = normalize(tok_ref[...].astype(F32))
    wgt = da * on_ref[0:1, :]
    n = da.shape[-1]
    grad = r * (wgt - rowsum(wgt) / n - hat * (rowsum(wgt * hat) / n))
    gt_ref[...] = (dh_ref[...] + grad).astype(BF)
    oe_ref[...] = jnp.concatenate([jnp.sum(da * hat, 0, keepdims=True), jnp.sum(da, 0, keepdims=True)], axis=0)


def shard_end(da_keep, da_one, da_two, tok, on, dh, idx, after=()):
    d = tok.shape[1]
    lead = pl.BlockSpec((1, BLK, d), lambda s, i: (0, 0, 0))
    return run(
        shard_end_kernel,
        (1,),
        [da_keep, da_one, da_two, tok, on, dh],
        [full((BLK, d)), lead, full((BLK, d)), pl.BlockSpec((BLK, d), lambda s, i: (i[1], 0)), full(on.shape), full((BLK, d))],
        [sds((BLK, d), BF), sds((2, d), F32)],
        [full((BLK, d)), full((2, d))],
        idx,
        "shard_end",
        0,
        after=after,
    )


def spread_rows(parts, idx, name, after=()):
    rows, d = parts[0].shape

    def kernel(idx, *refs):
        for k, part in enumerate(refs[:-2]):
            at = pl.ds(pl.multiple_of(jnp.bitwise_xor(idx[1], k) * rows, rows), rows)
            refs[-2][at, :] = part[...]
        refs[-1][...] = jnp.zeros(refs[-1].shape, F32)

    outs = [sds((rows * len(parts), d), BF), sds((8, 128), F32)]
    return run(kernel, (1,), parts, fulls(parts), outs, fulls(outs), idx, name, 0, (), after)


def far_sum(last, got, idx, after=(), tick=TICK):
    rows, d = last.shape

    def kernel(idx, last_ref, got_ref, out_ref):
        out_ref[...] = (last_ref[...] + got_ref[0].astype(F32)).astype(BF)

    second = pl.BlockSpec((1, rows, d), lambda s, i: (1, 0, 0))
    out = [sds((rows, d), BF)]
    return run(kernel, (1,), [last, got], [full((rows, d)), second], out, fulls(out), idx, "far_sum", tick, (), after)[0]


def fold(keep, got, idx, after=(), tick=TICK):
    count, rows, d = keep.shape
    half = count // 2

    def kernel(idx, keep_ref, got_ref, stay_ref, send_ref):
        stay_ref[...] = keep_ref[:half].astype(F32) + got_ref[:half].astype(F32)
        send = (keep_ref[half:].astype(F32) + got_ref[half:].astype(F32)).astype(BF)
        send_ref[...] = send if half > 1 else send[0]

    outs = [sds((half, rows, d), F32), sds((half, rows, d) if half > 1 else (rows, d), BF)]
    return run(kernel, (1,), [keep, got], fulls([keep, got]), outs, fulls(outs), idx, "fold", tick, (), after, (0,) if half > 1 else ())


def close(own, got, idx, after=(), vec=None, tick=TICK):
    rows, d = got[0].shape

    def kernel(idx, own_ref, *refs):
        out_ref = refs[-1]
        total = own_ref[...].reshape(rows, d)
        for ref in refs[: len(got)]:
            total = total + ref[...].astype(F32)
        out_ref[:rows, :] = total.astype(BF)
        if vec is not None:
            x = refs[len(got)][...]
            high = x.astype(BF).astype(F32)
            out_ref[rows:, :] = jnp.concatenate([high, x - high], axis=0).astype(BF)

    ins = [own, *got] + ([] if vec is None else [vec])
    out = [sds((rows if vec is None else rows + 2 * vec.shape[0], d), BF)]
    return run(kernel, (1,), ins, fulls(ins), out, fulls(out), idx, "close", tick, (), after)[0]


def join(parts, idx, after=(), tick=2 * TICK, hbm=()):
    shapes = [x.shape if len(x.shape) == 3 else (1, *x.shape) for x in parts]

    def kernel(idx, *refs):
        at = 0
        for ref, shape in zip(refs, shapes):
            refs[-1][at : at + shape[0]] = ref[...].reshape(shape)
            at += shape[0]

    out = [sds((sum(x[0] for x in shapes), *shapes[0][1:]), BF)]
    return run(kernel, (1,), parts, fulls(parts), out, fulls(out), idx, "join", tick, (), after, hbm)[0]


def block_end(h, keep, got, last, idx, after=()):
    rows, d = last.shape

    def kernel(idx, h_ref, keep_ref, got_ref, last_ref, out_ref):
        total = h_ref[...] + keep_ref[...] + got_ref[0].astype(F32) + last_ref[...].astype(F32)
        out_ref[...] = total.astype(BF)

    lead = pl.BlockSpec((1, rows, d), lambda s, i: (0, 0, 0))
    mine = pl.BlockSpec((rows, d), lambda s, i: (i[1], 0))
    own = full((rows, d))
    ins = [h, keep, got, last]
    out = [sds((rows, d), BF)]
    return run(
        kernel, (1,), ins, [mine, own, lead, own], out, fulls(out), idx, "block_end", TICK, (), after, (0,)
    )[0]


def vec_add(x, y, idx, after=(), tick=TICK):
    def kernel(idx, x_ref, y_ref, out_ref):
        out_ref[...] = x_ref[...] + y_ref[...]

    out = [sds(x.shape, F32)]
    return run(kernel, (1,), [x, y], fulls([x, y]), out, fulls(out), idx, "vec_add", tick, (), after)[0]


def pack_weights(w, w2, groups, idx):
    rows, n = w.shape

    def kernel(idx, w_ref, w2_ref, out_ref):
        out_ref[:, :n] = w_ref[...].astype(BF)
        out_ref[:, n:] = pack_rows(w2_ref[...], groups).astype(BF)

    out = [sds((rows, n + w2.shape[1] // groups), BF)]
    return run(kernel, (1,), [w, w2], fulls([w, w2]), out, fulls(out), idx, "pack_weights", 1, hbm=(0, 1))[0]


def cast_pair(x, y, idx):
    def kernel(idx, x_ref, y_ref, x_out, y_out):
        x_out[...] = x_ref[...].astype(BF)
        y_out[...] = y_ref[...].astype(BF)

    outs = [sds(x.shape, BF), sds(y.shape, BF)]
    return run(kernel, (1,), [x, y], fulls([x, y]), outs, fulls(outs), idx, "cast_pair", 1, hbm=(0, 1))


def warm(arrays, idx, after=()):
    count = len(arrays)

    def kernel(idx, *refs):
        for x, y in zip(refs[:count], refs[count:]):
            y[...] = x[...]

    outs = [near(x.shape, x.dtype) for x in arrays]
    return run(kernel, (1,), arrays, fulls(arrays), outs, fulls(outs), idx, "warm", 0, (), after, range(count))


def mark(idx, after, tick=0):
    def kernel(idx, out_ref):
        out_ref[...] = jnp.zeros(out_ref.shape, F32)

    out = [sds((8, 128), F32)]
    return run(kernel, (1,), [], [], out, fulls(out), idx, "mark", tick, (), after)[0]


def one_hot(place, count, width):
    at = lax.broadcasted_iota(jnp.int32, (count, width), 1)
    want = place * count + lax.broadcasted_iota(jnp.int32, (count, width), 0)
    return jnp.where(at == want, 1.0, 0.0).astype(BF)


def precondition(idx, ins, outs, scr, total, flip):
    w_ref, l_ref, r_ref, lr_ref, rr_ref = ins
    g_ref, nl_ref, nr_ref, nw_ref, copy_ref = outs
    d, n = scr.shape
    rows, side = w_ref.shape[0], r_ref.shape[0]
    whole = scr[...]
    g_ref[...] = whole.T if flip else whole
    grad = whole.astype(BF)
    scale = 1.0 / total
    own_cols = dot_nt(one_hot(idx[2], side, n), grad).astype(BF)
    own_rows = dot(one_hot(idx[2], rows, d), grad).astype(BF)
    nr_ref[...] = DECAY * r_ref[...] + ((1.0 - DECAY) * scale * scale) * dot(own_cols, grad)
    nl_ref[...] = DECAY * l_ref[...] + ((1.0 - DECAY) * scale * scale) * dot_nt(own_rows, grad)
    part = dot(lr_ref[...].astype(BF), grad).astype(BF)
    new = w_ref[...] - (MAT_RATE * scale) * dot(part, rr_ref[...].astype(BF))
    nw_ref[...] = new
    copy_ref[...] = new.astype(BF)


def update_outs(mats):
    w, left, right = mats[:3]
    (rows, n), d, side = w.shape, left.shape[1], right.shape[0]
    flip = n % 128 != 0
    outs = [sds((n, d) if flip else (d, n), F32), sds((rows, d), F32), sds((side, n), F32)]
    return outs + [sds((rows, n), F32), sds((rows, n), BF)], flip, pltpu.VMEM((d, n), F32)


def update_one(mats, near_blocks, far_blocks, total, idx, name, after=(), tick=0):
    outs, flip, scr = update_outs(mats)
    step = mats[1].shape[1] // WAYS

    def kernel(idx, *refs):
        ins, (even, odd), rest = refs[:5], refs[5:7], refs[7:]
        for i, k in enumerate(ORDER):
            for far_one, blocks in enumerate((even, odd)):
                j = jnp.bitwise_xor(idx[0], k + far_one)
                rest[6][pl.ds(pl.multiple_of(j * step, step), step), :] = blocks[i].astype(F32)
        precondition(idx, ins, rest[:5], rest[6], total, flip)
        rest[5][...] = jnp.zeros(rest[5].shape, F32)

    ins = [*mats, near_blocks, far_blocks]
    outs = outs + [sds((8, 128), F32)]
    res = run(kernel, (1,), ins, fulls(ins), outs, fulls(outs), idx, name, tick, [scr], after, range(5))
    return [res[0].T if flip else res[0], *res[1:]]


def update_pair(mats, mats2, near_blocks, far_blocks, norms, rates, total, idx, name, after=()):
    outs, flip, scr = update_outs(mats)
    outs2, flip2, scr2 = update_outs(mats2)
    step, n = mats[1].shape[1] // WAYS, mats[0].shape[1]
    step2, n2 = mats2[1].shape[1] // WAYS, mats2[0].shape[1]
    half = (near_blocks.shape[1] - step) // 2
    wide = norms[1].shape[1]

    def kernel(idx, *refs):
        ins, ins2, (even, odd), norm_refs, rest = refs[:5], refs[5:10], refs[10:12], refs[12:15], refs[15:]
        sums = 0.0
        for i, k in enumerate(ORDER):
            for far_one, blocks in enumerate((even, odd)):
                j = jnp.bitwise_xor(idx[0], k + far_one)
                block = blocks[i].astype(F32)
                rest[-2][pl.ds(pl.multiple_of(j * step, step), step), :] = block[:step, :n]
                rest[-1][pl.ds(pl.multiple_of(j * step2, step2), step2), :] = unpack_rows(block[:step, n:], n2)
                sums = sums + (block[step : step + half] + block[step + half :])
        grads = [sums[:4], jnp.concatenate([sums[4:5, :wide], sums[4:5, wide : 2 * wide]], axis=0), sums[5:7]]
        for i, (grad, rate) in enumerate(zip(grads, (rates[0], rates[0], rates[1]))):
            rest[10 + i][...] = grad
            rest[13 + i][...] = norm_refs[i][...] - rate * grad
        precondition(idx, ins2, rest[5:10], rest[-1], total, flip2)
        precondition(idx, ins, rest[:5], rest[-2], total, flip)

    all_outs = outs + outs2 + [sds(x.shape, F32) for x in [*norms, *norms]]
    ins = [*mats, *mats2, near_blocks, far_blocks, *norms]
    res = run(kernel, (1,), ins, fulls(ins), all_outs, fulls(all_outs), idx, name, 6, [scr, scr2], after)
    res = list(res)
    res[0] = res[0].T if flip else res[0]
    res[5] = res[5].T if flip2 else res[5]
    return res[:5], res[5:10], res[10:]


def body(
    tokens,
    cotangent,
    doc_lengths,
    outer_norms,
    attn_norm,
    ffn_norm,
    w_qkv,
    left_qkv,
    right_qkv,
    left_root_qkv,
    right_root_qkv,
    w_out,
    left_out,
    right_out,
    left_root_out,
    right_root_out,
    w_up,
    left_up,
    right_up,
    left_root_up,
    right_root_up,
    w_down,
    left_down,
    right_down,
    left_root_down,
    right_root_down,
):
    row_count = tokens.shape[0]
    n_dp, n_mp = lax.axis_size("dp"), lax.axis_size("mp")
    fine = n_dp // WAYS
    total = row_count * n_dp
    dp_at, mp_at = lax.axis_index("dp"), lax.axis_index("mp")
    idx = jnp.stack([dp_at // fine, mp_at, dp_at]).astype(jnp.int32)
    hw = w_qkv.shape[2] // 3

    def swap(x, axis, size, k):
        return lax.ppermute(x, axis, [(i, i ^ k) for i in range(size)])

    def dp(x, k):
        return swap(x, "dp", n_dp, k * fine)

    def mp(x, k):
        return swap(x, "mp", n_mp, k)

    def fine_rows(x):
        k = 1
        while k < fine:
            got = swap(x, "dp", n_dp, k)
            x = jnp.where((dp_at & k) == 0, jnp.concatenate([x, got], 0), jnp.concatenate([got, x], 0))
            k *= 2
        return x

    def fine_sum(x):
        k = 1
        while k < fine:
            x = x + swap(x, "dp", n_dp, k)
            k *= 2
        return x

    def gather8(own, *early):
        parts = {0: own}
        for k in (2, 4, 6):
            parts[k] = dp(own, k)
        parts[1] = dp(own, 1)
        for k in (2, 4, 6):
            parts[k ^ 1] = dp(after(parts[k], *early) if early else parts[k], 1)
        return [parts[k] for k in range(WAYS)]

    def gather4(own):
        far = mp(own, 2)
        return [own, mp(own, 1), far, mp(far, 1)]

    def scatter4(send, keep):
        got = mp(send, 1)
        return keep, got, mp((keep[1] + got[1].astype(F32)).astype(BF), 2)

    def gather8_halves(own):
        two = jnp.stack([own, dp(own, 4)])
        four = jnp.concatenate([two, dp(two, 2)])
        return four, dp(four, 1)

    def after(x, *deps):
        return lax.optimization_barrier((x, *deps))[0]

    groups = tokens.shape[1] // hw
    if fine == 1:
        first = pack_weights(w_qkv[0], w_out[0], groups, idx)
    else:
        out_rows = fine_rows(w_out[0].astype(BF))
        first = jnp.concatenate([fine_rows(w_qkv[0].astype(BF)), pack_rows(out_rows, groups)], axis=1)
    up_own, down_own = (fine_rows(x) for x in cast_pair(w_up[0], w_down[0], idx))
    down_two = jnp.stack([down_own, dp(down_own, 1)])
    first = gather8(first, down_two)

    ends = jnp.cumsum(doc_lengths[0])
    places = jnp.arange(row_count, dtype=jnp.int32)
    start = jnp.max(jnp.where(ends[None, :] <= places[:, None], ends[None, :], 0), axis=1, keepdims=True)
    start = start.astype(jnp.int32)
    hat, _ = normalize(tokens.astype(F32))
    a_low = (hat * outer_norms[0] + outer_norms[1]).astype(BF)

    up_go = after(up_own, first[2], first[4], first[6], down_two)
    up_z = [dp(up_go, k) for k in ORDER[1:]]
    down_z2 = dp(after(down_two, up_go), 4)
    q, k, v, wq, wo = project(a_low, attn_norm, first, hw, idx)
    wo_far = mp(wo, 2)
    o, *probs = attend(start, q, k, v, idx)
    o, *up_z = lax.optimization_barrier((o, *up_z))
    o_far = mp(o, 2)
    up_four = jnp.stack([up_own, *up_z])
    up_x = dp(up_four, 1)
    wo_near, wo_last = mp(after(wo, up_four), 1), mp(after(wo_far, up_four), 1)
    down_four = join([down_two, down_z2], idx, [wo_near, wo_last, mark(idx, [down_z2], 20)])
    down_z1 = dp(down_four, 2)
    o_near = mp(after(o, o_far), 1)
    o_all = [o, o_near, o_far, mp(o_far, 1)]
    wo_all = [wo, wo_near, wo_far, wo_last]
    hidden, c_low = outproj(outer_norms, tokens, o_all, wo_all, idx, [up_x])
    z, slope, dw, stats, wu, wd = ffn_up(c_low, cotangent, ffn_norm, [up_four, up_x, down_four, down_z1], idx)
    stats = lax.all_gather(stats, "mp")
    w_low, du, dc_send, dc_keep, dc_last, ffn_grads = ffn_mid(z, slope, dw, stats, ffn_norm, wu, idx)
    dc_got = mp(dc_send, 1)
    dc_sum = far_sum(dc_last, dc_got, idx)
    down_send, down_keep = weight_grad(w_low, cotangent, idx, "grad_down", [dc_sum])
    down_x = dp(down_send, 1)
    up_send, up_keep = weight_grad(c_low, du, idx, "grad_up", [down_send])
    up_x2 = dp(after(up_send, down_send), 1)
    dh, outer_late, attn_grads, *rest = shard_back(
        dc_keep, dc_got, mp(dc_sum, 2), hidden, cotangent, outer_norms, o_all, wo_all, idx, [up_send]
    )
    do, (go_send, go_keep, go_last) = rest[:n_mp], rest[n_mp:]
    do = [do[0]] + [mp(do[k], k) for k in range(1, n_mp)]
    go_got = mp(go_send, 1)
    bo_send, bo_keep, bo_last = ffn_out(w_low, wd, idx, [do[1]])
    down_t, down_low = fold(down_keep, down_x, idx, [bo_send], 0)
    go_sum = far_sum(go_last, go_got, idx, [down_low], 0)
    dqkv = attend_back(q, k, v, probs, do, idx, [go_sum])
    down_z1 = dp(down_low, 2)
    go_far = mp(go_sum, 2)
    bo_got = mp(after(bo_send, dqkv), 1)
    down_t, down_low = fold(down_t, down_z1, idx, [dqkv])
    up_t, up_low = fold(up_keep, up_x2, idx, [down_low])
    qkv_send, qkv_keep, da_send, da_keep, da_last = qkv_back(
        a_low, dqkv, wq, [go_keep, go_got, go_far], idx, [up_low]
    )

    down_z2, up_z1 = dp(down_low, 4), dp(up_low, 2)
    qkv_x = dp(qkv_send, 1)
    da_got = mp(da_send, 1)
    down_done = fine_sum(close(down_t, [down_z2], idx, [qkv_send], tick=20))
    down_r4 = dp(down_done, 4)
    up_t, up_low = fold(up_t, up_z1, idx, [down_done], 20)
    up_z2 = dp(up_low, 4)
    da_sum = far_sum(da_last, da_got, idx, [up_low])
    da_far = mp(da_sum, 2)
    bo_sum = far_sum(bo_last, bo_got, idx, [da_sum], 0)
    down_two = join([down_done, down_r4], idx, [bo_sum])
    down_r2 = dp(down_two, 2)
    qkv_t, qkv_low = fold(qkv_keep, qkv_x, idx, [down_two], 0)
    qkv_z1 = dp(qkv_low, 2)
    gt, outer_early = shard_end(da_keep, da_got, da_far, tokens, outer_norms, dh, idx, [qkv_low])
    lanes = outer_late.shape[1]
    vec = jnp.concatenate([outer_early, outer_late, attn_grads.reshape(-1, lanes)])
    vec_got = mp(vec, 1)
    up_done = fine_sum(close(up_t, [up_z2], idx, [gt]))
    up_r4 = dp(up_done, 4)
    vec = vec_add(vec, vec_got, idx, [up_done])
    vec_got = mp(vec, 2)
    gt_far = mp(after(gt, vec), 2)
    down_four = join([down_two, down_r2], idx, [vec])
    down_other = dp(down_four, 1)
    vec = vec_add(vec, vec_got, idx, [down_four])
    bo_far = mp(after(bo_sum, vec), 2)
    qkv_t, qkv_low = fold(qkv_t, qkv_z1, idx, [vec])
    qkv_z2 = dp(qkv_low, 4)
    up_two = join([up_done, up_r4], idx, [qkv_low], hbm=(0, 1))
    up_r2 = dp(up_two, 2)
    attn_own = lax.dynamic_slice_in_dim(vec[4:].reshape(n_mp, -1), mp_at, 1, 0)
    attn_own = jnp.pad(attn_own, ((0, 0), (0, lanes - attn_own.shape[1])))
    vec = jnp.concatenate([vec[:4], attn_own, ffn_grads, jnp.zeros((1, lanes), F32)])
    vec = fine_sum(vec)
    qkv_own = close(qkv_t, [qkv_z2], idx, [up_two, down_other, gt_far], None if fine > 1 else vec)
    if fine > 1:
        high = vec.astype(BF)
        qkv_own = jnp.concatenate([fine_sum(qkv_own), high, (vec - high.astype(F32)).astype(BF)])
    qkv_z = [dp(qkv_own, k) for k in ORDER[1:]]
    up_four = join([up_two, up_r2], idx, [qkv_own])
    out_own = block_end(hidden, bo_keep, bo_got, bo_far, idx, [up_four])
    out_far = mp(out_own, 2)
    up_other = dp(up_four, 1)
    down_mats = [x[0] for x in (w_down, left_down, right_down, left_root_down, right_root_down)]
    *down_res, token = update_one(down_mats, down_four, down_other, total, idx, "update_down", [up_four])
    qkv_four = join([qkv_own, *qkv_z], idx, [token], 10)
    qkv_other = dp(qkv_four, 1)

    def mats(*arrays):
        return [x[0] for x in arrays]

    ready = warm(
        mats(w_qkv, left_qkv, right_qkv, left_root_qkv, right_root_qkv)
        + mats(w_out, left_out, right_out, left_root_out, right_root_out),
        idx,
        [qkv_four],
    )
    up_mats = mats(w_up, left_up, right_up, left_root_up, right_root_up)
    *up_res, token = update_one(up_mats, up_four, up_other, total, idx, "update_up", [ready[0]], 0)
    gt_far, out_far = after(gt_far, token), after(out_far, token)
    gt_all = [gt, mp(after(gt, gt_far), 1), gt_far, mp(gt_far, 1)]
    grad_tokens, token = spread_rows(gt_all, idx, "spread_tokens", [token])
    out_all = [out_own, mp(after(out_own, out_far), 1), out_far, mp(out_far, 1)]
    block_out, token = spread_rows(out_all, idx, "spread_out", [token])
    qkv_res, out_res, vecs = update_pair(
        ready[:5],
        ready[5:],
        qkv_four,
        qkv_other,
        [outer_norms, attn_norm, ffn_norm],
        (VEC_RATE / math.sqrt(total), UNIT_RATE / math.sqrt(total)),
        total,
        idx,
        "update_qkv",
        [token],
    )

    return (
        block_out,
        grad_tokens,
        *vecs,
        *(x[None] for x in qkv_res),
        *(x[None] for x in out_res),
        *(x[None] for x in up_res),
        *(x[None] for x in down_res),
    )


def solution(mesh):
    rows = P("dp", None)
    mats = (P("mp", "dp", None),) * 4 + (P("mp", None, None),)
    res = (P("mp", None, None),) + (P("mp", "dp", None),) * 4
    cols = P(None, "mp")
    return jax.shard_map(
        body,
        mesh=mesh,
        in_specs=(rows, rows, rows, P(), cols, cols) + mats * 4,
        out_specs=(rows, rows, P(), cols, cols, P(), cols, cols) + res * 4,
        check_vma=False,
    )
```
